32 devices in a mesh: leaf: 4 (over y, x), rows: 8 (over z, core).
Axes of the slice: x: 2, y: 2, z: 4, core: 2. Of those that a mesh axis runs over, the one named last changes fastest.
Arguments:
- leaf_rhs: float32 [8, 16, 2048], P(None, 'leaf', 'rows'), may hold values from -6 to 6
- parent_rhs: float32 [8, 4, 4096], P(None, 'leaf', 'rows'), may hold values from -6 to 6
- root_rhs: float32 [8, 4096], P(None, ('leaf', 'rows')), may hold values from -6 to 6
- leaf_inv: bfloat16 [16, 2048, 2048], P('leaf', 'rows'), as said below
- leaf_panel: bfloat16 [16, 8192, 2048], P('leaf', 'rows'), may hold values from -0.0625 to 0.0625
- leaf_rows: int32 [16, 8192], P('leaf', 'rows'), may hold values from 0 to 8191, as said below
- leaf_height: int32 [16], P('leaf'), may hold values from 2048 to 8192
- parent_inv: bfloat16 [4, 4096, 4096], P('leaf', 'rows'), as said below
- parent_panel: bfloat16 [4, 4096, 4096], P('leaf', 'rows'), may hold values from -0.046875 to 0.046875
- parent_rows: int32 [4, 4096], P('leaf', 'rows'), may hold values from 0 to 4095, as said below
- parent_height: int32 [4], P('leaf'), may hold values from 1024 to 4096
- root_inv: bfloat16 [4096, 4096], P('rows'), as said below
Outputs:
- leaf_solution: float32 [8, 16, 2048], P(None, 'leaf', 'rows')
- parent_solution: float32 [8, 4, 4096], P(None, 'leaf', 'rows')
- root_solution: float32 [8, 4096], P(None, ('leaf', 'rows'))
The draws below stay inside these ranges and needn't reach their ends.
Inputs may be any that keep to these rules, and one draw needn't show every extreme that they name: `leaf_rows`: each leaf's first leaf_height entries are distinct and ascending; every entry is a valid ancestor index. `parent_rows`: each parent's first parent_height entries are distinct and ascending. `leaf_inv`: A dense well conditioned matrix. `parent_inv`: A dense well conditioned matrix. `root_inv`: A dense well conditioned matrix.
All inputs are finite; a program needn't handle non-finite values.
Results may differ from the reference program's by a relative error of at most 0.009.
Values may be sent and summed in bfloat16 or wider, within the bound.
No kernel may reach another device: no remote copies, remote signals or barrier semaphores. Data moves between devices by JAX's collectives and lax.ppermute only.
A program may use at most 128 MiB of HBM per device.

```python
import jax
import jax.numpy as jnp
from jax import lax

R = 8
WL = 2048
WP = 4096
WR = 4096
PARENTS = 4
LEAVES = 16
HL = 8192
HP = 4096


def subset_rows(key, count, length):
    k_one, k_two, k_three = jax.random.split(key, 3)
    heights = jax.random.randint(k_one, (count,), length // 4, length + 1)
    order = jax.random.permutation(k_two, count)
    heights = heights.at[order[0]].set(length).at[order[1]].set(length // 4)
    perms = jax.vmap(lambda kk: jax.random.permutation(kk, length))(jax.random.split(k_three, count))
    ranks = jnp.argsort(perms, axis=1)
    places = jnp.arange(length)[None, :]
    chosen = ranks < heights[:, None]
    keyvals = jnp.where(chosen, places, places + length)
    rows_out = jnp.argsort(keyvals, axis=1).astype(jnp.int32)
    return (rows_out, heights.astype(jnp.int32))


def leaf_struct(key):
    return subset_rows(jax.random.fold_in(key, 11), LEAVES, HL)


def parent_struct(key):
    return subset_rows(jax.random.fold_in(key, 23), PARENTS, HP)


def inverse_draw(key, count, width):
    noise = jax.random.normal(key, (count, width, width), jnp.float32)
    eye = jnp.eye(width, dtype=jnp.float32)[None, :, :]
    return (eye + 0.3 * noise / jnp.sqrt(width * 1.0)).astype(jnp.bfloat16)


def draw_leaf_rows(key, part):
    return leaf_struct(key)[0]


def draw_leaf_height(key, part):
    return leaf_struct(key)[1]


def draw_parent_rows(key, part):
    return parent_struct(key)[0]


def draw_parent_height(key, part):
    return parent_struct(key)[1]


def draw_leaf_inv(key, part):
    return inverse_draw(jax.random.fold_in(key, 31), LEAVES, WL)


def draw_parent_inv(key, part):
    return inverse_draw(jax.random.fold_in(key, 37), PARENTS, WP)


def draw_root_inv(key, part):
    return inverse_draw(jax.random.fold_in(key, 41), 1, WR)[0]


def level_of(key, dims, cuts, low, high):
    level = 1.0
    for axis_at, shards_of in cuts:
        steps = jax.random.uniform(jax.random.fold_in(jax.random.fold_in(key, 6), axis_at), (shards_of,), jnp.float32, low / len(cuts), high / len(cuts))
        level = level * jnp.repeat(jnp.exp(steps), dims[axis_at] // shards_of).reshape((-1,) + (1,) * (len(dims) - 1 - axis_at))
    return level


def scatter_about(rng, dims, scale, limit, cuts=(), kind=jnp.bfloat16):
    loudness = level_of(rng, dims, cuts, -0.22, 0.18) if cuts else 1.0
    drawn = jax.random.normal(rng, dims, jnp.float32) * scale * loudness
    return jnp.minimum(jnp.maximum(drawn, -limit), limit).astype(kind)


def setup_inputs(seed: int = 0) -> dict:
    key_list = jax.random.split(jax.random.key(seed), 13)
    return {
        "leaf_rhs": scatter_about(key_list[0], (R, LEAVES, WL), 1.0, 6.0, ((1, 4), (2, 8)), jnp.float32),
        "parent_rhs": scatter_about(key_list[1], (R, PARENTS, WP), 1.0, 6.0, ((1, 4), (2, 8)), jnp.float32),
        "root_rhs": scatter_about(key_list[2], (R, WR), 1.0, 6.0, ((1, 32),), jnp.float32),
        "leaf_inv": draw_leaf_inv(jax.random.fold_in(key_list[12], 71), 0),
        "leaf_panel": scatter_about(key_list[4], (LEAVES, HL, WL), (4 * WL) ** -0.5, 0.0625, ((0, 4), (1, 8))),
        "leaf_rows": draw_leaf_rows(jax.random.fold_in(key_list[12], 71), 0),
        "leaf_height": draw_leaf_height(jax.random.fold_in(key_list[12], 71), 0),
        "parent_inv": draw_parent_inv(jax.random.fold_in(key_list[12], 71), 0),
        "parent_panel": scatter_about(key_list[8], (PARENTS, HP, WP), (4 * WP) ** -0.5, 0.046875, ((0, 4), (1, 8))),
        "parent_rows": draw_parent_rows(jax.random.fold_in(key_list[12], 71), 0),
        "parent_height": draw_parent_height(jax.random.fold_in(key_list[12], 71), 0),
        "root_inv": draw_root_inv(jax.random.fold_in(key_list[12], 71), 0),
    }


def fdot(left, right):
    return jnp.dot(left.astype(jnp.float32), right.astype(jnp.float32), preferred_element_type=jnp.float32)


def reference(leaf_rhs, parent_rhs, root_rhs, leaf_inv, leaf_panel, leaf_rows, leaf_height, parent_inv, parent_panel, parent_rows, parent_height, root_inv):
    lb = jnp.moveaxis(leaf_rhs.astype(jnp.bfloat16), 1, 0)

    def apply_inv(args):
        vec, inverse = args
        return fdot(vec, inverse.T)

    ly = lax.map(apply_inv, (lb, leaf_inv))
    lyb = ly.astype(jnp.bfloat16)
    leaf_pos = jnp.arange(HL)

    def leaf_up(args):
        vec, panel, rows, height = args
        update = fdot(vec, panel.T)
        update = jnp.where(leaf_pos[None, :] < height, update, 0.0)
        return jnp.zeros((R, HL), jnp.float32).at[:, rows].add(update)

    acc = lax.map(leaf_up, (lyb, leaf_panel, leaf_rows, leaf_height))
    pacc = acc[:, :, :WP].reshape(PARENTS, 4, R, WP).sum(1)
    racc = acc[:, :, WP:].sum(0)
    prb = (jnp.moveaxis(parent_rhs, 1, 0) - pacc).astype(jnp.bfloat16)
    py = lax.map(apply_inv, (prb, parent_inv))
    pyb = py.astype(jnp.bfloat16)
    parent_pos = jnp.arange(HP)

    def parent_up(args):
        vec, panel, rows, height = args
        update = fdot(vec, panel.T)
        update = jnp.where(parent_pos[None, :] < height, update, 0.0)
        return jnp.zeros((R, WR), jnp.float32).at[:, rows].add(update)

    racc_two = lax.map(parent_up, (pyb, parent_panel, parent_rows, parent_height)).sum(0)
    rrb = (root_rhs - racc - racc_two).astype(jnp.bfloat16)
    ry = fdot(rrb, root_inv.T)
    root_solution = fdot(ry.astype(jnp.bfloat16), root_inv)
    rxb = root_solution.astype(jnp.bfloat16)

    def parent_back(args):
        partial_value, panel, rows, height, inverse = args
        ancestor = rxb[:, rows]
        ancestor = jnp.where(parent_pos[None, :] < height, ancestor, jnp.zeros_like(ancestor))
        term = fdot(ancestor, panel)
        value = (partial_value - term).astype(jnp.bfloat16)
        return fdot(value, inverse)

    px = lax.map(parent_back, (py, parent_panel, parent_rows, parent_height, parent_inv))
    pxb = jnp.repeat(px.astype(jnp.bfloat16), 4, axis=0)

    def leaf_back(args):
        partial_value, upper, panel, rows, height, inverse = args
        whole = jnp.concatenate([upper, rxb], axis=1)
        ancestor = whole[:, rows]
        ancestor = jnp.where(leaf_pos[None, :] < height, ancestor, jnp.zeros_like(ancestor))
        term = fdot(ancestor, panel)
        value = (partial_value - term).astype(jnp.bfloat16)
        return fdot(value, inverse)

    lx = lax.map(leaf_back, (ly, pxb, leaf_panel, leaf_rows, leaf_height, leaf_inv))
    return jnp.moveaxis(lx, 0, 1), jnp.moveaxis(px, 0, 1), root_solution
```

```python
import jax
import jax.numpy as jnp
from jax import lax
from jax.sharding import PartitionSpec as P

F32 = jnp.float32
BF16 = jnp.bfloat16


def a2a_gather(x, axis):
    n = lax.axis_size(axis)
    return lax.all_to_all(jnp.broadcast_to(x[None], (n,) + x.shape), axis, 0, 0)


def a2a_reduce(x, axis):
    return lax.all_to_all(x.astype(BF16), axis, 0, 0).astype(F32).sum(0)


def shift(x, axis, k):
    n = lax.axis_size(axis)
    return lax.ppermute(x, axis, [(i, (i + k) % n) for i in range(n)])


def direct_gather(x, axis):
    n = lax.axis_size(axis)
    me = lax.axis_index(axis)
    got = [x] + [shift(x, axis, k) for k in range(1, n)]
    order = jnp.stack(got[::-1] + got[::-1])
    return lax.dynamic_slice_in_dim(order, n - 1 - me, n, 0)


def direct_reduce(x, axis):
    n = lax.axis_size(axis)
    me = lax.axis_index(axis)
    x = x.astype(BF16)
    got = []
    for k in range(n):
        part = lax.dynamic_index_in_dim(x, lax.rem(me + k, n), 0, keepdims=False)
        got.append(part if k == 0 else shift(part, axis, k))
    return sum(p.astype(F32) for p in got)


def direct_sum(x, axis):
    n = lax.axis_size(axis)
    x = x.astype(BF16)
    got = [x] + [shift(x, axis, k) for k in range(1, n)]
    return sum(p.astype(F32) for p in got)


def doubling_gather(x, axis):
    n = lax.axis_size(axis)
    me = lax.axis_index(axis)
    cur = x[None]
    step = 1
    while step < n:
        got = lax.ppermute(cur, axis, [(i, i ^ step) for i in range(n)])
        upper = (me & step) != 0
        cur = jnp.concatenate([jnp.where(upper, got, cur), jnp.where(upper, cur, got)])
        step *= 2
    return cur


def shards(
    leaf_rhs,
    parent_rhs,
    root_rhs,
    leaf_inv,
    leaf_panel,
    leaf_rows,
    leaf_height,
    parent_inv,
    parent_panel,
    parent_rows,
    parent_height,
    root_inv,
):
    n = lax.axis_size("rows")
    groups = lax.axis_size("leaf")
    rcount = leaf_rhs.shape[0]
    group_leaves = leaf_rhs.shape[1]
    leaf_local = leaf_panel.shape[1]
    parent_width = parent_inv.shape[2]
    root_width = root_inv.shape[1]
    row_index = lax.axis_index("rows")
    leaf_index = lax.axis_index("leaf")
    parent_cols = parent_width // n
    root_cols = root_rhs.shape[1]

    lb = a2a_gather(leaf_rhs.astype(BF16), "rows")
    lb = jnp.moveaxis(lb, 0, 2).reshape(rcount, group_leaves, -1)
    ly = jnp.einsum("rln,lin->rli", lb, leaf_inv, preferred_element_type=F32)
    lyb = direct_gather(ly.astype(BF16), "rows")
    lyb = jnp.moveaxis(lyb, 0, 2).reshape(rcount, group_leaves, -1)
    lupd = jnp.einsum("rln,lhn->rlh", lyb, leaf_panel, preferred_element_type=F32)
    leaf_pos = row_index * leaf_local + jnp.arange(leaf_local, dtype=jnp.int32)
    leaf_mask = leaf_pos[None, :] < leaf_height[:, None]
    lupd = jnp.where(leaf_mask[None, :, :], lupd, 0.0)
    leaf_flat = leaf_rows.reshape(-1)
    local_acc = (
        jnp.zeros((rcount, parent_width + root_width), F32)
        .at[:, leaf_flat]
        .add(lupd.reshape(rcount, -1))
    )
    pacc = a2a_reduce(
        jnp.moveaxis(local_acc[:, :parent_width].reshape(rcount, n, parent_cols), 1, 0), "rows"
    )
    root_from_leaves = local_acc[:, parent_width:]
    prb = (parent_rhs[:, 0, :] - pacc).astype(BF16)
    prb = jnp.moveaxis(doubling_gather(prb, "rows"), 0, 1).reshape(rcount, -1)
    inverse_rows = parent_inv[0]
    panel_rows = parent_panel[0]
    py = jnp.dot(prb, inverse_rows.T, preferred_element_type=F32)
    pyb = jnp.moveaxis(a2a_gather(py.astype(BF16), "rows"), 0, 1).reshape(rcount, -1)
    parent_local = panel_rows.shape[0]
    pupd = jnp.dot(pyb, panel_rows.T, preferred_element_type=F32)
    parent_pos = row_index * parent_local + jnp.arange(parent_local, dtype=jnp.int32)
    parent_mask = parent_pos < parent_height[0]
    pupd = jnp.where(parent_mask[None, :], pupd, 0.0)
    root_part = root_from_leaves.at[:, parent_rows[0]].add(pupd)
    root_part = jnp.transpose(root_part.reshape(rcount, groups, n, root_cols), (2, 0, 1, 3))
    racc = direct_sum(direct_reduce(root_part, "rows"), "leaf")
    rhs_piece = jnp.moveaxis(direct_gather(root_rhs, "leaf"), 0, 1)
    rrb = direct_gather((rhs_piece - racc).astype(BF16), "rows")
    rrb = jnp.transpose(rrb, (1, 2, 0, 3)).reshape(rcount, root_width)
    ry = jnp.dot(rrb, root_inv.T, preferred_element_type=F32)
    root_term = jnp.dot(ry.astype(BF16), root_inv, preferred_element_type=F32)
    root_term = jnp.transpose(root_term.reshape(rcount, groups, n, root_cols), (2, 0, 1, 3))
    root_piece = a2a_reduce(root_term, "rows")
    root_solution = lax.dynamic_index_in_dim(root_piece, leaf_index, 1, keepdims=False)
    rxb = doubling_gather(root_piece.astype(BF16), "rows")
    rxb = jnp.transpose(rxb, (1, 2, 0, 3)).reshape(rcount, root_width)
    parent_anc = rxb[:, parent_rows[0]]
    parent_anc = jnp.where(parent_mask[None, :], parent_anc, jnp.zeros_like(parent_anc))
    parent_term = jnp.dot(parent_anc, panel_rows, preferred_element_type=F32)
    parent_tail = direct_reduce(
        jnp.moveaxis(parent_term.reshape(rcount, n, parent_cols), 1, 0), "rows"
    )
    pvb = (py - parent_tail).astype(BF16)
    parent_sol_term = jnp.dot(pvb, inverse_rows, preferred_element_type=F32)
    parent_sol = a2a_reduce(
        jnp.moveaxis(parent_sol_term.reshape(rcount, n, parent_cols), 1, 0), "rows"
    )
    parent_whole = jnp.moveaxis(direct_gather(parent_sol.astype(BF16), "rows"), 0, 1)
    ancestors = jnp.concatenate([parent_whole.reshape(rcount, -1), rxb], axis=1)
    leaf_anc = ancestors[:, leaf_flat].reshape(rcount, group_leaves, leaf_local)
    leaf_anc = jnp.where(leaf_mask[None, :, :], leaf_anc, jnp.zeros_like(leaf_anc))
    leaf_term = jnp.einsum("rlh,lhc->rlc", leaf_anc, leaf_panel, preferred_element_type=F32)
    leaf_term = jnp.moveaxis(leaf_term.reshape(rcount, group_leaves, n, -1), 2, 0)
    leaf_tail = a2a_reduce(leaf_term, "rows")
    lvb = (ly - leaf_tail).astype(BF16)
    leaf_sol_term = jnp.einsum("rli,lic->rlc", lvb, leaf_inv, preferred_element_type=F32)
    leaf_sol_term = jnp.moveaxis(leaf_sol_term.reshape(rcount, group_leaves, n, -1), 2, 0)
    leaf_sol = direct_reduce(leaf_sol_term, "rows")
    return (leaf_sol, parent_sol[:, None, :], root_solution)


def solution(mesh):
    return jax.shard_map(
        shards,
        mesh=mesh,
        in_specs=(
            P(None, "leaf", "rows"),
            P(None, "leaf", "rows"),
            P(None, ("leaf", "rows")),
            P("leaf", "rows", None),
            P("leaf", "rows", None),
            P("leaf", "rows"),
            P("leaf"),
            P("leaf", "rows", None),
            P("leaf", "rows", None),
            P("leaf", "rows"),
            P("leaf"),
            P("rows", None),
        ),
        out_specs=(P(None, "leaf", "rows"), P(None, "leaf", "rows"), P(None, ("leaf", "rows"))),
        check_vma=False,
    )
```

```python
import math

import jax
import jax.numpy as jnp
from jax import lax
from jax.experimental import pallas as pl
from jax.experimental.pallas import tpu as pltpu
from jax.sharding import PartitionSpec as P

F32 = jnp.float32
BF16 = jnp.bfloat16
I32 = jnp.int32


def fetch_body(count, *refs):
    sources, targets, sems = refs[:count], refs[count + 1 : 2 * count + 1], refs[-1]
    copies = [
        pltpu.make_async_copy(s, t, sems.at[i]) for i, (s, t) in enumerate(zip(sources, targets))
    ]
    for copy in copies:
        copy.start()
    for copy in copies:
        copy.wait()


def fetch(after, *weights):
    count = len(weights)
    size = sum(math.prod(w.shape) * w.dtype.itemsize for w in weights)
    return pl.pallas_call(
        lambda *refs: fetch_body(count, *refs),
        out_shape=[pltpu.VMEM(w.shape, w.dtype) for w in weights],
        in_specs=[pl.BlockSpec(memory_space=pltpu.HBM)] * count
        + [pl.BlockSpec(memory_space=pl.ANY)],
        out_specs=[pl.BlockSpec(memory_space=pltpu.VMEM)] * count,
        scratch_shapes=[pltpu.SemaphoreType.DMA((count,))],
        cost_estimate=pl.CostEstimate(flops=0, bytes_accessed=2 * size, transcendentals=0),
        compiler_params=pltpu.CompilerParams(vmem_limit_bytes=1 << 20),
        name="fetch_weights",
    )(*weights, after)


def swap(x):
    n = lax.axis_size("rows")
    return lax.ppermute(x, "rows", [(i, i ^ 1) for i in range(n)])


def far(x, k):
    n = lax.axis_size("rows")
    return lax.ppermute(x, "rows", [(i, i ^ (2 * k)) for i in range(n)])


def chips():
    return lax.axis_size("rows") // 2


def is_odd():
    return (lax.axis_index("rows") & 1) != 0


def by_chip(x):
    chip = lax.axis_index("rows") // 2
    step = 1
    while step < x.shape[0]:
        y = x.reshape((x.shape[0] // (2 * step), 2, step) + x.shape[1:])
        y = jnp.where((chip & step) != 0, y[:, ::-1], y)
        x = y.reshape(x.shape)
        step *= 2
    return x


def join(x):
    y = swap(x)
    odd = is_odd()
    pairs = jnp.stack([jnp.where(odd, y, x), jnp.where(odd, x, y)], axis=1)
    return pairs.reshape((2 * x.shape[0],) + x.shape[1:])


def part(x):
    x = x.reshape((x.shape[0] // 2, 2) + x.shape[1:])
    odd = is_odd()
    other = jnp.where(odd, x[:, 0], x[:, 1]).astype(BF16)
    return jnp.where(odd, x[:, 1], x[:, 0]) + swap(other).astype(F32)


def gather(x):
    got = [x] + [far(x, k) for k in range(1, chips())]
    return by_chip_pairs(jnp.stack(got))


def by_chip_pairs(x):
    return join(by_chip(x))


def reduce(x):
    x = by_chip(part(x))
    return x[0] + sum(far(x[k].astype(BF16), k).astype(F32) for k in range(1, chips()))


def total(x, leaf_too=False):
    x = part(x)
    if leaf_too:
        x = leaf_total(x)
    b = x.astype(BF16)
    return x + sum(far(b, k).astype(F32) for k in range(1, chips()))


def leaf_total(x):
    n = lax.axis_size("leaf")
    b = x.astype(BF16)
    for k in range(1, n):
        x = x + lax.ppermute(b, "leaf", [(i, (i + k) % n) for i in range(n)]).astype(F32)
    return x


def pieces(x, n):
    return jnp.moveaxis(x.reshape(x.shape[:-1] + (n, x.shape[-1] // n)), -2, 0)


def whole(x):
    x = jnp.moveaxis(x, 0, -2)
    return x.reshape(x.shape[:-2] + (-1,))


def place(piece, count, index):
    at = jnp.arange(count).reshape((count,) + (1,) * piece.ndim)
    return jnp.where(at == index, piece[None], jnp.zeros_like(piece[None]))


def shards(
    leaf_rhs,
    parent_rhs,
    root_rhs,
    leaf_inv,
    leaf_panel,
    leaf_rows,
    leaf_height,
    parent_inv,
    parent_panel,
    parent_rows,
    parent_height,
    root_inv,
):
    n = lax.axis_size("rows")
    groups = lax.axis_size("leaf")
    rcount = leaf_rhs.shape[0]
    group_leaves = leaf_rhs.shape[1]
    leaf_local = leaf_panel.shape[1]
    parent_width = parent_inv.shape[2]
    root_width = root_inv.shape[1]
    row_index = lax.axis_index("rows")
    flat_index = lax.axis_index("leaf") * n + row_index
    root_cols = root_rhs.shape[1]

    lb = jnp.moveaxis(leaf_rhs.astype(BF16), 1, 0)
    leaf_inv, leaf_panel = fetch(lb, leaf_inv, leaf_panel)
    lb = whole(gather(lb))
    ly = jnp.einsum("lrn,lin->lri", lb, leaf_inv, preferred_element_type=F32)
    lyb = ly.astype(BF16)
    parent_inv, parent_panel, root_inv = fetch(lyb, parent_inv[0], parent_panel[0], root_inv)
    lyb = whole(gather(lyb))
    lupd = jnp.einsum("lrn,lhn->lrh", lyb, leaf_panel, preferred_element_type=F32)
    leaf_pos = row_index * leaf_local + jnp.arange(leaf_local, dtype=I32)
    leaf_mask = leaf_pos[None, :] < leaf_height[:, None]
    lupd = jnp.where(leaf_mask[:, None, :], lupd, 0.0)
    leaf_flat = leaf_rows.reshape(-1)
    local_acc = (
        jnp.zeros((rcount, parent_width + root_width), F32)
        .at[:, leaf_flat]
        .add(jnp.moveaxis(lupd, 0, 1).reshape(rcount, -1))
    )
    pacc = pieces(local_acc[:, :parent_width], n) - place(parent_rhs[:, 0], n, row_index)
    prb = (-total(pacc)).astype(BF16)
    py = jnp.dot(whole(join(prb)), parent_inv.T, preferred_element_type=F32)
    pyb = whole(gather(py.astype(BF16)))
    parent_local = parent_panel.shape[0]
    pupd = jnp.dot(pyb, parent_panel.T, preferred_element_type=F32)
    parent_pos = row_index * parent_local + jnp.arange(parent_local, dtype=I32)
    parent_mask = parent_pos < parent_height[0]
    pupd = jnp.where(parent_mask[None, :], pupd, 0.0)
    racc = local_acc[:, parent_width:].at[:, parent_rows[0]].add(pupd)
    racc = pieces(racc, groups * n) - place(root_rhs, groups * n, flat_index)
    racc = racc.reshape((n, groups) + racc.shape[1:])
    rrb = (-total(racc, leaf_too=True)).astype(BF16)
    rrb = whole(join(rrb).reshape((n * groups,) + rrb.shape[2:]))
    ry = jnp.dot(rrb, root_inv.T, preferred_element_type=F32)
    root_term = jnp.dot(ry.astype(BF16), root_inv, preferred_element_type=F32)
    rxb = join(total(pieces(root_term, n)).astype(BF16))
    rxb = whole(rxb)
    root_solution = lax.dynamic_slice_in_dim(rxb, flat_index * root_cols, root_cols, 1).astype(F32)
    parent_anc = rxb[:, parent_rows[0]]
    parent_anc = jnp.where(parent_mask[None, :], parent_anc, jnp.zeros_like(parent_anc))
    parent_term = jnp.dot(parent_anc, parent_panel, preferred_element_type=F32)
    pvb = (py - reduce(pieces(parent_term, n))).astype(BF16)
    parent_term = jnp.dot(pvb, parent_inv, preferred_element_type=F32)
    parent_part = total(pieces(parent_term, n))
    parent_sol = lax.dynamic_index_in_dim(parent_part, row_index // 2, 0, keepdims=False)
    parent_whole = whole(join(parent_part.astype(BF16)))
    ancestors = jnp.concatenate([parent_whole, rxb], axis=1)
    leaf_anc = ancestors[:, leaf_flat].reshape(rcount, group_leaves, leaf_local)
    leaf_anc = jnp.where(leaf_mask[None, :, :], leaf_anc, jnp.zeros_like(leaf_anc))
    leaf_term = jnp.einsum("rlh,lhc->lrc", leaf_anc, leaf_panel, preferred_element_type=F32)
    lvb = (ly - reduce(pieces(leaf_term, n))).astype(BF16)
    leaf_term = jnp.einsum("lri,lic->lrc", lvb, leaf_inv, preferred_element_type=F32)
    leaf_sol = jnp.moveaxis(reduce(pieces(leaf_term, n)), 0, 1)
    return (leaf_sol, parent_sol[:, None, :], root_solution)


def solution(mesh):
    return jax.shard_map(
        shards,
        mesh=mesh,
        in_specs=(
            P(None, "leaf", "rows"),
            P(None, "leaf", "rows"),
            P(None, ("leaf", "rows")),
            P("leaf", "rows", None),
            P("leaf", "rows", None),
            P("leaf", "rows"),
            P("leaf"),
            P("leaf", "rows", None),
            P("leaf", "rows", None),
            P("leaf", "rows"),
            P("leaf"),
            P("rows", None),
        ),
        out_specs=(P(None, "leaf", "rows"), P(None, "leaf", "rows"), P(None, ("leaf", "rows"))),
        check_vma=False,
    )
```

```python
import math

import jax
import jax.numpy as jnp
from jax import lax
from jax.experimental import pallas as pl
from jax.experimental.pallas import tpu as pltpu
from jax.sharding import PartitionSpec as P

F32 = jnp.float32
BF16 = jnp.bfloat16
I32 = jnp.int32
LANES = 128
UNROLL = 4

VMEM = pl.BlockSpec(memory_space=pltpu.VMEM)
SMEM = pl.BlockSpec(memory_space=pltpu.SMEM)


def pinned(w):
    return pltpu.with_memory_space_constraint(w, pltpu.VMEM)


def call(body, outs, ins, specs, scratch=(), flops=0, moved=0, limit=6 << 20, name=None):
    return pl.pallas_call(
        body,
        out_shape=[jax.ShapeDtypeStruct(s, d) for s, d in outs],
        in_specs=list(specs),
        out_specs=[VMEM] * len(outs),
        scratch_shapes=list(scratch),
        cost_estimate=pl.CostEstimate(flops=flops, bytes_accessed=moved, transcendentals=0),
        compiler_params=pltpu.CompilerParams(vmem_limit_bytes=limit),
        name=name,
    )(*ins)


def times_transposed(x, w):
    return lax.dot_general(x, w, (((1,), (1,)), ((), ())), preferred_element_type=F32)


def times(x, w):
    return lax.dot_general(x, w, (((1,), (0,)), ((), ())), preferred_element_type=F32)


def fetch(after, *weights):
    count = len(weights)
    size = sum(math.prod(w.shape) * w.dtype.itemsize for w in weights)

    def body(*refs):
        sources, targets, sems = refs[:count], refs[count + 1 : 2 * count + 1], refs[-1]
        copies = [
            pltpu.make_async_copy(s, t, sems.at[i])
            for i, (s, t) in enumerate(zip(sources, targets))
        ]
        for copy in copies:
            copy.start()
        for copy in copies:
            copy.wait()

    return pl.pallas_call(
        body,
        out_shape=[pltpu.VMEM(w.shape, w.dtype) for w in weights],
        in_specs=[pl.BlockSpec(memory_space=pltpu.HBM)] * count
        + [pl.BlockSpec(memory_space=pl.ANY)],
        out_specs=[VMEM] * count,
        scratch_shapes=[pltpu.SemaphoreType.DMA((count,))],
        cost_estimate=pl.CostEstimate(flops=0, bytes_accessed=2 * size, transcendentals=0),
        compiler_params=pltpu.CompilerParams(vmem_limit_bytes=1 << 20),
        name="fetch_weights",
    )(*weights, after)


def walk_plan(rows, width):
    sets, length = rows.shape
    blocks = width // LANES
    tiled = rows.reshape(sets, length // LANES, LANES)
    first = tiled[:, :, 0] // LANES
    used = tiled[:, :, 0] >= 0
    last = tiled.max(-1) // LANES
    lo = jnp.where(used, first, blocks)
    span = jnp.where(used, last - first + 1, 0)
    trips = (span.max(0) + UNROLL - 1) // UNROLL
    return jnp.concatenate([lo.reshape(-1), trips]).astype(I32)


def walk(plan_ref, sets, tiles, blocks, tile, visit, carry):
    def trip(i, carry):
        at = []
        for s in range(sets):
            lo = plan_ref[s * tiles + tile] + i * UNROLL
            at += [(s, jnp.minimum(lo + u, blocks)) for u in range(UNROLL)]
        return visit(at, carry)

    return lax.fori_loop(0, plan_ref[sets * tiles + tile], trip, carry)


def pick(x, index):
    inside = (index >= 0) & (index < LANES)
    found = jnp.take_along_axis(
        x, index & (LANES - 1), axis=1, mode="promise_in_bounds"
    )
    return jnp.where(inside, found, 0.0)


def invert(rows, plan, width):
    sets, length = rows.shape
    tiles, blocks = length // LANES, width // LANES

    def body(plan_ref, rows_ref, out_ref):
        out_ref[...] = jnp.full(out_ref.shape, -1, I32)
        for tile in range(tiles):
            cols, spots = [], lax.broadcasted_iota(I32, (LANES, LANES), 0) + (tile * LANES + 1)
            for s in range(sets):
                line = rows_ref[s : s + 1, tile * LANES : (tile + 1) * LANES]
                cols.append(jnp.transpose(jnp.broadcast_to(line, (LANES, LANES))))

            def visit(at, carry):
                lane = lax.broadcasted_iota(I32, (LANES, LANES), 1)
                got = []
                for s, block in at:
                    hit = cols[s] == lane + block * LANES
                    got.append(jnp.sum(jnp.where(hit, spots, 0), axis=0, keepdims=True))
                for (s, block), g in zip(at, got):
                    out_ref[s, block] += jnp.broadcast_to(g, out_ref.shape[2:])
                return carry

            walk(plan_ref, sets, tiles, blocks, tile, visit, 0)

    return call(
        body,
        [((sets, blocks + 1, 8, LANES), I32)],
        [plan, rows],
        [SMEM, VMEM],
        moved=16 << 20,
        limit=4 << 20,
        name="invert_rows",
    )[0]


def scatter_walk(plan_ref, inverse_ref, update_ref, acc_ref, tiles):
    sets, blocks = inverse_ref.shape[0], inverse_ref.shape[1] - 1
    for tile in range(tiles):

        def visit(at, carry):
            got = []
            for s, block in at:
                x = update_ref[s, :, tile * LANES : (tile + 1) * LANES]
                got.append(pick(x, inverse_ref[s, block] - tile * LANES))
            for (s, block), g in zip(at, got):
                acc_ref[block] += g
            return carry

        walk(plan_ref, sets, tiles, blocks, tile, visit, 0)


def gather_walk(plan_ref, rows_ref, source_ref, out_ref):
    sets, length = rows_ref.shape
    tiles, blocks = length // LANES, source_ref.shape[0] - 1
    for tile in range(tiles):
        index = [
            jnp.broadcast_to(
                rows_ref[s : s + 1, tile * LANES : (tile + 1) * LANES], (8, LANES)
            )
            for s in range(sets)
        ]

        def visit(at, carry):
            carry = list(carry)
            for s, block in at:
                carry[s] = carry[s] + pick(source_ref[block], index[s] - block * LANES)
            return tuple(carry)

        zero = tuple(jnp.zeros((8, LANES), F32) for _ in range(sets))
        found = walk(plan_ref, sets, tiles, blocks, tile, visit, zero)
        for s in range(sets):
            out_ref[s, :, tile * LANES : (tile + 1) * LANES] = found[s].astype(out_ref.dtype)


def joined(ref, *at):
    return jnp.concatenate([ref[(j,) + at] for j in range(ref.shape[0])], axis=1)


def split(value, n):
    w = value.shape[1] // n
    return [value[:, j * w : (j + 1) * w] for j in range(n)]


def unite(where_ref, own_ref, other_ref, out_ref):
    core = where_ref[0]
    chips, _, w = own_ref.shape
    for k in range(chips):
        for ref, odd in ((own_ref, core), (other_ref, 1 - core)):
            out_ref[:, pl.ds(pl.multiple_of((2 * k + odd) * w, LANES), w)] = ref[k]


def deal(where_ref, value_ref, own_ref, other_ref):
    core = where_ref[0]
    chips, _, w = own_ref.shape
    for k in range(chips):
        for ref, odd in ((own_ref, core), (other_ref, 1 - core)):
            piece = value_ref[:, pl.ds(pl.multiple_of((2 * k + odd) * w, LANES), w)]
            ref[k] = piece.astype(ref.dtype)


def all_gather(copies):
    return lax.all_to_all(copies, "rows", 0, 0)


def scatter_pieces(x):
    return lax.all_to_all(x, "rows", 0, 0)


def swap(x):
    n = lax.axis_size("rows")
    return lax.ppermute(x, "rows", [(i, i ^ 1) for i in range(n)])


def far(x, k):
    n = lax.axis_size("rows")
    return lax.ppermute(x, "rows", [(i, i ^ (2 * k)) for i in range(n)])


def chips_sum(x):
    b = x.astype(BF16)
    return x + sum(far(b, k).astype(F32) for k in range(1, lax.axis_size("rows") // 2))


def chips_sum_at_once(x):
    n = lax.axis_size("rows")
    b = jnp.broadcast_to(x.astype(BF16)[None], (n // 2,) + x.shape)
    groups = [list(range(c, n, 2)) for c in range(2)]
    got = lax.all_to_all(b, "rows", 0, 0, axis_index_groups=groups)
    return got.astype(F32).sum(0)


def leaf_sum(x):
    n = lax.axis_size("leaf")
    b = x.astype(BF16)
    for k in range(1, n):
        x = x + lax.ppermute(b, "leaf", [(i, (i + k) % n) for i in range(n)]).astype(F32)
    return x


def shards(
    leaf_rhs,
    parent_rhs,
    root_rhs,
    leaf_inv,
    leaf_panel,
    leaf_rows,
    leaf_height,
    parent_inv,
    parent_panel,
    parent_rows,
    parent_height,
    root_inv,
):
    n = lax.axis_size("rows")
    chips = n // 2
    rcount, leaves, leaf_cols = leaf_rhs.shape
    leaf_local, leaf_width = leaf_panel.shape[1:]
    parent_cols, parent_width = parent_inv.shape[1:]
    parent_local = parent_panel.shape[1]
    root_local, root_width = root_inv.shape
    root_cols = root_rhs.shape[1]
    piece = root_width // n
    tall = parent_width + root_width
    row = lax.axis_index("rows")
    flat = lax.axis_index("leaf") * n + row
    where = jnp.stack([row & 1, row // 2, row, flat]).astype(I32)
    aligned = leaf_cols % LANES == 0

    def leaf_vector(got):
        return got if aligned else jnp.moveaxis(got, 0, 2).reshape(1, leaves, rcount, leaf_width)

    def leaf_pieces(x):
        if aligned:
            return x
        return jnp.moveaxis(x[0].reshape(leaves, rcount, n, leaf_cols), 2, 0)

    cuts = n if aligned else 1
    leaf_cut = leaf_width // cuts

    leaf_pos = row * leaf_local + jnp.arange(leaf_local, dtype=I32)
    leaf_list = jnp.where(leaf_pos[None, :] < leaf_height[:, None], leaf_rows, -1)
    parent_pos = row * parent_local + jnp.arange(parent_local, dtype=I32)
    parent_list = jnp.where(parent_pos[None, :] < parent_height[:, None], parent_rows, -1)
    leaf_plan = walk_plan(leaf_list, tall)
    parent_plan = walk_plan(parent_list, root_width)
    rhs_spread = lax.dynamic_update_slice_in_dim(
        jnp.zeros((rcount, root_width), F32), root_rhs, flat * root_cols, 1
    )

    lb = jnp.moveaxis(leaf_rhs.astype(BF16), 1, 0)
    lb = all_gather(jnp.broadcast_to(lb[None], (n,) + lb.shape))
    leaf_inv, leaf_panel = fetch(where, leaf_inv, leaf_panel)
    leaf_inverse = invert(leaf_list, leaf_plan, tall)
    parent_inverse = invert(parent_list, parent_plan, root_width)

    def leaf_solve(x_ref, w_ref, y_ref, copies_ref):
        for s in range(leaves):
            y = times_transposed(joined(x_ref, s), w_ref[s])
            y_ref[s] = y
            for j in range(n):
                copies_ref[j, s] = y.astype(BF16)

    ly, lyb = call(
        leaf_solve,
        [((leaves, rcount, leaf_cols), F32), ((n, leaves, rcount, leaf_cols), BF16)],
        [leaf_vector(lb), pinned(leaf_inv)],
        [VMEM] * 2,
        name="leaf_solve",
    )
    lyb = all_gather(lyb)
    parent_inv, parent_panel, root_inv = fetch(where, parent_inv[0], parent_panel[0], root_inv)

    def leaf_update(
        where_ref, plan_ref, x_ref, w_ref, inverse_ref, rhs_ref, own_ref, other_ref, root_ref,
        update_ref, acc_ref, sum_ref,
    ):
        acc_ref[...] = jnp.zeros(acc_ref.shape, F32)
        for s in range(leaves):
            update_ref[s] = times_transposed(joined(x_ref, s), w_ref[s])
        scatter_walk(plan_ref, inverse_ref, update_ref, acc_ref, leaf_local // LANES)
        for b in range(parent_width // LANES):
            sum_ref[:, b * LANES : (b + 1) * LANES] = -acc_ref[b]
        spot = pl.ds(pl.multiple_of(where_ref[2] * parent_cols, LANES), parent_cols)
        sum_ref[:, spot] += rhs_ref[...]
        deal(where_ref, sum_ref, own_ref, other_ref)
        for b in range(root_width // LANES):
            root_ref[b] = acc_ref[parent_width // LANES + b]

    own, other, root_acc = call(
        leaf_update,
        [
            ((chips, rcount, parent_cols), F32),
            ((chips, rcount, parent_cols), BF16),
            ((root_width // LANES, rcount, LANES), F32),
        ],
        [where, leaf_plan, leaf_vector(lyb), pinned(leaf_panel), leaf_inverse, parent_rhs[:, 0]],
        [SMEM, SMEM] + [VMEM] * 4,
        scratch=[
            pltpu.VMEM((leaves, rcount, leaf_local), F32),
            pltpu.VMEM((tall // LANES + 1, rcount, LANES), F32),
            pltpu.VMEM((rcount, parent_width), F32),
        ],
        name="leaf_update",
    )
    prb = chips_sum(own + swap(other).astype(F32)).astype(BF16)

    def parent_solve(where_ref, own_ref, other_ref, w_ref, y_ref, copies_ref, x_ref):
        unite(where_ref, own_ref, other_ref, x_ref)
        y = times_transposed(x_ref[...], w_ref[...])
        y_ref[...] = y
        for j in range(n):
            copies_ref[j] = y.astype(BF16)

    py, pyb = call(
        parent_solve,
        [((rcount, parent_cols), F32), ((n, rcount, parent_cols), BF16)],
        [where, prb, swap(prb), pinned(parent_inv)],
        [SMEM] + [VMEM] * 3,
        scratch=[pltpu.VMEM((rcount, parent_width), BF16)],
        name="parent_solve",
    )
    pyb = all_gather(pyb)

    def parent_update(
        where_ref, plan_ref, x_ref, w_ref, inverse_ref, root_ref, rhs_ref, own_ref, other_ref,
        update_ref, acc_ref, sum_ref,
    ):
        for b in range(root_width // LANES):
            acc_ref[b] = root_ref[b]
        update_ref[0] = times_transposed(joined(x_ref), w_ref[...])
        scatter_walk(plan_ref, inverse_ref, update_ref, acc_ref, parent_local // LANES)
        for b in range(root_width // LANES):
            lanes = slice(b * LANES, (b + 1) * LANES)
            sum_ref[:, lanes] = rhs_ref[:, lanes] - acc_ref[b]
        deal(where_ref, sum_ref, own_ref, other_ref)

    own, other = call(
        parent_update,
        [((chips, rcount, piece), F32), ((chips, rcount, piece), BF16)],
        [where, parent_plan, pyb, pinned(parent_panel), parent_inverse, root_acc, rhs_spread],
        [SMEM, SMEM] + [VMEM] * 5,
        scratch=[
            pltpu.VMEM((1, rcount, parent_local), F32),
            pltpu.VMEM((root_width // LANES + 1, rcount, LANES), F32),
            pltpu.VMEM((rcount, root_width), F32),
        ],
        name="parent_update",
    )
    rrb = chips_sum_at_once(leaf_sum(own + swap(other).astype(F32))).astype(BF16)

    def root_solve(where_ref, own_ref, other_ref, w_ref, own_out, other_out, x_ref, sum_ref):
        unite(where_ref, own_ref, other_ref, x_ref)
        y = times_transposed(x_ref[...], w_ref[...]).astype(BF16)
        sum_ref[...] = times(y, w_ref[...])
        deal(where_ref, sum_ref, own_out, other_out)

    own, other = call(
        root_solve,
        [((chips, rcount, piece), F32), ((chips, rcount, piece), BF16)],
        [where, rrb, swap(rrb), pinned(root_inv)],
        [SMEM] + [VMEM] * 3,
        scratch=[pltpu.VMEM((rcount, root_width), BF16), pltpu.VMEM((rcount, root_width), F32)],
        name="root_solve",
    )
    rxb = chips_sum_at_once(own + swap(other).astype(F32)).astype(BF16)

    def blocks_of(source_ref, target_ref, start, width):
        for b in range(width // LANES):
            target_ref[start + b] = source_ref[:, b * LANES : (b + 1) * LANES].astype(F32)

    def parent_back(
        where_ref, plan_ref, own_ref, other_ref, rows_ref, w_ref, out_ref, whole_ref,
        x_ref, found_ref,
    ):
        unite(where_ref, own_ref, other_ref, x_ref)
        blocks_of(x_ref, whole_ref, 0, root_width)
        whole_ref[root_width // LANES] = jnp.zeros((rcount, LANES), F32)
        gather_walk(plan_ref, rows_ref, whole_ref, found_ref)
        term = times(found_ref[0], w_ref[...])
        for j, part in enumerate(split(term, n)):
            out_ref[j] = part.astype(BF16)

    term, root_whole = call(
        parent_back,
        [((n, rcount, parent_cols), BF16), ((root_width // LANES + 1, rcount, LANES), F32)],
        [where, parent_plan, rxb, swap(rxb), parent_list, pinned(parent_panel)],
        [SMEM, SMEM] + [VMEM] * 4,
        scratch=[
            pltpu.VMEM((rcount, root_width), BF16),
            pltpu.VMEM((1, rcount, parent_local), BF16),
        ],
        name="parent_back",
    )
    tail = scatter_pieces(term)

    def parent_solve_back(where_ref, tail_ref, y_ref, w_ref, own_ref, other_ref, sum_ref):
        lost = sum(tail_ref[j].astype(F32) for j in range(n))
        sum_ref[...] = times((y_ref[...] - lost).astype(BF16), w_ref[...])
        deal(where_ref, sum_ref, own_ref, other_ref)

    own, other = call(
        parent_solve_back,
        [((chips, rcount, parent_cols), F32), ((chips, rcount, parent_cols), BF16)],
        [where, tail, py, pinned(parent_inv)],
        [SMEM] + [VMEM] * 3,
        scratch=[pltpu.VMEM((rcount, parent_width), F32)],
        name="parent_solve_back",
    )
    px = chips_sum(own + swap(other).astype(F32))
    pxb = px.astype(BF16)

    def leaf_back(
        where_ref, plan_ref, px_ref, own_ref, other_ref, root_ref, rows_ref, w_ref, out_ref, sol_ref,
        x_ref, whole_ref, found_ref,
    ):
        sol_ref[...] = px_ref[where_ref[1]]
        unite(where_ref, own_ref, other_ref, x_ref)
        blocks_of(x_ref, whole_ref, 0, parent_width)
        for b in range(root_width // LANES + 1):
            whole_ref[parent_width // LANES + b] = root_ref[b]
        gather_walk(plan_ref, rows_ref, whole_ref, found_ref)
        for s in range(leaves):
            for j, part in enumerate(split(times(found_ref[s], w_ref[s]), cuts)):
                out_ref[j, s] = part.astype(BF16)

    term, parent_sol = call(
        leaf_back,
        [((cuts, leaves, rcount, leaf_cut), BF16), ((rcount, parent_cols), F32)],
        [where, leaf_plan, px, pxb, swap(pxb), root_whole, leaf_list, pinned(leaf_panel)],
        [SMEM, SMEM] + [VMEM] * 6,
        scratch=[
            pltpu.VMEM((rcount, parent_width), BF16),
            pltpu.VMEM((tall // LANES + 1, rcount, LANES), F32),
            pltpu.VMEM((leaves, rcount, leaf_local), BF16),
        ],
        name="leaf_back",
    )
    tail = scatter_pieces(leaf_pieces(term))

    def leaf_solve_back(tail_ref, y_ref, w_ref, out_ref):
        for s in range(leaves):
            lost = sum(tail_ref[j, s].astype(F32) for j in range(n))
            term = times((y_ref[s] - lost).astype(BF16), w_ref[s])
            for j, part in enumerate(split(term, cuts)):
                out_ref[j, s] = part.astype(BF16)

    term = call(
        leaf_solve_back,
        [((cuts, leaves, rcount, leaf_cut), BF16)],
        [tail, ly, pinned(leaf_inv)],
        [VMEM] * 3,
        name="leaf_solve_back",
    )[0]
    leaf_sol = scatter_pieces(leaf_pieces(term)).astype(F32).sum(0)
    root_mine = jnp.moveaxis(root_whole[:-1], 0, 1).reshape(rcount, root_width)
    root_sol = lax.dynamic_slice_in_dim(root_mine, flat * root_cols, root_cols, 1)
    return (jnp.moveaxis(leaf_sol, 0, 1), parent_sol[:, None, :], root_sol)


def solution(mesh):
    return jax.shard_map(
        shards,
        mesh=mesh,
        in_specs=(
            P(None, "leaf", "rows"),
            P(None, "leaf", "rows"),
            P(None, ("leaf", "rows")),
            P("leaf", "rows", None),
            P("leaf", "rows", None),
            P("leaf", "rows"),
            P("leaf"),
            P("leaf", "rows", None),
            P("leaf", "rows", None),
            P("leaf", "rows"),
            P("leaf"),
            P("rows", None),
        ),
        out_specs=(P(None, "leaf", "rows"), P(None, "leaf", "rows"), P(None, ("leaf", "rows"))),
        check_vma=False,
    )
```

```python
import jax
import jax.numpy as jnp
from jax import lax
from jax.experimental import pallas as pl
from jax.experimental.pallas import tpu as pltpu
from jax.sharding import PartitionSpec as P

F32 = jnp.float32
BF16 = jnp.bfloat16
I32 = jnp.int32
LANES = 128
UNROLL = 4

VMEM = pl.BlockSpec(memory_space=pltpu.VMEM)
SMEM = pl.BlockSpec(memory_space=pltpu.SMEM)


def pinned(w):
    return pltpu.with_memory_space_constraint(w, pltpu.VMEM)


def call(
    body, outs, ins, specs, out_specs=None, scratch=(), moved=0, limit=6 << 20, name=None
):
    return pl.pallas_call(
        body,
        out_shape=[jax.ShapeDtypeStruct(s, d) for s, d in outs],
        in_specs=list(specs),
        out_specs=out_specs or [VMEM] * len(outs),
        scratch_shapes=list(scratch),
        cost_estimate=pl.CostEstimate(flops=0, bytes_accessed=moved, transcendentals=0),
        compiler_params=pltpu.CompilerParams(vmem_limit_bytes=limit),
        name=name,
    )(*ins)


def times_transposed(x, w):
    return lax.dot_general(x, w, (((1,), (1,)), ((), ())), preferred_element_type=F32)


def times(x, w):
    return lax.dot_general(x, w, (((1,), (0,)), ((), ())), preferred_element_type=F32)


def walk(plan_ref, sets, tiles, blocks, tile, visit, carry):
    def trip(i, carry):
        at = []
        for s in range(sets):
            lo = plan_ref[s * tiles + tile] + i * UNROLL
            at += [(s, jnp.minimum(lo + u, blocks)) for u in range(UNROLL)]
        return visit(at, carry)

    return lax.fori_loop(0, plan_ref[sets * tiles + tile], trip, carry)


def pick(x, index):
    inside = (index >= 0) & (index < LANES)
    found = jnp.take_along_axis(
        x, index & (LANES - 1), axis=1, mode="promise_in_bounds"
    )
    return jnp.where(inside, found, 0.0)


def prepare(lists, first, heights, widths):
    count = len(lists)

    def one(rows_ref, scalar_ref, height_ref, list_ref, plan_ref, out_ref, first, width):
        sets, length = rows_ref.shape
        tiles, blocks = length // LANES, width // LANES
        out_ref[...] = jnp.full(out_ref.shape, -1, I32)
        used = [height_ref[s] - first for s in range(sets)]
        lane = lax.broadcasted_iota(I32, (1, LANES), 1)
        for tile in range(tiles):
            lanes = slice(tile * LANES, (tile + 1) * LANES)
            spots = lax.broadcasted_iota(I32, (LANES, LANES), 0) + (tile * LANES + 1)
            cols, trips = [], 0
            for s in range(sets):
                line = jnp.where(lane + tile * LANES < used[s], rows_ref[s : s + 1, lanes], -1)
                list_ref[s : s + 1, lanes] = line
                cols.append(jnp.transpose(jnp.broadcast_to(line, (LANES, LANES))))
                end = jnp.maximum(jnp.minimum(used[s], (tile + 1) * LANES) - 1, 0)
                lo = lax.shift_right_logical(scalar_ref[s, tile * LANES], 7)
                hi = lax.shift_right_logical(scalar_ref[s, end], 7)
                met = used[s] > tile * LANES
                plan_ref[s * tiles + tile] = jnp.where(met, lo, blocks)
                span = jnp.where(met, hi - lo + UNROLL, 0)
                trips = jnp.maximum(trips, lax.div(span, UNROLL))
            plan_ref[sets * tiles + tile] = trips

            def visit(at, carry):
                across = lax.broadcasted_iota(I32, (LANES, LANES), 1)
                got = []
                for s, block in at:
                    hit = cols[s] == across + block * LANES
                    got.append(jnp.sum(jnp.where(hit, spots, 0), axis=0, keepdims=True))
                for (s, block), g in zip(at, got):
                    out_ref[s, block] += jnp.broadcast_to(g, out_ref.shape[2:])
                return carry

            walk(plan_ref, sets, tiles, blocks, tile, visit, 0)

    def body(*refs):
        ins, outs = refs[: 3 * count], refs[3 * count :]
        row = lax.axis_index("rows")
        for i in range(count):
            one(*ins[3 * i : 3 * i + 3], *outs[3 * i : 3 * i + 3], row * first[i], widths[i])

    shapes, specs, ins = [], [], []
    for rows, height, width in zip(lists, heights, widths):
        sets, length = rows.shape
        shapes += [
            (rows.shape, I32),
            (((sets + 1) * (length // LANES),), I32),
            ((sets, width // LANES + 1, 8, LANES), I32),
        ]
        ins += [rows, rows, height]
        specs += [VMEM, SMEM, SMEM]
    got = call(
        body,
        shapes,
        ins,
        specs,
        out_specs=[VMEM, SMEM, VMEM] * count,
        moved=16 << 20,
        limit=4 << 20,
        name="prepare",
    )
    return [got[3 * i : 3 * i + 3] for i in range(count)]


def scatter_walk(plan_ref, inverse_ref, update_ref, acc_ref, tiles):
    sets, blocks = inverse_ref.shape[0], inverse_ref.shape[1] - 1
    for tile in range(tiles):

        def visit(at, carry):
            got = []
            for s, block in at:
                x = update_ref[s, :, tile * LANES : (tile + 1) * LANES]
                got.append(pick(x, inverse_ref[s, block] - tile * LANES))
            for (s, block), g in zip(at, got):
                acc_ref[block] += g
            return carry

        walk(plan_ref, sets, tiles, blocks, tile, visit, 0)


def gather_walk(plan_ref, rows_ref, source_ref, out_ref):
    sets, length = rows_ref.shape
    tiles, blocks = length // LANES, source_ref.shape[0] - 1
    for tile in range(tiles):
        index = [
            jnp.broadcast_to(
                rows_ref[s : s + 1, tile * LANES : (tile + 1) * LANES], (8, LANES)
            )
            for s in range(sets)
        ]

        def visit(at, carry):
            carry = list(carry)
            for s, block in at:
                carry[s] = carry[s] + pick(source_ref[block], index[s] - block * LANES)
            return tuple(carry)

        zero = tuple(jnp.zeros((8, LANES), F32) for _ in range(sets))
        found = walk(plan_ref, sets, tiles, blocks, tile, visit, zero)
        for s in range(sets):
            out_ref[s, :, tile * LANES : (tile + 1) * LANES] = found[s].astype(out_ref.dtype)


def joined(ref, *at):
    return jnp.concatenate([ref[(j,) + at] for j in range(ref.shape[0])], axis=1)


def split(value, n):
    w = value.shape[1] // n
    return [value[:, j * w : (j + 1) * w] for j in range(n)]


def core():
    return lax.axis_index("rows") & 1


def chip():
    return lax.axis_index("rows") // 2


def spot(r, w):
    return pl.ds(pl.multiple_of(r * w, LANES), w)


def unite(own_ref, other_ref, out_ref, *at, xor=False):
    odd, w = core(), own_ref.shape[-1]
    for k in range(own_ref.shape[0]):
        c = chip() ^ k if xor else k
        out_ref[:, spot(2 * c + odd, w)] = own_ref[(k,) + at]
        out_ref[:, spot(2 * c + 1 - odd, w)] = other_ref[(k,) + at]


def deal(value_ref, own_ref, other_ref):
    odd = core()
    chips, _, w = own_ref.shape
    for k in range(chips):
        own_ref[k] = value_ref[:, spot(2 * k + odd, w)].astype(own_ref.dtype)
        other_ref[k] = value_ref[:, spot(2 * k + 1 - odd, w)].astype(other_ref.dtype)


def all_gather(copies):
    return lax.all_to_all(copies, "rows", 0, 0)


def scatter_pieces(x):
    return lax.all_to_all(x, "rows", 0, 0)


def swap(x):
    n = lax.axis_size("rows")
    return lax.ppermute(x, "rows", [(i, i ^ 1) for i in range(n)])


def far(x, k):
    n = lax.axis_size("rows")
    return lax.ppermute(x, "rows", [(i, i ^ (2 * k)) for i in range(n)])


def chips_sum(x):
    b = x.astype(BF16)
    return x + sum(far(b, k).astype(F32) for k in range(1, lax.axis_size("rows") // 2))


def leaf_sum(x):
    n = lax.axis_size("leaf")
    b = x.astype(BF16)
    for k in range(1, n):
        x = x + lax.ppermute(b, "leaf", [(i, (i + k) % n) for i in range(n)]).astype(F32)
    return x


def shards(
    leaf_rhs,
    parent_rhs,
    root_rhs,
    leaf_inv,
    leaf_panel,
    leaf_rows,
    leaf_height,
    parent_inv,
    parent_panel,
    parent_rows,
    parent_height,
    root_inv,
):
    n = lax.axis_size("rows")
    chips = n // 2
    rcount, leaves, leaf_cols = leaf_rhs.shape
    leaf_local, leaf_width = leaf_panel.shape[1:]
    parent_cols, parent_width = parent_inv.shape[1:]
    parent_local = parent_panel.shape[1]
    root_width = root_inv.shape[1]
    root_cols = root_rhs.shape[1]
    piece = root_width // n
    tall = parent_width + root_width
    leaf_aligned = leaf_cols % LANES == 0
    root_aligned = root_cols % LANES == 0

    def flat():
        return lax.axis_index("leaf") * n + lax.axis_index("rows")

    def leaf_gather(x, copies):
        if leaf_aligned and not copies:
            own = jnp.stack([x] + [far(x, k) for k in range(1, chips)])
            return own, swap(own)
        got = all_gather(x if copies else jnp.broadcast_to(x[None], (n,) + x.shape))
        if leaf_aligned:
            return (got,)
        return (jnp.moveaxis(got, 0, 2).reshape(1, leaves, rcount, leaf_width),)

    rhs = root_rhs
    if not root_aligned:
        rhs = lax.dynamic_update_slice_in_dim(
            jnp.zeros((rcount, root_width), F32), root_rhs, flat() * root_cols, 1
        )
    lb = leaf_gather(jnp.moveaxis(leaf_rhs.astype(BF16), 1, 0), False)
    prepared = prepare(
        [leaf_rows, parent_rows],
        [leaf_local, parent_local],
        [leaf_height, parent_height],
        [tall, root_width],
    )
    lb, prepared, parent_rhs, rhs = lax.optimization_barrier(
        (lb, prepared, parent_rhs[:, 0], rhs)
    )
    (leaf_list, leaf_plan, leaf_inverse), (parent_list, parent_plan, parent_inverse) = prepared

    def leaf_solve(*refs):
        x_refs, (w_ref, y_ref, copies_ref, x_ref) = refs[: len(lb)], refs[len(lb) :]
        for s in range(leaves):
            if len(lb) == 2:
                unite(*x_refs, x_ref, s, xor=True)
                x = x_ref[...]
            else:
                x = joined(x_refs[0], s)
            y = times_transposed(x, w_ref[s])
            y_ref[s] = y
            for j in range(n):
                copies_ref[j, s] = y.astype(BF16)

    ly, lyb = call(
        leaf_solve,
        [((leaves, rcount, leaf_cols), F32), ((n, leaves, rcount, leaf_cols), BF16)],
        [*lb, pinned(leaf_inv)],
        [VMEM] * (len(lb) + 1),
        scratch=[pltpu.VMEM((rcount, leaf_width), BF16)],
        name="leaf_solve",
    )
    (lyb,) = leaf_gather(lyb, True)

    def leaf_update(
        plan_ref, x_ref, w_ref, inverse_ref, rhs_ref, own_ref, other_ref, root_ref,
        update_ref, acc_ref, sum_ref,
    ):
        acc_ref[...] = jnp.zeros(acc_ref.shape, F32)
        for s in range(leaves):
            update_ref[s] = times_transposed(joined(x_ref, s), w_ref[s])
        scatter_walk(plan_ref, inverse_ref, update_ref, acc_ref, leaf_local // LANES)
        for b in range(parent_width // LANES):
            sum_ref[:, b * LANES : (b + 1) * LANES] = -acc_ref[b]
        sum_ref[:, spot(lax.axis_index("rows"), parent_cols)] += rhs_ref[...]
        deal(sum_ref, own_ref, other_ref)
        for b in range(root_width // LANES):
            root_ref[b] = acc_ref[parent_width // LANES + b]

    own, other, root_acc = call(
        leaf_update,
        [
            ((chips, rcount, parent_cols), F32),
            ((chips, rcount, parent_cols), BF16),
            ((root_width // LANES, rcount, LANES), F32),
        ],
        [leaf_plan, lyb, pinned(leaf_panel), leaf_inverse, parent_rhs],
        [SMEM] + [VMEM] * 4,
        scratch=[
            pltpu.VMEM((leaves, rcount, leaf_local), F32),
            pltpu.VMEM((tall // LANES + 1, rcount, LANES), F32),
            pltpu.VMEM((rcount, parent_width), F32),
        ],
        name="leaf_update",
    )
    prb = chips_sum(own + swap(other).astype(F32)).astype(BF16)

    def parent_solve(own_ref, other_ref, w_ref, y_ref, copies_ref, x_ref):
        unite(own_ref, other_ref, x_ref)
        y = times_transposed(x_ref[...], w_ref[0])
        y_ref[...] = y
        for j in range(n):
            copies_ref[j] = y.astype(BF16)

    py, pyb = call(
        parent_solve,
        [((rcount, parent_cols), F32), ((n, rcount, parent_cols), BF16)],
        [prb, swap(prb), pinned(parent_inv)],
        [VMEM] * 3,
        scratch=[pltpu.VMEM((rcount, parent_width), BF16)],
        name="parent_solve",
    )
    pyb = all_gather(pyb)

    def parent_update(
        plan_ref, x_ref, w_ref, inverse_ref, root_ref, rhs_ref, own_ref, other_ref,
        update_ref, acc_ref, sum_ref,
    ):
        for b in range(root_width // LANES):
            acc_ref[b] = root_ref[b]
        update_ref[0] = times_transposed(joined(x_ref), w_ref[0])
        scatter_walk(plan_ref, inverse_ref, update_ref, acc_ref, parent_local // LANES)
        for b in range(root_width // LANES):
            sum_ref[:, b * LANES : (b + 1) * LANES] = -acc_ref[b]
        if root_aligned:
            sum_ref[:, spot(flat(), root_cols)] += rhs_ref[...]
        else:
            sum_ref[...] += rhs_ref[...]
        deal(sum_ref, own_ref, other_ref)

    own, other = call(
        parent_update,
        [((chips, rcount, piece), F32), ((chips, rcount, piece), BF16)],
        [parent_plan, pyb, pinned(parent_panel), parent_inverse, root_acc, rhs],
        [SMEM] + [VMEM] * 5,
        scratch=[
            pltpu.VMEM((1, rcount, parent_local), F32),
            pltpu.VMEM((root_width // LANES + 1, rcount, LANES), F32),
            pltpu.VMEM((rcount, root_width), F32),
        ],
        name="parent_update",
    )
    rrb = chips_sum(leaf_sum(own + swap(other).astype(F32))).astype(BF16)

    def root_solve(own_ref, other_ref, w_ref, own_out, other_out, x_ref, sum_ref):
        unite(own_ref, other_ref, x_ref)
        y = times_transposed(x_ref[...], w_ref[...]).astype(BF16)
        sum_ref[...] = times(y, w_ref[...])
        deal(sum_ref, own_out, other_out)

    own, other = call(
        root_solve,
        [((chips, rcount, piece), F32), ((chips, rcount, piece), BF16)],
        [rrb, swap(rrb), pinned(root_inv)],
        [VMEM] * 3,
        scratch=[pltpu.VMEM((rcount, root_width), BF16), pltpu.VMEM((rcount, root_width), F32)],
        name="root_solve",
    )
    rxb = chips_sum(own + swap(other).astype(F32)).astype(BF16)

    def blocks_of(source_ref, target_ref, start, width):
        for b in range(width // LANES):
            target_ref[start + b] = source_ref[:, b * LANES : (b + 1) * LANES].astype(F32)

    def parent_back(
        plan_ref, own_ref, other_ref, rows_ref, w_ref, out_ref, whole_ref, sol_ref,
        x_ref, found_ref,
    ):
        unite(own_ref, other_ref, x_ref)
        if root_aligned:
            sol_ref[...] = x_ref[:, spot(flat(), root_cols)].astype(F32)
        else:
            sol_ref[...] = x_ref[...].astype(F32)
        blocks_of(x_ref, whole_ref, 0, root_width)
        whole_ref[root_width // LANES] = jnp.zeros((rcount, LANES), F32)
        gather_walk(plan_ref, rows_ref, whole_ref, found_ref)
        term = times(found_ref[0], w_ref[0])
        for j, part in enumerate(split(term, n)):
            out_ref[j] = part.astype(BF16)

    term, root_whole, root_sol = call(
        parent_back,
        [
            ((n, rcount, parent_cols), BF16),
            ((root_width // LANES + 1, rcount, LANES), F32),
            ((rcount, root_cols if root_aligned else root_width), F32),
        ],
        [parent_plan, rxb, swap(rxb), parent_list, pinned(parent_panel)],
        [SMEM] + [VMEM] * 4,
        scratch=[
            pltpu.VMEM((rcount, root_width), BF16),
            pltpu.VMEM((1, rcount, parent_local), BF16),
        ],
        name="parent_back",
    )
    tail = scatter_pieces(term)

    def parent_solve_back(tail_ref, y_ref, w_ref, own_ref, other_ref, sum_ref):
        lost = sum(tail_ref[j].astype(F32) for j in range(n))
        sum_ref[...] = times((y_ref[...] - lost).astype(BF16), w_ref[0])
        deal(sum_ref, own_ref, other_ref)

    own, other = call(
        parent_solve_back,
        [((chips, rcount, parent_cols), F32), ((chips, rcount, parent_cols), BF16)],
        [tail, py, pinned(parent_inv)],
        [VMEM] * 3,
        scratch=[pltpu.VMEM((rcount, parent_width), F32)],
        name="parent_solve_back",
    )
    px = chips_sum(own + swap(other).astype(F32))
    pxb = px.astype(BF16)

    def ancestors(
        plan_ref, px_ref, own_ref, other_ref, root_ref, rows_ref, sol_ref,
        x_ref, whole_ref, found_ref,
    ):
        sol_ref[...] = px_ref[chip()]
        unite(own_ref, other_ref, x_ref)
        blocks_of(x_ref, whole_ref, 0, parent_width)
        for b in range(root_width // LANES + 1):
            whole_ref[parent_width // LANES + b] = root_ref[b]
        gather_walk(plan_ref, rows_ref, whole_ref, found_ref)

    def terms(x_ref, w_ref, out_ref, odd):
        for k in range(chips):
            cols = spot(2 * (chip() ^ k) + odd, leaf_cols)
            for s in range(leaves):
                out_ref[k, s] = times(x_ref[s], w_ref[s, :, cols]).astype(out_ref.dtype)

    split_terms = (chips, leaves, rcount, leaf_cols)

    def own_terms(x, w, name):
        def body(x_ref, w_ref, out_ref):
            terms(x_ref, w_ref, out_ref, core())

        return call(
            body, [(split_terms, F32)], [x, pinned(w)], [VMEM] * 2, moved=12 << 20, name=name
        )[0]

    def leaf_reduce(own, other):
        other = swap(other)
        sums = [own[k] + other[k].astype(F32) for k in range(chips)]
        return [sums[0]] + [far(sums[k].astype(BF16), k) for k in range(1, chips)]

    def all_terms(x_ref, w_ref, out_ref):
        for s in range(leaves):
            out_ref[s] = times(x_ref[s], w_ref[s]).astype(BF16)

    def pieces_apart(term):
        return jnp.moveaxis(term.reshape(leaves, rcount, n, leaf_cols), 2, 0)

    whole_term = (leaves, rcount, leaf_width)
    found_shape = (leaves, rcount, leaf_local)
    scratch = [
        pltpu.VMEM((rcount, parent_width), BF16),
        pltpu.VMEM((tall // LANES + 1, rcount, LANES), F32),
    ]

    def leaf_back(*refs):
        ins, (w_ref, out_ref, sol_ref, found_ref, x_ref, whole_ref) = refs[:6], refs[6:]
        ancestors(*ins, sol_ref, x_ref, whole_ref, found_ref)
        if leaf_aligned:
            terms(found_ref, w_ref, out_ref, 1 - core())
        else:
            all_terms(found_ref, w_ref, out_ref)

    term, parent_sol, found = call(
        leaf_back,
        [
            (split_terms if leaf_aligned else whole_term, BF16),
            ((rcount, parent_cols), F32),
            (found_shape, BF16),
        ],
        [leaf_plan, px, pxb, swap(pxb), root_whole, leaf_list, pinned(leaf_panel)],
        [SMEM] + [VMEM] * 6,
        scratch=scratch,
        name="leaf_back",
    )
    if leaf_aligned:
        tails = leaf_reduce(own_terms(found, leaf_panel, "leaf_back_own"), term)
    else:
        tails = [scatter_pieces(pieces_apart(term)).astype(F32).sum(0)]

    def leaf_solve_back(*refs):
        tail_refs, (y_ref, w_ref, out_ref, v_ref) = refs[: len(tails)], refs[len(tails) :]
        for s in range(leaves):
            lost = sum(ref[s].astype(F32) for ref in tail_refs)
            v_ref[s] = (y_ref[s] - lost).astype(BF16)
        if leaf_aligned:
            terms(v_ref, w_ref, out_ref, 1 - core())
        else:
            all_terms(v_ref, w_ref, out_ref)

    term, lvb = call(
        leaf_solve_back,
        [
            (split_terms if leaf_aligned else whole_term, BF16),
            ((leaves, rcount, leaf_cols), BF16),
        ],
        [*tails, ly, pinned(leaf_inv)],
        [VMEM] * (len(tails) + 2),
        name="leaf_solve_back",
    )
    if leaf_aligned:
        parts = leaf_reduce(own_terms(lvb, leaf_inv, "leaf_solve_back_own"), term)
        leaf_sol = sum(p.astype(F32) for p in parts)
    else:
        leaf_sol = scatter_pieces(pieces_apart(term)).astype(F32).sum(0)
    if not root_aligned:
        root_sol = lax.dynamic_slice_in_dim(root_sol, flat() * root_cols, root_cols, 1)
    return (jnp.moveaxis(leaf_sol, 0, 1), parent_sol[:, None, :], root_sol)


def solution(mesh):
    return jax.shard_map(
        shards,
        mesh=mesh,
        in_specs=(
            P(None, "leaf", "rows"),
            P(None, "leaf", "rows"),
            P(None, ("leaf", "rows")),
            P("leaf", "rows", None),
            P("leaf", "rows", None),
            P("leaf", "rows"),
            P("leaf"),
            P("leaf", "rows", None),
            P("leaf", "rows", None),
            P("leaf", "rows"),
            P("leaf"),
            P("rows", None),
        ),
        out_specs=(P(None, "leaf", "rows"), P(None, "leaf", "rows"), P(None, ("leaf", "rows"))),
        check_vma=False,
    )
```

```python
import jax
import jax.numpy as jnp
from jax import lax
from jax.experimental import pallas as pl
from jax.experimental.pallas import tpu as pltpu
from jax.sharding import PartitionSpec as P

F32 = jnp.float32
BF16 = jnp.bfloat16
I32 = jnp.int32
LANES = 128
UNROLL = 4

VMEM = pl.BlockSpec(memory_space=pltpu.VMEM)
SMEM = pl.BlockSpec(memory_space=pltpu.SMEM)


def pinned(w):
    return pltpu.with_memory_space_constraint(w, pltpu.VMEM)


def call(
    body, outs, ins, specs, out_specs=None, scratch=(), moved=0, limit=6 << 20, name=None
):
    return pl.pallas_call(
        body,
        out_shape=[jax.ShapeDtypeStruct(*o) if isinstance(o, tuple) else o for o in outs],
        in_specs=list(specs),
        out_specs=out_specs or [VMEM] * len(outs),
        scratch_shapes=list(scratch),
        cost_estimate=pl.CostEstimate(flops=0, bytes_accessed=moved, transcendentals=0),
        compiler_params=pltpu.CompilerParams(vmem_limit_bytes=limit),
        name=name,
    )(*ins)


def times_transposed(x, w):
    return lax.dot_general(x, w, (((1,), (1,)), ((), ())), preferred_element_type=F32)


def times(x, w):
    return lax.dot_general(x, w, (((1,), (0,)), ((), ())), preferred_element_type=F32)


def split_at(refs, *counts):
    out = []
    for c in counts:
        out.append(refs[:c])
        refs = refs[c:]
    return *out, refs


def walk(plan_ref, sets, tiles, blocks, tile, visit, carry):
    def trip(i, carry):
        at = []
        for s in range(sets):
            lo = plan_ref[s * tiles + tile] + i * UNROLL
            at += [(s, jnp.minimum(lo + u, blocks)) for u in range(UNROLL)]
        return visit(at, carry)

    return lax.fori_loop(0, plan_ref[sets * tiles + tile], trip, carry)


def pick(x, index):
    inside = (index >= 0) & (index < LANES)
    found = jnp.take_along_axis(
        x, index & (LANES - 1), axis=1, mode="promise_in_bounds"
    )
    return jnp.where(inside, found, 0.0)


def prepare(weights, lists, first, heights, widths):
    count = len(lists)

    def one(rows_ref, scalar_ref, height_ref, list_ref, plan_ref, out_ref, first, width):
        sets, length = rows_ref.shape
        tiles, blocks = length // LANES, width // LANES
        out_ref[...] = jnp.full(out_ref.shape, -1, I32)
        used = [height_ref[s] - first for s in range(sets)]
        lane = lax.broadcasted_iota(I32, (1, LANES), 1)
        for tile in range(tiles):
            lanes = slice(tile * LANES, (tile + 1) * LANES)
            spots = lax.broadcasted_iota(I32, (LANES, LANES), 0) + (tile * LANES + 1)
            cols, trips = [], 0
            for s in range(sets):
                line = jnp.where(lane + tile * LANES < used[s], rows_ref[s : s + 1, lanes], -1)
                list_ref[s : s + 1, lanes] = line
                cols.append(jnp.transpose(jnp.broadcast_to(line, (LANES, LANES))))
                end = jnp.maximum(jnp.minimum(used[s], (tile + 1) * LANES) - 1, 0)
                lo = lax.shift_right_logical(scalar_ref[s, tile * LANES], 7)
                hi = lax.shift_right_logical(scalar_ref[s, end], 7)
                met = used[s] > tile * LANES
                plan_ref[s * tiles + tile] = jnp.where(met, lo, blocks)
                span = jnp.where(met, hi - lo + UNROLL, 0)
                trips = jnp.maximum(trips, lax.div(span, UNROLL))
            plan_ref[sets * tiles + tile] = trips

            def visit(at, carry):
                across = lax.broadcasted_iota(I32, (LANES, LANES), 1)
                got = []
                for s, block in at:
                    hit = cols[s] == across + block * LANES
                    got.append(jnp.sum(jnp.where(hit, spots, 0), axis=0, keepdims=True))
                for (s, block), g in zip(at, got):
                    out_ref[s, block] += jnp.broadcast_to(g, out_ref.shape[2:])
                return carry

            walk(plan_ref, sets, tiles, blocks, tile, visit, 0)

    held = len(weights)

    def body(*refs):
        sources, rows, heights, refs = split_at(refs, held, count, count)
        targets, outs, lines, scalars, (weight_sems, row_sems) = split_at(
            refs, held, 3 * count, count, count
        )
        row = lax.axis_index("rows")
        ahead = []
        for i in range(count):
            ahead.append(pltpu.make_async_copy(rows[i], lines[i], row_sems.at[2 * i]))
            ahead.append(pltpu.make_async_copy(rows[i], scalars[i], row_sems.at[2 * i + 1]))
        behind = [
            pltpu.make_async_copy(source, target, weight_sems.at[i])
            for i, (source, target) in enumerate(zip(sources, targets))
        ]
        for copy in ahead + behind:
            copy.start()
        for copy in ahead:
            copy.wait()
        for i in range(count):
            one(lines[i], scalars[i], heights[i], *outs[3 * i : 3 * i + 3], row * first[i], widths[i])
        for copy in behind:
            copy.wait()

    shapes = [pltpu.VMEM(w.shape, w.dtype) for w in weights]
    for rows, width in zip(lists, widths):
        sets, length = rows.shape
        shapes += [
            (rows.shape, I32),
            (((sets + 1) * (length // LANES),), I32),
            ((sets, width // LANES + 1, 8, LANES), I32),
        ]
    outside = pl.BlockSpec(memory_space=pltpu.HBM)
    got = call(
        body,
        shapes,
        [pltpu.with_memory_space_constraint(x, pltpu.HBM) for x in (*weights, *lists)] + heights,
        [outside] * (held + count) + [SMEM] * count,
        out_specs=[VMEM] * held + [VMEM, SMEM, VMEM] * count,
        scratch=[pltpu.VMEM(x.shape, I32) for x in lists]
        + [pltpu.SMEM(x.shape, I32) for x in lists]
        + [pltpu.SemaphoreType.DMA((held,)), pltpu.SemaphoreType.DMA((2 * count,))],
        moved=20 << 20,
        limit=4 << 20,
        name="prepare",
    )
    return got[:held], [got[held + 3 * i : held + 3 * i + 3] for i in range(count)]


def scatter_walk(plan_ref, inverse_ref, update_ref, acc_ref, tiles):
    sets, blocks = inverse_ref.shape[0], inverse_ref.shape[1] - 1
    for tile in range(tiles):

        def visit(at, carry):
            got = []
            for s, block in at:
                x = update_ref[s, :, tile * LANES : (tile + 1) * LANES]
                got.append(pick(x, inverse_ref[s, block] - tile * LANES))
            for (s, block), g in zip(at, got):
                acc_ref[block] += g
            return carry

        walk(plan_ref, sets, tiles, blocks, tile, visit, 0)


def gather_walk(plan_ref, rows_ref, source_ref, out_ref):
    sets, length = rows_ref.shape
    tiles, blocks = length // LANES, source_ref.shape[0] - 1
    for tile in range(tiles):
        index = [
            jnp.broadcast_to(
                rows_ref[s : s + 1, tile * LANES : (tile + 1) * LANES], (8, LANES)
            )
            for s in range(sets)
        ]

        def visit(at, carry):
            carry = list(carry)
            for s, block in at:
                carry[s] = carry[s] + pick(source_ref[block], index[s] - block * LANES)
            return tuple(carry)

        zero = tuple(jnp.zeros((8, LANES), F32) for _ in range(sets))
        found = walk(plan_ref, sets, tiles, blocks, tile, visit, zero)
        for s in range(sets):
            out_ref[s, :, tile * LANES : (tile + 1) * LANES] = found[s].astype(out_ref.dtype)


def core():
    return lax.axis_index("rows") & 1


def chip():
    return lax.axis_index("rows") // 2


def spot(r, w):
    return pl.ds(pl.multiple_of(r * w, LANES), w)


def unite(own_ref, other_ref, out_ref, *at, xor=False):
    odd, w = core(), own_ref.shape[-1]
    for k in range(own_ref.shape[0]):
        c = chip() ^ k if xor else k
        out_ref[:, spot(2 * c + odd, w)] = own_ref[(k,) + at]
        out_ref[:, spot(2 * c + 1 - odd, w)] = other_ref[(k,) + at]


def deal(value_ref, own_ref, other_ref):
    odd = core()
    chips, _, w = own_ref.shape
    for k in range(chips):
        own_ref[k] = value_ref[:, spot(2 * k + odd, w)].astype(own_ref.dtype)
        other_ref[k] = value_ref[:, spot(2 * k + 1 - odd, w)].astype(other_ref.dtype)


def all_to_all(x):
    return lax.all_to_all(x, "rows", 0, 0)


def swap(x):
    n = lax.axis_size("rows")
    return lax.ppermute(x, "rows", [(i, i ^ 1) for i in range(n)])


def far(x, k):
    n = lax.axis_size("rows")
    return lax.ppermute(x, "rows", [(i, i ^ (2 * k)) for i in range(n)])


def chips_sum(x):
    b = x.astype(BF16)
    return x + sum(far(b, k).astype(F32) for k in range(1, lax.axis_size("rows") // 2))


def leaf_sum(x):
    n = lax.axis_size("leaf")
    b = x.astype(BF16)
    for k in range(1, n):
        x = x + lax.ppermute(b, "leaf", [(i, (i + k) % n) for i in range(n)]).astype(F32)
    return x


def shards(
    leaf_rhs,
    parent_rhs,
    root_rhs,
    leaf_inv,
    leaf_panel,
    leaf_rows,
    leaf_height,
    parent_inv,
    parent_panel,
    parent_rows,
    parent_height,
    root_inv,
):
    n = lax.axis_size("rows")
    chips = n // 2
    rcount, leaves, leaf_cols = leaf_rhs.shape
    leaf_local, leaf_width = leaf_panel.shape[1:]
    parent_cols, parent_width = parent_inv.shape[1:]
    parent_local = parent_panel.shape[1]
    root_width = root_inv.shape[1]
    root_cols = root_rhs.shape[1]
    piece = root_width // n
    tall = parent_width + root_width
    leaf_aligned = leaf_cols % LANES == 0
    root_aligned = root_cols % LANES == 0

    def flat():
        return lax.axis_index("leaf") * n + lax.axis_index("rows")

    def far_gather(x):
        return jnp.stack([x] + [far(x, k) for k in range(1, chips)])

    def leaf_columns(x):
        got = all_to_all(jnp.broadcast_to(x[None], (n,) + x.shape))
        return jnp.moveaxis(got, 0, 2).reshape(1, leaves, rcount, leaf_width)

    def join_in(x_refs, x_ref, *at):
        if len(x_refs) == 1:
            return x_refs[0][(0,) + at]
        unite(*x_refs, x_ref, *at, xor=True)
        return x_ref[...]

    rhs = root_rhs
    if not root_aligned:
        rhs = lax.dynamic_update_slice_in_dim(
            jnp.zeros((rcount, root_width), F32), root_rhs, flat() * root_cols, 1
        )
    lb = jnp.moveaxis(leaf_rhs.astype(BF16), 1, 0)
    lb = far_gather(lb) if leaf_aligned else leaf_columns(lb)
    early, prepared = prepare(
        [leaf_inv, leaf_panel],
        [leaf_rows, parent_rows],
        [leaf_local, parent_local],
        [leaf_height, parent_height],
        [tall, root_width],
    )
    lb, early, prepared, rhs = lax.optimization_barrier((lb, early, prepared, rhs))
    leaf_inv_early, leaf_panel_early = early
    (leaf_list, leaf_plan, leaf_inverse), (parent_list, parent_plan, parent_inverse) = prepared
    lb = (lb, swap(lb)) if leaf_aligned else (lb,)

    def leaf_solve(*refs):
        x_refs, (w_ref, y_ref, send_ref, x_ref) = refs[: len(lb)], refs[len(lb) :]
        for s in range(leaves):
            y = times_transposed(join_in(x_refs, x_ref, s), w_ref[s])
            y_ref[s] = y
            send_ref[s] = y.astype(BF16)

    ly, lyb = call(
        leaf_solve,
        [((leaves, rcount, leaf_cols), F32), ((leaves, rcount, leaf_cols), BF16)],
        [*lb, pinned(leaf_inv_early)],
        [VMEM] * (len(lb) + 1),
        scratch=[pltpu.VMEM((rcount, leaf_width), BF16)],
        name="leaf_solve",
    )
    if leaf_aligned:
        lyb = far_gather(lyb)
        lyb = (lyb, swap(lyb))
    else:
        lyb = (leaf_columns(lyb),)

    def leaf_update(*refs):
        x_refs, refs = refs[: len(lyb)], refs[len(lyb) :]
        plan_ref, w_ref, inverse_ref, rhs_ref, own_ref, other_ref, root_ref, *refs = refs
        x_ref, update_ref, acc_ref, sum_ref = refs
        acc_ref[...] = jnp.zeros(acc_ref.shape, F32)
        for s in range(leaves):
            update_ref[s] = times_transposed(join_in(x_refs, x_ref, s), w_ref[s])
        scatter_walk(plan_ref, inverse_ref, update_ref, acc_ref, leaf_local // LANES)
        for b in range(parent_width // LANES):
            sum_ref[:, b * LANES : (b + 1) * LANES] = -acc_ref[b]
        sum_ref[:, spot(lax.axis_index("rows"), parent_cols)] += rhs_ref[:, 0, :]
        deal(sum_ref, own_ref, other_ref)
        for b in range(root_width // LANES):
            root_ref[b] = acc_ref[parent_width // LANES + b]

    own, other, root_acc = call(
        leaf_update,
        [
            ((chips, rcount, parent_cols), F32),
            ((chips, rcount, parent_cols), BF16),
            ((root_width // LANES, rcount, LANES), F32),
        ],
        [*lyb, leaf_plan, pinned(leaf_panel_early), leaf_inverse, parent_rhs],
        [VMEM] * len(lyb) + [SMEM] + [VMEM] * 3,
        scratch=[
            pltpu.VMEM((rcount, leaf_width), BF16),
            pltpu.VMEM((leaves, rcount, leaf_local), F32),
            pltpu.VMEM((tall // LANES + 1, rcount, LANES), F32),
            pltpu.VMEM((rcount, parent_width), F32),
        ],
        name="leaf_update",
    )
    prb = chips_sum(own + swap(other).astype(F32)).astype(BF16)

    def parent_solve(own_ref, other_ref, w_ref, y_ref, send_ref, x_ref):
        unite(own_ref, other_ref, x_ref)
        y = times_transposed(x_ref[...], w_ref[0])
        y_ref[...] = y
        send_ref[...] = y.astype(BF16)

    py, pyb = call(
        parent_solve,
        [((rcount, parent_cols), F32), ((rcount, parent_cols), BF16)],
        [prb, swap(prb), pinned(parent_inv)],
        [VMEM] * 3,
        scratch=[pltpu.VMEM((rcount, parent_width), BF16)],
        name="parent_solve",
    )
    pyb = far_gather(pyb)

    def parent_update(
        plan_ref, x_own_ref, x_other_ref, w_ref, inverse_ref, root_ref, rhs_ref, own_ref, other_ref,
        x_ref, update_ref, acc_ref, sum_ref,
    ):
        unite(x_own_ref, x_other_ref, x_ref, xor=True)
        for b in range(root_width // LANES):
            acc_ref[b] = root_ref[b]
        update_ref[0] = times_transposed(x_ref[...], w_ref[0])
        scatter_walk(plan_ref, inverse_ref, update_ref, acc_ref, parent_local // LANES)
        for b in range(root_width // LANES):
            sum_ref[:, b * LANES : (b + 1) * LANES] = -acc_ref[b]
        if root_aligned:
            sum_ref[:, spot(flat(), root_cols)] += rhs_ref[...]
        else:
            sum_ref[...] += rhs_ref[...]
        deal(sum_ref, own_ref, other_ref)

    own, other = call(
        parent_update,
        [((chips, rcount, piece), F32), ((chips, rcount, piece), BF16)],
        [parent_plan, pyb, swap(pyb), pinned(parent_panel), parent_inverse, root_acc, rhs],
        [SMEM] + [VMEM] * 6,
        scratch=[
            pltpu.VMEM((rcount, parent_width), BF16),
            pltpu.VMEM((1, rcount, parent_local), F32),
            pltpu.VMEM((root_width // LANES + 1, rcount, LANES), F32),
            pltpu.VMEM((rcount, root_width), F32),
        ],
        name="parent_update",
    )
    rrb = chips_sum(leaf_sum(own + swap(other).astype(F32))).astype(BF16)

    def root_solve(own_ref, other_ref, w_ref, own_out, other_out, x_ref, sum_ref):
        unite(own_ref, other_ref, x_ref)
        y = times_transposed(x_ref[...], w_ref[...]).astype(BF16)
        sum_ref[...] = times(y, w_ref[...])
        deal(sum_ref, own_out, other_out)

    own, other = call(
        root_solve,
        [((chips, rcount, piece), F32), ((chips, rcount, piece), BF16)],
        [rrb, swap(rrb), pinned(root_inv)],
        [VMEM] * 3,
        scratch=[pltpu.VMEM((rcount, root_width), BF16), pltpu.VMEM((rcount, root_width), F32)],
        name="root_solve",
    )
    rxb = chips_sum(own + swap(other).astype(F32)).astype(BF16)

    def blocks_of(source_ref, target_ref, start, width):
        for b in range(width // LANES):
            target_ref[start + b] = source_ref[:, b * LANES : (b + 1) * LANES].astype(F32)

    def terms(x_ref, w_ref, out_ref, odd):
        _, sets, _, cols = out_ref.shape
        for k in range(chips):
            at = spot(2 * (chip() ^ k) + odd, cols)
            for s in range(sets):
                out_ref[k, s] = times(x_ref[s], w_ref[s, :, at]).astype(out_ref.dtype)

    def split_terms(w):
        return (chips, w.shape[0], rcount, w.shape[2] // n)

    def own_terms(x, w, name):
        def body(x_ref, w_ref, out_ref):
            terms(x_ref, w_ref, out_ref, core())

        return call(
            body, [(split_terms(w), F32)], [x, pinned(w)], [VMEM] * 2, moved=12 << 20, name=name
        )[0]

    def reduce(own, other):
        other = swap(other)
        sums = [own[k] + other[k].astype(F32) for k in range(chips)]
        return [sums[0]] + [far(sums[k].astype(BF16), k) for k in range(1, chips)]

    def parent_back(
        plan_ref, own_ref, other_ref, rows_ref, w_ref, out_ref, whole_ref, sol_ref, found_ref, x_ref,
    ):
        unite(own_ref, other_ref, x_ref)
        if root_aligned:
            sol_ref[...] = x_ref[:, spot(flat(), root_cols)].astype(F32)
        else:
            sol_ref[...] = x_ref[...].astype(F32)
        blocks_of(x_ref, whole_ref, 0, root_width)
        whole_ref[root_width // LANES] = jnp.zeros((rcount, LANES), F32)
        gather_walk(plan_ref, rows_ref, whole_ref, found_ref)
        terms(found_ref, w_ref, out_ref, 1 - core())

    term, root_whole, root_sol, found = call(
        parent_back,
        [
            (split_terms(parent_panel), BF16),
            ((root_width // LANES + 1, rcount, LANES), F32),
            ((rcount, root_cols if root_aligned else root_width), F32),
            ((1, rcount, parent_local), BF16),
        ],
        [parent_plan, rxb, swap(rxb), parent_list, pinned(parent_panel)],
        [SMEM] + [VMEM] * 4,
        scratch=[pltpu.VMEM((rcount, root_width), BF16)],
        name="parent_back",
    )
    tails = reduce(own_terms(found, parent_panel, "parent_back_own"), term)

    def parent_solve_back(*refs):
        tail_refs, (y_ref, w_ref, own_ref, other_ref, sum_ref) = refs[:chips], refs[chips:]
        lost = sum(ref[0].astype(F32) for ref in tail_refs)
        sum_ref[...] = times((y_ref[...] - lost).astype(BF16), w_ref[0])
        deal(sum_ref, own_ref, other_ref)

    own, other = call(
        parent_solve_back,
        [((chips, rcount, parent_cols), F32), ((chips, rcount, parent_cols), BF16)],
        [*tails, py, pinned(parent_inv)],
        [VMEM] * (chips + 2),
        scratch=[pltpu.VMEM((rcount, parent_width), F32)],
        name="parent_solve_back",
    )
    px = chips_sum(own + swap(other).astype(F32))
    pxb = px.astype(BF16)

    def ancestors(
        plan_ref, px_ref, own_ref, other_ref, root_ref, rows_ref, sol_ref,
        x_ref, whole_ref, found_ref,
    ):
        sol_ref[...] = px_ref[chip()]
        unite(own_ref, other_ref, x_ref)
        blocks_of(x_ref, whole_ref, 0, parent_width)
        for b in range(root_width // LANES + 1):
            whole_ref[parent_width // LANES + b] = root_ref[b]
        gather_walk(plan_ref, rows_ref, whole_ref, found_ref)

    def all_terms(x_ref, w_ref, out_ref):
        for s in range(leaves):
            out_ref[s] = times(x_ref[s], w_ref[s]).astype(BF16)

    def pieces_apart(term):
        return jnp.moveaxis(term.reshape(leaves, rcount, n, leaf_cols), 2, 0)

    whole_term = (leaves, rcount, leaf_width)
    found_shape = (leaves, rcount, leaf_local)
    scratch = [
        pltpu.VMEM((rcount, parent_width), BF16),
        pltpu.VMEM((tall // LANES + 1, rcount, LANES), F32),
    ]

    def leaf_back(*refs):
        ins, (w_ref, out_ref, sol_ref, found_ref, x_ref, whole_ref) = refs[:6], refs[6:]
        ancestors(*ins, sol_ref, x_ref, whole_ref, found_ref)
        if leaf_aligned:
            terms(found_ref, w_ref, out_ref, 1 - core())
        else:
            all_terms(found_ref, w_ref, out_ref)

    term, parent_sol, found = call(
        leaf_back,
        [
            (split_terms(leaf_panel) if leaf_aligned else whole_term, BF16),
            ((rcount, parent_cols), F32),
            (found_shape, BF16),
        ],
        [leaf_plan, px, pxb, swap(pxb), root_whole, leaf_list, pinned(leaf_panel)],
        [SMEM] + [VMEM] * 6,
        scratch=scratch,
        name="leaf_back",
    )
    if leaf_aligned:
        tails = reduce(own_terms(found, leaf_panel, "leaf_back_own"), term)
    else:
        tails = [all_to_all(pieces_apart(term)).astype(F32).sum(0)]

    def leaf_solve_back(*refs):
        tail_refs, (y_ref, w_ref, out_ref, v_ref) = refs[: len(tails)], refs[len(tails) :]
        for s in range(leaves):
            lost = sum(ref[s].astype(F32) for ref in tail_refs)
            v_ref[s] = (y_ref[s] - lost).astype(BF16)
        if leaf_aligned:
            terms(v_ref, w_ref, out_ref, 1 - core())
        else:
            all_terms(v_ref, w_ref, out_ref)

    term, lvb = call(
        leaf_solve_back,
        [
            (split_terms(leaf_panel) if leaf_aligned else whole_term, BF16),
            ((leaves, rcount, leaf_cols), BF16),
        ],
        [*tails, ly, pinned(leaf_inv)],
        [VMEM] * (len(tails) + 2),
        name="leaf_solve_back",
    )
    if leaf_aligned:
        parts = reduce(own_terms(lvb, leaf_inv, "leaf_solve_back_own"), term)
        leaf_sol = sum(p.astype(F32) for p in parts)
    else:
        leaf_sol = all_to_all(pieces_apart(term)).astype(F32).sum(0)
    if not root_aligned:
        root_sol = lax.dynamic_slice_in_dim(root_sol, flat() * root_cols, root_cols, 1)
    return (jnp.moveaxis(leaf_sol, 0, 1), parent_sol[:, None, :], root_sol)


def solution(mesh):
    return jax.shard_map(
        shards,
        mesh=mesh,
        in_specs=(
            P(None, "leaf", "rows"),
            P(None, "leaf", "rows"),
            P(None, ("leaf", "rows")),
            P("leaf", "rows", None),
            P("leaf", "rows", None),
            P("leaf", "rows"),
            P("leaf"),
            P("leaf", "rows", None),
            P("leaf", "rows", None),
            P("leaf", "rows"),
            P("leaf"),
            P("rows", None),
        ),
        out_specs=(P(None, "leaf", "rows"), P(None, "leaf", "rows"), P(None, ("leaf", "rows"))),
        check_vma=False,
    )
```

```python
import jax
import jax.numpy as jnp
from jax import lax
from jax.experimental import pallas as pl
from jax.experimental.pallas import tpu as pltpu
from jax.sharding import PartitionSpec as P

F32 = jnp.float32
BF16 = jnp.bfloat16
I32 = jnp.int32
LANES = 128
UNROLL = 4

VMEM = pl.BlockSpec(memory_space=pltpu.VMEM)
SMEM = pl.BlockSpec(memory_space=pltpu.SMEM)


def pinned(w):
    return pltpu.with_memory_space_constraint(w, pltpu.VMEM)


def outside(w):
    return pltpu.with_memory_space_constraint(w, pltpu.HBM)


def call(
    body, outs, ins, specs, out_specs=None, scratch=(), moved=0, limit=6 << 20, name=None
):
    return pl.pallas_call(
        body,
        out_shape=[jax.ShapeDtypeStruct(*o) if isinstance(o, tuple) else o for o in outs],
        in_specs=list(specs),
        out_specs=out_specs or [VMEM] * len(outs),
        scratch_shapes=list(scratch),
        cost_estimate=pl.CostEstimate(flops=0, bytes_accessed=moved, transcendentals=0),
        compiler_params=pltpu.CompilerParams(vmem_limit_bytes=limit),
        name=name,
    )(*ins)


def times_transposed(x, w):
    return lax.dot_general(x, w, (((1,), (1,)), ((), ())), preferred_element_type=F32)


def times(x, w):
    return lax.dot_general(x, w, (((1,), (0,)), ((), ())), preferred_element_type=F32)


def walk(plan_ref, sets, tiles, blocks, tile, visit, carry):
    def trip(i, carry):
        at = []
        for s in range(sets):
            lo = plan_ref[s * tiles + tile] + i * UNROLL
            at += [(s, jnp.minimum(lo + u, blocks)) for u in range(UNROLL)]
        return visit(at, carry)

    return lax.fori_loop(0, plan_ref[sets * tiles + tile], trip, carry)


def pick(x, index):
    inside = (index >= 0) & (index < LANES)
    found = jnp.take_along_axis(
        x, index & (LANES - 1), axis=1, mode="promise_in_bounds"
    )
    return jnp.where(inside, found, 0.0)


def prepare(after, rows, first, height, width, sets):
    of = range(*sets)
    sets, length = rows.shape
    tiles, blocks = length // LANES, width // LANES

    def body(after_ref, given_ref, height_ref, list_ref, plan_ref, out_ref, rows_ref, scalar_ref, sems):
        copies = [
            pltpu.make_async_copy(given_ref, target, sems.at[i])
            for i, target in enumerate((rows_ref, scalar_ref))
        ]
        for copy in copies:
            copy.start()
        out_ref[...] = jnp.full(out_ref.shape, -1, I32)
        start = lax.axis_index("rows") * first
        used = [height_ref[s] - start for s in range(sets)]
        for copy in copies:
            copy.wait()
        lane = lax.broadcasted_iota(I32, (1, LANES), 1)
        for tile in range(tiles):
            lanes = slice(tile * LANES, (tile + 1) * LANES)
            spots = lax.broadcasted_iota(I32, (LANES, LANES), 0) + (tile * LANES + 1)
            cols, trips = [], 0
            for s in range(sets):
                line = jnp.where(lane + tile * LANES < used[s], rows_ref[s : s + 1, lanes], -1)
                list_ref[s : s + 1, lanes] = line
                if s in of:
                    cols.append(jnp.transpose(jnp.broadcast_to(line, (LANES, LANES))))
                end = jnp.maximum(jnp.minimum(used[s], (tile + 1) * LANES) - 1, 0)
                lo = lax.shift_right_logical(scalar_ref[s, tile * LANES], 7)
                hi = lax.shift_right_logical(scalar_ref[s, end], 7)
                met = used[s] > tile * LANES
                plan_ref[s * tiles + tile] = jnp.where(met, lo, blocks)
                span = jnp.where(met, hi - lo + UNROLL, 0)
                trips = jnp.maximum(trips, lax.div(span, UNROLL))
            plan_ref[sets * tiles + tile] = trips

            def visit(at, carry):
                across = lax.broadcasted_iota(I32, (LANES, LANES), 1)
                got = []
                at = [(s - of.start, block) for s, block in at if s in of]
                for s, block in at:
                    hit = cols[s] == across + block * LANES
                    got.append(jnp.sum(jnp.where(hit, spots, 0), axis=0, keepdims=True))
                for (s, block), g in zip(at, got):
                    out_ref[s, block] += jnp.broadcast_to(g, out_ref.shape[2:])
                return carry

            walk(plan_ref, sets, tiles, blocks, tile, visit, 0)

    return call(
        body,
        [
            (rows.shape, I32),
            (((sets + 1) * tiles,), I32),
            ((len(of), blocks + 1, 8, LANES), I32),
        ],
        [after, outside(rows), height],
        [pl.BlockSpec(memory_space=pl.ANY), pl.BlockSpec(memory_space=pltpu.HBM), SMEM],
        out_specs=[VMEM, SMEM, VMEM],
        scratch=[
            pltpu.VMEM(rows.shape, I32),
            pltpu.SMEM(rows.shape, I32),
            pltpu.SemaphoreType.DMA((2,)),
        ],
        moved=8 << 20,
        limit=4 << 20,
        name="prepare",
    )


def scatter_walk(plan_ref, inverse_refs, update_ref, acc_ref, tiles):
    sets, blocks = update_ref.shape[0], inverse_refs[0].shape[1] - 1
    inverse = [ref.at[s] for ref in inverse_refs for s in range(ref.shape[0])]
    for tile in range(tiles):

        def visit(at, carry):
            got = []
            for s, block in at:
                x = update_ref[s, :, tile * LANES : (tile + 1) * LANES]
                got.append(pick(x, inverse[s][block] - tile * LANES))
            for (s, block), g in zip(at, got):
                acc_ref[block] += g
            return carry

        walk(plan_ref, sets, tiles, blocks, tile, visit, 0)


def gather_walk(plan_ref, rows_ref, source_ref, out_ref):
    sets, length = rows_ref.shape
    tiles, blocks = length // LANES, source_ref.shape[0] - 1
    for tile in range(tiles):
        index = [
            jnp.broadcast_to(
                rows_ref[s : s + 1, tile * LANES : (tile + 1) * LANES], (8, LANES)
            )
            for s in range(sets)
        ]

        def visit(at, carry):
            carry = list(carry)
            for s, block in at:
                carry[s] = carry[s] + pick(source_ref[block], index[s] - block * LANES)
            return tuple(carry)

        zero = tuple(jnp.zeros((8, LANES), F32) for _ in range(sets))
        found = walk(plan_ref, sets, tiles, blocks, tile, visit, zero)
        for s in range(sets):
            out_ref[s, :, tile * LANES : (tile + 1) * LANES] = found[s].astype(out_ref.dtype)


def core():
    return lax.axis_index("rows") & 1


def chip():
    return lax.axis_index("rows") // 2


def spot(r, w):
    return pl.ds(pl.multiple_of(r * w, LANES), w)


def unite(own_ref, other_ref, out_ref, *at, xor=False):
    odd, w = core(), own_ref.shape[-1]
    for k in range(own_ref.shape[0]):
        c = chip() ^ (-k % own_ref.shape[0]) if xor else k
        out_ref[:, spot(2 * c + odd, w)] = own_ref[(k,) + at]
        out_ref[:, spot(2 * c + 1 - odd, w)] = other_ref[(k,) + at]


def deal(value_ref, own_ref, other_ref):
    odd = core()
    chips, _, w = own_ref.shape
    for k in range(chips):
        own_ref[k] = value_ref[:, spot(2 * k + odd, w)].astype(own_ref.dtype)
        other_ref[k] = value_ref[:, spot(2 * k + 1 - odd, w)].astype(other_ref.dtype)


def all_to_all(x):
    return lax.all_to_all(x, "rows", 0, 0)


def swap(x):
    n = lax.axis_size("rows")
    return lax.ppermute(x, "rows", [(i, i ^ 1) for i in range(n)])


def far(x, k):
    n = lax.axis_size("rows")
    return lax.ppermute(x, "rows", [(i, i ^ (2 * k)) for i in range(n)])


def from_chips(piece):
    chips = lax.axis_size("rows") // 2
    return [far(piece(k), k) for k in range(chips - 1, 0, -1)]


def chips_sum(x):
    b = x.astype(BF16)
    return x + sum(got.astype(F32) for got in from_chips(lambda k: b))


def leaf_sum(x):
    n = lax.axis_size("leaf")
    b = x.astype(BF16)
    for k in range(1, n):
        x = x + lax.ppermute(b, "leaf", [(i, (i + k) % n) for i in range(n)]).astype(F32)
    return x


def shards(
    leaf_rhs,
    parent_rhs,
    root_rhs,
    leaf_inv,
    leaf_panel,
    leaf_rows,
    leaf_height,
    parent_inv,
    parent_panel,
    parent_rows,
    parent_height,
    root_inv,
):
    n = lax.axis_size("rows")
    chips = n // 2
    rcount, leaves, leaf_cols = leaf_rhs.shape
    leaf_local, leaf_width = leaf_panel.shape[1:]
    parent_cols, parent_width = parent_inv.shape[1:]
    parent_local = parent_panel.shape[1]
    root_width = root_inv.shape[1]
    root_cols = root_rhs.shape[1]
    piece = root_width // n
    tall = parent_width + root_width
    leaf_aligned = leaf_cols % LANES == 0
    root_aligned = root_cols % LANES == 0

    def flat():
        return lax.axis_index("leaf") * n + lax.axis_index("rows")

    def far_gather(x):
        return jnp.stack([x] + from_chips(lambda k: x))

    def leaf_columns(x):
        got = all_to_all(jnp.broadcast_to(x[None], (n,) + x.shape))
        return jnp.moveaxis(got, 0, 2).reshape(1, leaves, rcount, leaf_width)

    def join_in(x_refs, x_ref, *at):
        if len(x_refs) == 1:
            return x_refs[0][(0,) + at]
        unite(*x_refs, x_ref, *at, xor=True)
        return x_ref[...]

    rhs = root_rhs
    if not root_aligned:
        rhs = lax.dynamic_update_slice_in_dim(
            jnp.zeros((rcount, root_width), F32), root_rhs, flat() * root_cols, 1
        )
    weights = (leaf_inv, leaf_panel, parent_inv, parent_panel, root_inv)

    def round_rhs(x_ref, *refs):
        out_ref = refs[-1]
        for s in range(leaves):
            out_ref[s] = x_ref[:, s, :].astype(BF16)

    lb = call(
        round_rhs,
        [((leaves, rcount, leaf_cols), BF16)],
        [leaf_rhs] + [outside(w) for w in weights],
        [VMEM] + [pl.BlockSpec(memory_space=pltpu.HBM)] * len(weights),
        name="round_rhs",
    )[0]
    half = leaves // 2

    def prepare_leaves(after, *sets):
        return prepare(after, leaf_rows, leaf_local, leaf_height, tall, sets)

    leaf_list, leaf_plan, inverse_low = prepare_leaves(lb, 0, half)
    lb = far_gather(lb) if leaf_aligned else leaf_columns(lb)
    lb, inverse_low, rhs = lax.optimization_barrier((lb, inverse_low, rhs))
    lb = (lb, swap(lb)) if leaf_aligned else (lb,)

    def leaf_solve(*refs):
        x_refs, (w_ref, y_ref, send_ref, x_ref) = refs[: len(lb)], refs[len(lb) :]
        for s in range(leaves):
            y = times_transposed(join_in(x_refs, x_ref, s), w_ref[s])
            y_ref[s] = y
            send_ref[s] = y.astype(BF16)

    ly, lyb = call(
        leaf_solve,
        [((leaves, rcount, leaf_cols), F32), ((leaves, rcount, leaf_cols), BF16)],
        [*lb, pinned(leaf_inv)],
        [VMEM] * (len(lb) + 1),
        scratch=[pltpu.VMEM((rcount, leaf_width), BF16)],
        name="leaf_solve",
    )
    inverse_high = prepare_leaves(lyb, half, leaves)[2]
    if leaf_aligned:
        lyb, inverse_high = lax.optimization_barrier((far_gather(lyb), inverse_high))
        lyb = (lyb, swap(lyb))
    else:
        lyb = (leaf_columns(lyb),)
    leaf_inverse = (inverse_low, inverse_high)

    def leaf_update(*refs):
        x_refs, refs = refs[: len(lyb)], refs[len(lyb) :]
        plan_ref, w_ref, *inverse_refs, rhs_ref, own_ref, other_ref, root_ref = refs[:-4]
        refs = refs[-4:]
        x_ref, update_ref, acc_ref, sum_ref = refs
        acc_ref[...] = jnp.zeros(acc_ref.shape, F32)
        for s in range(leaves):
            update_ref[s] = times_transposed(join_in(x_refs, x_ref, s), w_ref[s])
        scatter_walk(plan_ref, inverse_refs, update_ref, acc_ref, leaf_local // LANES)
        for b in range(parent_width // LANES):
            sum_ref[:, b * LANES : (b + 1) * LANES] = -acc_ref[b]
        sum_ref[:, spot(lax.axis_index("rows"), parent_cols)] += rhs_ref[:, 0, :]
        deal(sum_ref, own_ref, other_ref)
        for b in range(root_width // LANES):
            root_ref[b] = acc_ref[parent_width // LANES + b]

    own, other, root_acc = call(
        leaf_update,
        [
            ((chips, rcount, parent_cols), F32),
            ((chips, rcount, parent_cols), BF16),
            ((root_width // LANES, rcount, LANES), F32),
        ],
        [*lyb, leaf_plan, pinned(leaf_panel), *leaf_inverse, parent_rhs],
        [VMEM] * len(lyb) + [SMEM] + [VMEM] * 4,
        scratch=[
            pltpu.VMEM((rcount, leaf_width), BF16),
            pltpu.VMEM((leaves, rcount, leaf_local), F32),
            pltpu.VMEM((tall // LANES + 1, rcount, LANES), F32),
            pltpu.VMEM((rcount, parent_width), F32),
        ],
        name="leaf_update",
    )
    prb = chips_sum(own + swap(other).astype(F32)).astype(BF16)

    def parent_solve(own_ref, other_ref, w_ref, y_ref, send_ref, x_ref):
        unite(own_ref, other_ref, x_ref)
        y = times_transposed(x_ref[...], w_ref[0])
        y_ref[...] = y
        send_ref[...] = y.astype(BF16)

    py, pyb = call(
        parent_solve,
        [((rcount, parent_cols), F32), ((rcount, parent_cols), BF16)],
        [prb, swap(prb), pinned(parent_inv)],
        [VMEM] * 3,
        scratch=[pltpu.VMEM((rcount, parent_width), BF16)],
        name="parent_solve",
    )
    parent_list, parent_plan, parent_inverse = prepare(
        pyb, parent_rows, parent_local, parent_height, root_width, (0, 1)
    )
    pyb, parent_inverse = lax.optimization_barrier((far_gather(pyb), parent_inverse))

    def parent_update(
        plan_ref, x_own_ref, x_other_ref, w_ref, inverse_ref, root_ref, rhs_ref, own_ref, other_ref,
        x_ref, update_ref, acc_ref, sum_ref,
    ):
        unite(x_own_ref, x_other_ref, x_ref, xor=True)
        for b in range(root_width // LANES):
            acc_ref[b] = root_ref[b]
        update_ref[0] = times_transposed(x_ref[...], w_ref[0])
        scatter_walk(plan_ref, [inverse_ref], update_ref, acc_ref, parent_local // LANES)
        for b in range(root_width // LANES):
            sum_ref[:, b * LANES : (b + 1) * LANES] = -acc_ref[b]
        if root_aligned:
            sum_ref[:, spot(flat(), root_cols)] += rhs_ref[...]
        else:
            sum_ref[...] += rhs_ref[...]
        deal(sum_ref, own_ref, other_ref)

    own, other = call(
        parent_update,
        [((chips, rcount, piece), F32), ((chips, rcount, piece), BF16)],
        [parent_plan, pyb, swap(pyb), pinned(parent_panel), parent_inverse, root_acc, rhs],
        [SMEM] + [VMEM] * 6,
        scratch=[
            pltpu.VMEM((rcount, parent_width), BF16),
            pltpu.VMEM((1, rcount, parent_local), F32),
            pltpu.VMEM((root_width // LANES + 1, rcount, LANES), F32),
            pltpu.VMEM((rcount, root_width), F32),
        ],
        name="parent_update",
    )
    rrb = chips_sum(leaf_sum(own + swap(other).astype(F32))).astype(BF16)

    def root_solve(own_ref, other_ref, w_ref, own_out, other_out, x_ref, sum_ref):
        unite(own_ref, other_ref, x_ref)
        y = times_transposed(x_ref[...], w_ref[...]).astype(BF16)
        sum_ref[...] = times(y, w_ref[...])
        deal(sum_ref, own_out, other_out)

    own, other = call(
        root_solve,
        [((chips, rcount, piece), F32), ((chips, rcount, piece), BF16)],
        [rrb, swap(rrb), pinned(root_inv)],
        [VMEM] * 3,
        scratch=[pltpu.VMEM((rcount, root_width), BF16), pltpu.VMEM((rcount, root_width), F32)],
        name="root_solve",
    )
    rxb = chips_sum(own + swap(other).astype(F32)).astype(BF16)

    def blocks_of(source_ref, target_ref, start, width):
        for b in range(width // LANES):
            target_ref[start + b] = source_ref[:, b * LANES : (b + 1) * LANES].astype(F32)

    def terms(x_ref, w_ref, out_ref, odd):
        _, sets, _, cols = out_ref.shape
        for k in range(chips):
            at = spot(2 * (chip() ^ k) + odd, cols)
            for s in range(sets):
                out_ref[k, s] = times(x_ref[s], w_ref[s, :, at]).astype(out_ref.dtype)

    def split_terms(w):
        return (chips, w.shape[0], rcount, w.shape[2] // n)

    def own_terms(x, w, name):
        def body(x_ref, w_ref, out_ref):
            terms(x_ref, w_ref, out_ref, core())

        return call(
            body, [(split_terms(w), F32)], [x, pinned(w)], [VMEM] * 2, moved=12 << 20, name=name
        )[0]

    def reduce(own, other):
        other = swap(other)
        sums = [own[k] + other[k].astype(F32) for k in range(chips)]
        return [sums[0]] + from_chips(lambda k: sums[k].astype(BF16))

    def parent_back(
        plan_ref, own_ref, other_ref, rows_ref, w_ref, out_ref, whole_ref, sol_ref, found_ref, x_ref,
    ):
        unite(own_ref, other_ref, x_ref)
        if root_aligned:
            sol_ref[...] = x_ref[:, spot(flat(), root_cols)].astype(F32)
        else:
            sol_ref[...] = x_ref[...].astype(F32)
        blocks_of(x_ref, whole_ref, 0, root_width)
        whole_ref[root_width // LANES] = jnp.zeros((rcount, LANES), F32)
        gather_walk(plan_ref, rows_ref, whole_ref, found_ref)
        terms(found_ref, w_ref, out_ref, 1 - core())

    term, root_whole, root_sol, found = call(
        parent_back,
        [
            (split_terms(parent_panel), BF16),
            ((root_width // LANES + 1, rcount, LANES), F32),
            ((rcount, root_cols if root_aligned else root_width), F32),
            ((1, rcount, parent_local), BF16),
        ],
        [parent_plan, rxb, swap(rxb), parent_list, pinned(parent_panel)],
        [SMEM] + [VMEM] * 4,
        scratch=[pltpu.VMEM((rcount, root_width), BF16)],
        name="parent_back",
    )
    tails = reduce(own_terms(found, parent_panel, "parent_back_own"), term)

    def parent_solve_back(*refs):
        tail_refs, (y_ref, w_ref, own_ref, other_ref, sum_ref) = refs[:chips], refs[chips:]
        lost = sum(ref[0].astype(F32) for ref in tail_refs)
        sum_ref[...] = times((y_ref[...] - lost).astype(BF16), w_ref[0])
        deal(sum_ref, own_ref, other_ref)

    own, other = call(
        parent_solve_back,
        [((chips, rcount, parent_cols), F32), ((chips, rcount, parent_cols), BF16)],
        [*tails, py, pinned(parent_inv)],
        [VMEM] * (chips + 2),
        scratch=[pltpu.VMEM((rcount, parent_width), F32)],
        name="parent_solve_back",
    )
    px = chips_sum(own + swap(other).astype(F32))
    pxb = px.astype(BF16)

    def ancestors(
        plan_ref, px_ref, own_ref, other_ref, root_ref, rows_ref, sol_ref,
        x_ref, whole_ref, found_ref,
    ):
        sol_ref[...] = px_ref[chip()]
        unite(own_ref, other_ref, x_ref)
        blocks_of(x_ref, whole_ref, 0, parent_width)
        for b in range(root_width // LANES + 1):
            whole_ref[parent_width // LANES + b] = root_ref[b]
        gather_walk(plan_ref, rows_ref, whole_ref, found_ref)

    def all_terms(x_ref, w_ref, out_ref):
        for s in range(leaves):
            out_ref[s] = times(x_ref[s], w_ref[s]).astype(BF16)

    def pieces_apart(term):
        return jnp.moveaxis(term.reshape(leaves, rcount, n, leaf_cols), 2, 0)

    whole_term = (leaves, rcount, leaf_width)
    found_shape = (leaves, rcount, leaf_local)
    scratch = [
        pltpu.VMEM((rcount, parent_width), BF16),
        pltpu.VMEM((tall // LANES + 1, rcount, LANES), F32),
    ]

    def leaf_back(*refs):
        ins, (w_ref, out_ref, sol_ref, found_ref, x_ref, whole_ref) = refs[:6], refs[6:]
        ancestors(*ins, sol_ref, x_ref, whole_ref, found_ref)
        if leaf_aligned:
            terms(found_ref, w_ref, out_ref, 1 - core())
        else:
            all_terms(found_ref, w_ref, out_ref)

    term, parent_sol, found = call(
        leaf_back,
        [
            (split_terms(leaf_panel) if leaf_aligned else whole_term, BF16),
            ((rcount, parent_cols), F32),
            (found_shape, BF16),
        ],
        [leaf_plan, px, pxb, swap(pxb), root_whole, leaf_list, pinned(leaf_panel)],
        [SMEM] + [VMEM] * 6,
        scratch=scratch,
        name="leaf_back",
    )
    if leaf_aligned:
        tails = reduce(own_terms(found, leaf_panel, "leaf_back_own"), term)
    else:
        tails = [all_to_all(pieces_apart(term)).astype(F32).sum(0)]

    def leaf_solve_back(*refs):
        tail_refs, (y_ref, w_ref, out_ref, v_ref) = refs[: len(tails)], refs[len(tails) :]
        for s in range(leaves):
            lost = sum(ref[s].astype(F32) for ref in tail_refs)
            v_ref[s] = (y_ref[s] - lost).astype(BF16)
        if leaf_aligned:
            terms(v_ref, w_ref, out_ref, 1 - core())
        else:
            all_terms(v_ref, w_ref, out_ref)

    term, lvb = call(
        leaf_solve_back,
        [
            (split_terms(leaf_panel) if leaf_aligned else whole_term, BF16),
            ((leaves, rcount, leaf_cols), BF16),
        ],
        [*tails, ly, pinned(leaf_inv)],
        [VMEM] * (len(tails) + 2),
        name="leaf_solve_back",
    )
    if leaf_aligned:
        parts = reduce(own_terms(lvb, leaf_inv, "leaf_solve_back_own"), term)
        leaf_sol = sum(p.astype(F32) for p in parts)
    else:
        leaf_sol = all_to_all(pieces_apart(term)).astype(F32).sum(0)
    if not root_aligned:
        root_sol = lax.dynamic_slice_in_dim(root_sol, flat() * root_cols, root_cols, 1)
    return (jnp.moveaxis(leaf_sol, 0, 1), parent_sol[:, None, :], root_sol)


def solution(mesh):
    return jax.shard_map(
        shards,
        mesh=mesh,
        in_specs=(
            P(None, "leaf", "rows"),
            P(None, "leaf", "rows"),
            P(None, ("leaf", "rows")),
            P("leaf", "rows", None),
            P("leaf", "rows", None),
            P("leaf", "rows"),
            P("leaf"),
            P("leaf", "rows", None),
            P("leaf", "rows", None),
            P("leaf", "rows"),
            P("leaf"),
            P("rows", None),
        ),
        out_specs=(P(None, "leaf", "rows"), P(None, "leaf", "rows"), P(None, ("leaf", "rows"))),
        check_vma=False,
    )
```

```python
import jax
import jax.numpy as jnp
from jax import lax
from jax.experimental import pallas as pl
from jax.experimental.pallas import tpu as pltpu
from jax.sharding import PartitionSpec as P

F32 = jnp.float32
BF16 = jnp.bfloat16
I32 = jnp.int32
LANES = 128
UNROLL = 4

VMEM = pl.BlockSpec(memory_space=pltpu.VMEM)
SMEM = pl.BlockSpec(memory_space=pltpu.SMEM)


def pinned(w):
    return pltpu.with_memory_space_constraint(w, pltpu.VMEM)


def outside(w):
    return pltpu.with_memory_space_constraint(w, pltpu.HBM)


def call(
    body, outs, ins, specs, out_specs=None, scratch=(), moved=0, limit=6 << 20, name=None
):
    return pl.pallas_call(
        body,
        out_shape=[jax.ShapeDtypeStruct(*o) if isinstance(o, tuple) else o for o in outs],
        in_specs=list(specs),
        out_specs=out_specs or [VMEM] * len(outs),
        scratch_shapes=list(scratch),
        cost_estimate=pl.CostEstimate(flops=0, bytes_accessed=moved, transcendentals=0),
        compiler_params=pltpu.CompilerParams(vmem_limit_bytes=limit),
        name=name,
    )(*ins)


def times_transposed(x, w):
    return lax.dot_general(x, w, (((1,), (1,)), ((), ())), preferred_element_type=F32)


def times(x, w):
    return lax.dot_general(x, w, (((1,), (0,)), ((), ())), preferred_element_type=F32)


def walk(plan_ref, sets, tiles, blocks, tile, visit, carry):
    def trip(i, carry):
        at = []
        for s in range(sets):
            lo = plan_ref[s * tiles + tile] + i * UNROLL
            at += [(s, jnp.minimum(lo + u, blocks)) for u in range(UNROLL)]
        return visit(at, carry)

    return lax.fori_loop(0, plan_ref[sets * tiles + tile], trip, carry)


def pick(x, index):
    inside = (index >= 0) & (index < LANES)
    found = jnp.take_along_axis(
        x, index & (LANES - 1), axis=1, mode="promise_in_bounds"
    )
    return jnp.where(inside, found, 0.0)


def prepare(after, rows, first, height, width, sets):
    of = range(*sets)
    sets, length = rows.shape
    tiles, blocks = length // LANES, width // LANES

    def body(after_ref, rows_ref, height_ref, list_ref, plan_ref, out_ref, scalar_ref, sem):
        copy = pltpu.make_async_copy(rows_ref, scalar_ref, sem)
        copy.start()
        out_ref[...] = jnp.full(out_ref.shape, -1, I32)
        start = lax.axis_index("rows") * first
        used = [height_ref[s] - start for s in range(sets)]
        copy.wait()
        lane = lax.broadcasted_iota(I32, (1, LANES), 1)
        for tile in range(tiles):
            lanes = slice(tile * LANES, (tile + 1) * LANES)
            spots = lax.broadcasted_iota(I32, (LANES, LANES), 0) + (tile * LANES + 1)
            cols, trips = [], 0
            for s in range(sets):
                line = jnp.where(lane + tile * LANES < used[s], rows_ref[s : s + 1, lanes], -1)
                list_ref[s : s + 1, lanes] = line
                if s in of:
                    cols.append(jnp.transpose(jnp.broadcast_to(line, (LANES, LANES))))
                end = jnp.maximum(jnp.minimum(used[s], (tile + 1) * LANES) - 1, 0)
                lo = lax.shift_right_logical(scalar_ref[s, tile * LANES], 7)
                hi = lax.shift_right_logical(scalar_ref[s, end], 7)
                met = used[s] > tile * LANES
                plan_ref[s * tiles + tile] = jnp.where(met, lo, blocks)
                span = jnp.where(met, hi - lo + UNROLL, 0)
                trips = jnp.maximum(trips, lax.div(span, UNROLL))
            plan_ref[sets * tiles + tile] = trips

            def visit(at, carry):
                across = lax.broadcasted_iota(I32, (LANES, LANES), 1)
                got = []
                at = [(s - of.start, block) for s, block in at if s in of]
                for s, block in at:
                    hit = cols[s] == across + block * LANES
                    got.append(jnp.sum(jnp.where(hit, spots, 0), axis=0, keepdims=True))
                for (s, block), g in zip(at, got):
                    out_ref[s, block] += jnp.broadcast_to(g, out_ref.shape[2:])
                return carry

            walk(plan_ref, sets, tiles, blocks, tile, visit, 0)

    return call(
        body,
        [
            (rows.shape, I32),
            (((sets + 1) * tiles,), I32),
            ((len(of), blocks + 1, 8, LANES), I32),
        ],
        [after, rows, height],
        [pl.BlockSpec(memory_space=pl.ANY), VMEM, SMEM],
        out_specs=[VMEM, SMEM, VMEM],
        scratch=[
            pltpu.SMEM(rows.shape, I32),
            pltpu.SemaphoreType.DMA(()),
        ],
        moved=8 << 20,
        limit=4 << 20,
        name="prepare",
    )


def scatter_walk(plan_ref, inverse_refs, update_ref, acc_ref, tiles):
    sets, blocks = update_ref.shape[0], inverse_refs[0].shape[1] - 1
    inverse = [ref.at[s] for ref in inverse_refs for s in range(ref.shape[0])]
    for tile in range(tiles):

        def visit(at, carry):
            got = []
            for s, block in at:
                x = update_ref[s, :, tile * LANES : (tile + 1) * LANES]
                got.append(pick(x, inverse[s][block] - tile * LANES))
            for (s, block), g in zip(at, got):
                acc_ref[block] += g
            return carry

        walk(plan_ref, sets, tiles, blocks, tile, visit, 0)


def gather_walk(plan_ref, rows_ref, source_ref, out_ref):
    sets, length = rows_ref.shape
    tiles, blocks = length // LANES, source_ref.shape[0] - 1
    for tile in range(tiles):
        index = [
            jnp.broadcast_to(
                rows_ref[s : s + 1, tile * LANES : (tile + 1) * LANES], (8, LANES)
            )
            for s in range(sets)
        ]

        def visit(at, carry):
            carry = list(carry)
            for s, block in at:
                carry[s] = carry[s] + pick(source_ref[block], index[s] - block * LANES)
            return tuple(carry)

        zero = tuple(jnp.zeros((8, LANES), F32) for _ in range(sets))
        found = walk(plan_ref, sets, tiles, blocks, tile, visit, zero)
        for s in range(sets):
            out_ref[s, :, tile * LANES : (tile + 1) * LANES] = found[s].astype(out_ref.dtype)


def core():
    return lax.axis_index("rows") & 1


def chip():
    return lax.axis_index("rows") // 2


def spot(r, w):
    return pl.ds(pl.multiple_of(r * w, LANES), w)


def unite(own_ref, other_ref, out_ref, *at, xor=False):
    odd, w = core(), own_ref.shape[-1]
    for k in range(own_ref.shape[0]):
        c = chip() ^ (-k % own_ref.shape[0]) if xor else k
        out_ref[:, spot(2 * c + odd, w)] = own_ref[(k,) + at]
        out_ref[:, spot(2 * c + 1 - odd, w)] = other_ref[(k,) + at]


def deal(value_ref, own_ref, other_ref):
    odd = core()
    chips, _, w = own_ref.shape
    for k in range(chips):
        own_ref[k] = value_ref[:, spot(2 * k + odd, w)].astype(own_ref.dtype)
        other_ref[k] = value_ref[:, spot(2 * k + 1 - odd, w)].astype(other_ref.dtype)


def half_of(x_ref, w_ref, s, odd, xor):
    at = (s,) if len(x_ref.shape) == 4 else ()
    chips, cols = x_ref.shape[0], x_ref.shape[-1]
    terms = []
    for k in range(chips):
        c = chip() ^ (-k % chips) if xor else k
        terms.append(times_transposed(x_ref[(k,) + at], w_ref[s, :, spot(2 * c + odd, cols)]))
    return sum(terms[1:], terms[0])


def own_half(x, w, name, xor=False):
    sets, rows = w.shape[:2]

    def body(x_ref, w_ref, out_ref):
        for s in range(sets):
            out_ref[s] = half_of(x_ref, w_ref, s, core(), xor)

    return call(
        body,
        [((sets, x.shape[-2], rows), F32)],
        [x, pinned(w)],
        [VMEM] * 2,
        moved=12 << 20,
        name=name,
    )[0]


def both_halves(part_ref, x_ref, w_ref, s, xor=False):
    return part_ref[s] + half_of(x_ref, w_ref, s, 1 - core(), xor)


def all_to_all(x):
    return lax.all_to_all(x, "rows", 0, 0)


def swap(x):
    n = lax.axis_size("rows")
    return lax.ppermute(x, "rows", [(i, i ^ 1) for i in range(n)])


def far(x, k):
    n = lax.axis_size("rows")
    return lax.ppermute(x, "rows", [(i, i ^ (2 * k)) for i in range(n)])


def from_chips(piece):
    chips = lax.axis_size("rows") // 2
    return [far(piece(k), k) for k in range(chips - 1, 0, -1)]


def chips_sum(x):
    b = x.astype(BF16)
    return x + sum(got.astype(F32) for got in from_chips(lambda k: b))


def leaf_sum(x):
    n = lax.axis_size("leaf")
    b = x.astype(BF16)
    for k in range(1, n):
        x = x + lax.ppermute(b, "leaf", [(i, (i + k) % n) for i in range(n)]).astype(F32)
    return x


def shards(
    leaf_rhs,
    parent_rhs,
    root_rhs,
    leaf_inv,
    leaf_panel,
    leaf_rows,
    leaf_height,
    parent_inv,
    parent_panel,
    parent_rows,
    parent_height,
    root_inv,
):
    n = lax.axis_size("rows")
    chips = n // 2
    rcount, leaves, leaf_cols = leaf_rhs.shape
    leaf_local, leaf_width = leaf_panel.shape[1:]
    parent_cols, parent_width = parent_inv.shape[1:]
    parent_local = parent_panel.shape[1]
    root_width = root_inv.shape[1]
    root_inv = root_inv[None]
    root_local = root_inv.shape[1]
    root_cols = root_rhs.shape[1]
    piece = root_width // n
    tall = parent_width + root_width
    leaf_aligned = leaf_cols % LANES == 0
    root_aligned = root_cols % LANES == 0

    def flat():
        return lax.axis_index("leaf") * n + lax.axis_index("rows")

    def far_gather(x):
        return jnp.stack([x] + from_chips(lambda k: x))

    def leaf_columns(x):
        got = all_to_all(jnp.broadcast_to(x[None], (n,) + x.shape))
        return jnp.moveaxis(got, 0, 2).reshape(1, leaves, rcount, leaf_width)

    def leaf_product(x_refs, w_ref, s):
        if leaf_aligned:
            return both_halves(*x_refs, w_ref, s, xor=True)
        return times_transposed(x_refs[0][0, s], w_ref[s])

    def leaf_halves(x, w, name):
        return own_half(x, w, name, xor=True), swap(x)

    rhs = root_rhs
    if not root_aligned:
        rhs = lax.dynamic_update_slice_in_dim(
            jnp.zeros((rcount, root_width), F32), root_rhs, flat() * root_cols, 1
        )
    weights = (leaf_inv, leaf_panel, parent_inv, parent_panel, root_inv, leaf_rows, parent_rows)

    def round_rhs(x_ref, *refs):
        out_ref = refs[-1]
        for s in range(leaves):
            out_ref[s] = x_ref[:, s, :].astype(BF16)

    lb = call(
        round_rhs,
        [((leaves, rcount, leaf_cols), BF16)],
        [leaf_rhs] + [outside(w) for w in weights],
        [VMEM] + [pl.BlockSpec(memory_space=pltpu.HBM)] * len(weights),
        name="round_rhs",
    )[0]
    half = leaves // 2

    def prepare_leaves(after, *sets):
        return prepare(after, leaf_rows, leaf_local, leaf_height, tall, sets)

    leaf_list, leaf_plan, inverse_low = prepare_leaves(lb, 0, half)
    lb = far_gather(lb) if leaf_aligned else leaf_columns(lb)
    lb, inverse_low, rhs = lax.optimization_barrier((lb, inverse_low, rhs))
    lb = leaf_halves(lb, leaf_inv, "leaf_solve_own") if leaf_aligned else (lb,)

    def leaf_solve(*refs):
        x_refs, (w_ref, y_ref, send_ref) = refs[: len(lb)], refs[len(lb) :]
        for s in range(leaves):
            y = leaf_product(x_refs, w_ref, s)
            y_ref[s] = y
            send_ref[s] = y.astype(BF16)

    ly, lyb = call(
        leaf_solve,
        [((leaves, rcount, leaf_cols), F32), ((leaves, rcount, leaf_cols), BF16)],
        [*lb, pinned(leaf_inv)],
        [VMEM] * (len(lb) + 1),
        name="leaf_solve",
    )
    inverse_high = prepare_leaves(lyb, half, leaves)[2]
    if leaf_aligned:
        lyb, inverse_high = lax.optimization_barrier((far_gather(lyb), inverse_high))
        lyb = leaf_halves(lyb, leaf_panel, "leaf_update_own")
    else:
        lyb = (leaf_columns(lyb),)
    leaf_inverse = (inverse_low, inverse_high)

    def leaf_update(*refs):
        x_refs, refs = refs[: len(lyb)], refs[len(lyb) :]
        plan_ref, w_ref, *inverse_refs, rhs_ref, own_ref, other_ref, root_ref = refs[:-3]
        update_ref, acc_ref, sum_ref = refs[-3:]
        acc_ref[...] = jnp.zeros(acc_ref.shape, F32)
        for s in range(leaves):
            update_ref[s] = leaf_product(x_refs, w_ref, s)
        scatter_walk(plan_ref, inverse_refs, update_ref, acc_ref, leaf_local // LANES)
        for b in range(parent_width // LANES):
            sum_ref[:, b * LANES : (b + 1) * LANES] = -acc_ref[b]
        sum_ref[:, spot(lax.axis_index("rows"), parent_cols)] += rhs_ref[:, 0, :]
        deal(sum_ref, own_ref, other_ref)
        for b in range(root_width // LANES):
            root_ref[b] = acc_ref[parent_width // LANES + b]

    own, other, root_acc = call(
        leaf_update,
        [
            ((chips, rcount, parent_cols), F32),
            ((chips, rcount, parent_cols), BF16),
            ((root_width // LANES, rcount, LANES), F32),
        ],
        [*lyb, leaf_plan, pinned(leaf_panel), *leaf_inverse, parent_rhs],
        [VMEM] * len(lyb) + [SMEM] + [VMEM] * 4,
        scratch=[
            pltpu.VMEM((leaves, rcount, leaf_local), F32),
            pltpu.VMEM((tall // LANES + 1, rcount, LANES), F32),
            pltpu.VMEM((rcount, parent_width), F32),
        ],
        name="leaf_update",
    )
    prb = chips_sum(own + swap(other).astype(F32)).astype(BF16)

    def parent_solve(part_ref, x_ref, w_ref, y_ref, send_ref):
        y = both_halves(part_ref, x_ref, w_ref, 0)
        y_ref[...] = y
        send_ref[...] = y.astype(BF16)

    py, pyb = call(
        parent_solve,
        [((rcount, parent_cols), F32), ((rcount, parent_cols), BF16)],
        [own_half(prb, parent_inv, "parent_solve_own"), swap(prb), pinned(parent_inv)],
        [VMEM] * 3,
        name="parent_solve",
    )
    parent_list, parent_plan, parent_inverse = prepare(
        pyb, parent_rows, parent_local, parent_height, root_width, (0, 1)
    )
    pyb, parent_inverse = lax.optimization_barrier((far_gather(pyb), parent_inverse))

    def parent_update(
        plan_ref, part_ref, x_ref, w_ref, inverse_ref, root_ref, rhs_ref, own_ref, other_ref,
        update_ref, acc_ref, sum_ref,
    ):
        for b in range(root_width // LANES):
            acc_ref[b] = root_ref[b]
        update_ref[0] = both_halves(part_ref, x_ref, w_ref, 0, xor=True)
        scatter_walk(plan_ref, [inverse_ref], update_ref, acc_ref, parent_local // LANES)
        for b in range(root_width // LANES):
            sum_ref[:, b * LANES : (b + 1) * LANES] = -acc_ref[b]
        if root_aligned:
            sum_ref[:, spot(flat(), root_cols)] += rhs_ref[...]
        else:
            sum_ref[...] += rhs_ref[...]
        deal(sum_ref, own_ref, other_ref)

    own, other = call(
        parent_update,
        [((chips, rcount, piece), F32), ((chips, rcount, piece), BF16)],
        [
            parent_plan,
            own_half(pyb, parent_panel, "parent_update_own", xor=True),
            swap(pyb),
            pinned(parent_panel),
            parent_inverse,
            root_acc,
            rhs,
        ],
        [SMEM] + [VMEM] * 6,
        scratch=[
            pltpu.VMEM((1, rcount, parent_local), F32),
            pltpu.VMEM((root_width // LANES + 1, rcount, LANES), F32),
            pltpu.VMEM((rcount, root_width), F32),
        ],
        name="parent_update",
    )
    rrb = chips_sum(leaf_sum(own + swap(other).astype(F32))).astype(BF16)

    def terms(x_ref, w_ref, out_ref, odd, xor=True):
        _, sets, _, cols = out_ref.shape
        for k in range(chips):
            at = spot(2 * (chip() ^ k if xor else k) + odd, cols)
            for s in range(sets):
                out_ref[k, s] = times(x_ref[s], w_ref[s, :, at]).astype(out_ref.dtype)

    def split_terms(w):
        return (chips, w.shape[0], rcount, w.shape[2] // n)

    def own_terms(x, w, name, xor=True):
        def body(x_ref, w_ref, out_ref):
            terms(x_ref, w_ref, out_ref, core(), xor)

        return call(
            body, [(split_terms(w), F32)], [x, pinned(w)], [VMEM] * 2, moved=12 << 20, name=name
        )[0]

    def total(x, w, other, name):
        own = own_terms(x, w, name, xor=False)
        return chips_sum((own + swap(other).astype(F32))[:, 0])

    def root_solve(part_ref, x_ref, w_ref, out_ref, y_ref):
        y_ref[0] = both_halves(part_ref, x_ref, w_ref, 0).astype(BF16)
        terms(y_ref, w_ref, out_ref, 1 - core(), xor=False)

    term, ryb = call(
        root_solve,
        [(split_terms(root_inv), BF16), ((1, rcount, root_local), BF16)],
        [own_half(rrb, root_inv, "root_solve_own"), swap(rrb), pinned(root_inv)],
        [VMEM] * 3,
        name="root_solve",
    )
    rxb = total(ryb, root_inv, term, "root_solve_back_own").astype(BF16)

    def blocks_of(source_ref, target_ref, start, width):
        for b in range(width // LANES):
            target_ref[start + b] = source_ref[:, b * LANES : (b + 1) * LANES].astype(F32)

    def reduce(own, other):
        other = swap(other)
        sums = [own[k] + other[k].astype(F32) for k in range(chips)]
        return [sums[0]] + from_chips(lambda k: sums[k].astype(BF16))

    def parent_back(
        plan_ref, own_ref, other_ref, rows_ref, w_ref, out_ref, whole_ref, sol_ref, found_ref, x_ref,
    ):
        unite(own_ref, other_ref, x_ref)
        if root_aligned:
            sol_ref[...] = x_ref[:, spot(flat(), root_cols)].astype(F32)
        else:
            sol_ref[...] = x_ref[...].astype(F32)
        blocks_of(x_ref, whole_ref, 0, root_width)
        whole_ref[root_width // LANES] = jnp.zeros((rcount, LANES), F32)
        gather_walk(plan_ref, rows_ref, whole_ref, found_ref)
        terms(found_ref, w_ref, out_ref, 1 - core())

    term, root_whole, root_sol, found = call(
        parent_back,
        [
            (split_terms(parent_panel), BF16),
            ((root_width // LANES + 1, rcount, LANES), F32),
            ((rcount, root_cols if root_aligned else root_width), F32),
            ((1, rcount, parent_local), BF16),
        ],
        [parent_plan, rxb, swap(rxb), parent_list, pinned(parent_panel)],
        [SMEM] + [VMEM] * 4,
        scratch=[pltpu.VMEM((rcount, root_width), BF16)],
        name="parent_back",
    )
    tails = reduce(own_terms(found, parent_panel, "parent_back_own"), term)

    def parent_solve_back(*refs):
        tail_refs, (y_ref, w_ref, out_ref, v_ref) = refs[:chips], refs[chips:]
        lost = sum(ref[0].astype(F32) for ref in tail_refs)
        v_ref[0] = (y_ref[...] - lost).astype(BF16)
        terms(v_ref, w_ref, out_ref, 1 - core(), xor=False)

    term, pvb = call(
        parent_solve_back,
        [(split_terms(parent_inv), BF16), ((1, rcount, parent_cols), BF16)],
        [*tails, py, pinned(parent_inv)],
        [VMEM] * (chips + 2),
        name="parent_solve_back",
    )
    px = total(pvb, parent_inv, term, "parent_solve_back_own")
    pxb = px.astype(BF16)

    def ancestors(
        plan_ref, px_ref, own_ref, other_ref, root_ref, rows_ref, sol_ref,
        x_ref, whole_ref, found_ref,
    ):
        sol_ref[...] = px_ref[chip()]
        unite(own_ref, other_ref, x_ref)
        blocks_of(x_ref, whole_ref, 0, parent_width)
        for b in range(root_width // LANES + 1):
            whole_ref[parent_width // LANES + b] = root_ref[b]
        gather_walk(plan_ref, rows_ref, whole_ref, found_ref)

    def all_terms(x_ref, w_ref, out_ref):
        for s in range(leaves):
            out_ref[s] = times(x_ref[s], w_ref[s]).astype(BF16)

    def pieces_apart(term):
        return jnp.moveaxis(term.reshape(leaves, rcount, n, leaf_cols), 2, 0)

    whole_term = (leaves, rcount, leaf_width)
    found_shape = (leaves, rcount, leaf_local)
    scratch = [
        pltpu.VMEM((rcount, parent_width), BF16),
        pltpu.VMEM((tall // LANES + 1, rcount, LANES), F32),
    ]

    def leaf_back(*refs):
        ins, (w_ref, out_ref, sol_ref, found_ref, x_ref, whole_ref) = refs[:6], refs[6:]
        ancestors(*ins, sol_ref, x_ref, whole_ref, found_ref)
        if leaf_aligned:
            terms(found_ref, w_ref, out_ref, 1 - core())
        else:
            all_terms(found_ref, w_ref, out_ref)

    term, parent_sol, found = call(
        leaf_back,
        [
            (split_terms(leaf_panel) if leaf_aligned else whole_term, BF16),
            ((rcount, parent_cols), F32),
            (found_shape, BF16),
        ],
        [leaf_plan, px, pxb, swap(pxb), root_whole, leaf_list, pinned(leaf_panel)],
        [SMEM] + [VMEM] * 6,
        scratch=scratch,
        name="leaf_back",
    )
    if leaf_aligned:
        tails = reduce(own_terms(found, leaf_panel, "leaf_back_own"), term)
    else:
        tails = [all_to_all(pieces_apart(term)).astype(F32).sum(0)]

    def leaf_solve_back(*refs):
        tail_refs, (y_ref, w_ref, out_ref, v_ref) = refs[: len(tails)], refs[len(tails) :]
        for s in range(leaves):
            lost = sum(ref[s].astype(F32) for ref in tail_refs)
            v_ref[s] = (y_ref[s] - lost).astype(BF16)
        if leaf_aligned:
            terms(v_ref, w_ref, out_ref, 1 - core())
        else:
            all_terms(v_ref, w_ref, out_ref)

    term, lvb = call(
        leaf_solve_back,
        [
            (split_terms(leaf_panel) if leaf_aligned else whole_term, BF16),
            ((leaves, rcount, leaf_cols), BF16),
        ],
        [*tails, ly, pinned(leaf_inv)],
        [VMEM] * (len(tails) + 2),
        name="leaf_solve_back",
    )
    if leaf_aligned:
        parts = reduce(own_terms(lvb, leaf_inv, "leaf_solve_back_own"), term)
        leaf_sol = sum(p.astype(F32) for p in parts)
    else:
        leaf_sol = all_to_all(pieces_apart(term)).astype(F32).sum(0)
    if not root_aligned:
        root_sol = lax.dynamic_slice_in_dim(root_sol, flat() * root_cols, root_cols, 1)
    return (jnp.moveaxis(leaf_sol, 0, 1), parent_sol[:, None, :], root_sol)


def solution(mesh):
    return jax.shard_map(
        shards,
        mesh=mesh,
        in_specs=(
            P(None, "leaf", "rows"),
            P(None, "leaf", "rows"),
            P(None, ("leaf", "rows")),
            P("leaf", "rows", None),
            P("leaf", "rows", None),
            P("leaf", "rows"),
            P("leaf"),
            P("leaf", "rows", None),
            P("leaf", "rows", None),
            P("leaf", "rows"),
            P("leaf"),
            P("rows", None),
        ),
        out_specs=(P(None, "leaf", "rows"), P(None, "leaf", "rows"), P(None, ("leaf", "rows"))),
        check_vma=False,
    )
```

```python
import jax
import jax.numpy as jnp
from jax import lax
from jax.experimental import pallas as pl
from jax.experimental.pallas import tpu as pltpu
from jax.sharding import PartitionSpec as P

F32 = jnp.float32
BF16 = jnp.bfloat16
I32 = jnp.int32
LANES = 128
BLOCKS = 8
NONE = 1 << 24

VMEM = pl.BlockSpec(memory_space=pltpu.VMEM)
SMEM = pl.BlockSpec(memory_space=pltpu.SMEM)


def pinned(w):
    return pltpu.with_memory_space_constraint(w, pltpu.VMEM)


def outside(w):
    return pltpu.with_memory_space_constraint(w, pltpu.HBM)


def call(
    body, outs, ins, specs, out_specs=None, scratch=(), moved=0, limit=6 << 20, name=None
):
    return pl.pallas_call(
        body,
        out_shape=[jax.ShapeDtypeStruct(*o) if isinstance(o, tuple) else o for o in outs],
        in_specs=list(specs),
        out_specs=out_specs or [VMEM] * len(outs),
        scratch_shapes=list(scratch),
        cost_estimate=pl.CostEstimate(flops=0, bytes_accessed=moved, transcendentals=0),
        compiler_params=pltpu.CompilerParams(vmem_limit_bytes=limit),
        name=name,
    )(*ins)


def times_transposed(x, w):
    return lax.dot_general(x, w, (((1,), (1,)), ((), ())), preferred_element_type=F32)


def times(x, w):
    return lax.dot_general(x, w, (((1,), (0,)), ((), ())), preferred_element_type=F32)


def prepare(after, lists):
    count = len(lists)

    def one(first, rows_ref, height_ref, list_ref, plan_ref, scalar_ref):
        sets, length = rows_ref.shape
        tiles = length // LANES
        start = lax.axis_index("rows") * first
        lane = lax.broadcasted_iota(I32, (1, LANES), 1)
        rounds = 0
        for s in range(sets):
            used = height_ref[s] - start
            for tile in range(tiles):
                lanes = slice(tile * LANES, (tile + 1) * LANES)
                line = rows_ref[s : s + 1, lanes]
                list_ref[s : s + 1, lanes] = jnp.where(lane + tile * LANES < used, line, NONE)
                end = jnp.maximum(jnp.minimum(used, (tile + 1) * LANES) - 1, 0)
                lo = lax.shift_right_logical(scalar_ref[s, tile * LANES], 7)
                hi = lax.shift_right_logical(scalar_ref[s, end], 7)
                met = used > tile * LANES
                plan_ref[s * tiles + tile] = jnp.where(met, lo, 0)
                span = jnp.where(met, hi - lo + BLOCKS, 0)
                rounds = jnp.maximum(rounds, lax.shift_right_logical(span, 3))
        plan_ref[sets * tiles] = rounds

    def body(*refs):
        ins, outs = refs[1 : 2 * count + 1], refs[2 * count + 1 : 4 * count + 1]
        scalars, sems = refs[4 * count + 1 : -1], refs[-1]
        copies = [
            pltpu.make_async_copy(ins[2 * i], scalars[i], sems.at[i]) for i in range(count)
        ]
        for copy in copies:
            copy.start()
        for i, copy in enumerate(copies):
            copy.wait()
            one(lists[i][1], *ins[2 * i : 2 * i + 2], *outs[2 * i : 2 * i + 2], scalars[i])

    shapes, ins = [], [after]
    for rows, _, height in lists:
        sets, length = rows.shape
        shapes += [(rows.shape, I32), ((sets * (length // LANES) + 1,), I32)]
        ins += [rows, height]
    return call(
        body,
        shapes,
        ins,
        [pl.BlockSpec(memory_space=pl.ANY)] + [VMEM, SMEM] * count,
        out_specs=[VMEM, SMEM] * count,
        scratch=[pltpu.SMEM(x[0].shape, I32) for x in lists] + [pltpu.SemaphoreType.DMA((count,))],
        moved=4 << 20,
        limit=4 << 20,
        name="prepare",
    )


def walk(plan_ref, list_ref, blocks, visit):
    sets, length = list_ref.shape
    tiles = length // LANES

    def take_round(i, first):
        for tile in range(tiles):
            lanes = slice(tile * LANES, (tile + 1) * LANES)
            for s in range(sets):
                line = jnp.broadcast_to(list_ref[s : s + 1, lanes], (BLOCKS, LANES))
                lo = jnp.minimum(plan_ref[s * tiles + tile] + i * BLOCKS, blocks)
                visit(s, lanes, line, lo, first)

    take_round(0, True)

    def again(i, carry):
        take_round(i, False)
        return carry

    lax.fori_loop(1, plan_ref[sets * tiles], again, 0)


def along(x, index):
    return jnp.take_along_axis(x, index, axis=1, mode="promise_in_bounds")


def pick(x, index):
    inside = (index >= 0) & (index < LANES)
    return jnp.where(inside, along(x, index & (LANES - 1)), 0.0)


def position(line, lo):
    block = lax.broadcasted_iota(I32, line.shape, 0) + lo
    target = block * LANES + lax.broadcasted_iota(I32, line.shape, 1)
    below = jnp.zeros(line.shape, I32)
    step = LANES // 2
    while step:
        below = jnp.where(along(line, below + (step - 1)) < target, below + step, below)
        step //= 2
    return jnp.where(along(line, below) == target, below, -1)


def scatter_walk(plan_ref, list_ref, update_ref, acc_ref):
    def visit(s, lanes, line, lo, first):
        x, at = update_ref[s, :, lanes], position(line, lo)
        parts = [pick(x, jnp.broadcast_to(at[u : u + 1], x.shape)) for u in range(BLOCKS)]
        acc_ref[pl.ds(lo, BLOCKS)] += jnp.stack(parts)

    walk(plan_ref, list_ref, acc_ref.shape[0] - BLOCKS, visit)


def gather_walk(plan_ref, list_ref, source_ref, out_ref):
    def visit(s, lanes, line, lo, first):
        x = source_ref[pl.ds(lo, BLOCKS)]
        parts = [pick(x[u], line - (lo + u) * LANES) for u in range(BLOCKS)]
        found = sum(parts[1:], parts[0]).astype(out_ref.dtype)
        out_ref[s, :, lanes] = found if first else out_ref[s, :, lanes] + found

    walk(plan_ref, list_ref, source_ref.shape[0] - BLOCKS, visit)


def core():
    return lax.axis_index("rows") & 1


def chip():
    return lax.axis_index("rows") // 2


def spot(r, w):
    return pl.ds(pl.multiple_of(r * w, LANES), w)


def unite(own_ref, other_ref, out_ref, *at, xor=False):
    odd, w = core(), own_ref.shape[-1]
    for k in range(own_ref.shape[0]):
        c = chip() ^ k if xor else k
        out_ref[:, spot(2 * c + odd, w)] = own_ref[(k,) + at]
        out_ref[:, spot(2 * c + 1 - odd, w)] = other_ref[(k,) + at]


def deal(value_ref, own_ref, other_ref):
    odd = core()
    chips, _, w = own_ref.shape
    for k in range(chips):
        own_ref[k] = value_ref[:, spot(2 * k + odd, w)].astype(own_ref.dtype)
        other_ref[k] = value_ref[:, spot(2 * k + 1 - odd, w)].astype(other_ref.dtype)


def half_of(x_ref, w_ref, s, odd, xor):
    at = (s,) if len(x_ref.shape) == 4 else ()
    chips, cols = x_ref.shape[0], x_ref.shape[-1]
    terms = []
    for k in range(chips):
        c = chip() ^ k if xor else k
        terms.append(times_transposed(x_ref[(k,) + at], w_ref[s, :, spot(2 * c + odd, cols)]))
    return sum(terms[1:], terms[0])


def own_half(x, w, name, xor=False):
    sets, rows = w.shape[:2]

    def body(x_ref, w_ref, out_ref):
        for s in range(sets):
            out_ref[s] = half_of(x_ref, w_ref, s, core(), xor)

    return call(
        body,
        [((sets, x.shape[-2], rows), F32)],
        [x, pinned(w)],
        [VMEM] * 2,
        moved=12 << 20,
        name=name,
    )[0]


def both_halves(part_ref, x_ref, w_ref, s, xor=False):
    return part_ref[s] + half_of(x_ref, w_ref, s, 1 - core(), xor)


def all_to_all(x):
    return lax.all_to_all(x, "rows", 0, 0)


def swap(x):
    n = lax.axis_size("rows")
    return lax.ppermute(x, "rows", [(i, i ^ 1) for i in range(n)])


def far(x, k):
    n = lax.axis_size("rows")
    return lax.ppermute(x, "rows", [(i, i ^ (2 * k)) for i in range(n)])


def from_chips(piece):
    return [far(piece(k), k) for k in range(1, lax.axis_size("rows") // 2)]


def chips_sum(x):
    b = x.astype(BF16)
    return x + sum(got.astype(F32) for got in from_chips(lambda k: b))


def leaf_sum(x):
    n = lax.axis_size("leaf")
    b = x.astype(BF16)
    for k in range(1, n):
        x = x + lax.ppermute(b, "leaf", [(i, (i + k) % n) for i in range(n)]).astype(F32)
    return x


def shards(
    leaf_rhs,
    parent_rhs,
    root_rhs,
    leaf_inv,
    leaf_panel,
    leaf_rows,
    leaf_height,
    parent_inv,
    parent_panel,
    parent_rows,
    parent_height,
    root_inv,
):
    n = lax.axis_size("rows")
    chips = n // 2
    rcount, leaves, leaf_cols = leaf_rhs.shape
    leaf_local, leaf_width = leaf_panel.shape[1:]
    parent_cols, parent_width = parent_inv.shape[1:]
    parent_local = parent_panel.shape[1]
    root_width = root_inv.shape[1]
    root_inv = root_inv[None]
    root_local = root_inv.shape[1]
    root_cols = root_rhs.shape[1]
    piece = root_width // n
    tall = parent_width + root_width
    leaf_aligned = leaf_cols % LANES == 0
    root_aligned = root_cols % LANES == 0

    def flat():
        return lax.axis_index("leaf") * n + lax.axis_index("rows")

    def far_gather(x):
        return jnp.stack([x] + from_chips(lambda k: x))

    def leaf_columns(x):
        got = all_to_all(jnp.broadcast_to(x[None], (n,) + x.shape))
        return jnp.moveaxis(got, 0, 2).reshape(1, leaves, rcount, leaf_width)

    def leaf_product(x_refs, w_ref, s):
        if leaf_aligned:
            return both_halves(*x_refs, w_ref, s, xor=True)
        return times_transposed(x_refs[0][0, s], w_ref[s])

    def leaf_halves(x, w, name):
        return own_half(x, w, name, xor=True), swap(x)

    rhs = root_rhs
    if not root_aligned:
        rhs = lax.dynamic_update_slice_in_dim(
            jnp.zeros((rcount, root_width), F32), root_rhs, flat() * root_cols, 1
        )
    weights = (leaf_inv, leaf_panel, parent_inv, parent_panel, root_inv, leaf_rows, parent_rows)

    def round_rhs(x_ref, *refs):
        out_ref = refs[-1]
        for s in range(leaves):
            out_ref[s] = x_ref[:, s, :].astype(BF16)

    lb = call(
        round_rhs,
        [((leaves, rcount, leaf_cols), BF16)],
        [leaf_rhs] + [outside(w) for w in weights],
        [VMEM] + [pl.BlockSpec(memory_space=pltpu.HBM)] * len(weights),
        name="round_rhs",
    )[0]
    prepared = prepare(
        lb,
        [(leaf_rows, leaf_local, leaf_height), (parent_rows, parent_local, parent_height)],
    )
    lb = far_gather(lb) if leaf_aligned else leaf_columns(lb)
    lb, prepared, rhs = lax.optimization_barrier((lb, prepared, rhs))
    leaf_list, leaf_plan, parent_list, parent_plan = prepared
    lb = leaf_halves(lb, leaf_inv, "leaf_solve_own") if leaf_aligned else (lb,)

    def leaf_solve(*refs):
        x_refs, (w_ref, y_ref, send_ref) = refs[: len(lb)], refs[len(lb) :]
        for s in range(leaves):
            y = leaf_product(x_refs, w_ref, s)
            y_ref[s] = y
            send_ref[s] = y.astype(BF16)

    ly, lyb = call(
        leaf_solve,
        [((leaves, rcount, leaf_cols), F32), ((leaves, rcount, leaf_cols), BF16)],
        [*lb, pinned(leaf_inv)],
        [VMEM] * (len(lb) + 1),
        name="leaf_solve",
    )
    if leaf_aligned:
        lyb = leaf_halves(far_gather(lyb), leaf_panel, "leaf_update_own")
    else:
        lyb = (leaf_columns(lyb),)

    def leaf_update(*refs):
        x_refs, refs = refs[: len(lyb)], refs[len(lyb) :]
        plan_ref, w_ref, list_ref, rhs_ref, own_ref, other_ref, root_ref, *refs = refs
        update_ref, acc_ref, sum_ref = refs
        acc_ref[...] = jnp.zeros(acc_ref.shape, F32)
        for s in range(leaves):
            update_ref[s] = leaf_product(x_refs, w_ref, s)
        scatter_walk(plan_ref, list_ref, update_ref, acc_ref)
        for b in range(parent_width // LANES):
            sum_ref[:, b * LANES : (b + 1) * LANES] = -acc_ref[b]
        sum_ref[:, spot(lax.axis_index("rows"), parent_cols)] += rhs_ref[:, 0, :]
        deal(sum_ref, own_ref, other_ref)
        for b in range(root_width // LANES):
            root_ref[b] = acc_ref[parent_width // LANES + b]

    own, other, root_acc = call(
        leaf_update,
        [
            ((chips, rcount, parent_cols), F32),
            ((chips, rcount, parent_cols), BF16),
            ((root_width // LANES, rcount, LANES), F32),
        ],
        [*lyb, leaf_plan, pinned(leaf_panel), leaf_list, parent_rhs],
        [VMEM] * len(lyb) + [SMEM] + [VMEM] * 3,
        scratch=[
            pltpu.VMEM((leaves, rcount, leaf_local), F32),
            pltpu.VMEM((tall // LANES + BLOCKS, rcount, LANES), F32),
            pltpu.VMEM((rcount, parent_width), F32),
        ],
        name="leaf_update",
    )
    prb = chips_sum(own + swap(other).astype(F32)).astype(BF16)

    def parent_solve(part_ref, x_ref, w_ref, y_ref, send_ref):
        y = both_halves(part_ref, x_ref, w_ref, 0)
        y_ref[...] = y
        send_ref[...] = y.astype(BF16)

    py, pyb = call(
        parent_solve,
        [((rcount, parent_cols), F32), ((rcount, parent_cols), BF16)],
        [own_half(prb, parent_inv, "parent_solve_own"), swap(prb), pinned(parent_inv)],
        [VMEM] * 3,
        name="parent_solve",
    )
    pyb = far_gather(pyb)

    def parent_update(
        plan_ref, part_ref, x_ref, w_ref, list_ref, root_ref, rhs_ref, own_ref, other_ref,
        update_ref, acc_ref, sum_ref,
    ):
        for b in range(root_width // LANES):
            acc_ref[b] = root_ref[b]
        update_ref[0] = both_halves(part_ref, x_ref, w_ref, 0, xor=True)
        scatter_walk(plan_ref, list_ref, update_ref, acc_ref)
        for b in range(root_width // LANES):
            sum_ref[:, b * LANES : (b + 1) * LANES] = -acc_ref[b]
        if root_aligned:
            sum_ref[:, spot(flat(), root_cols)] += rhs_ref[...]
        else:
            sum_ref[...] += rhs_ref[...]
        deal(sum_ref, own_ref, other_ref)

    own, other = call(
        parent_update,
        [((chips, rcount, piece), F32), ((chips, rcount, piece), BF16)],
        [
            parent_plan,
            own_half(pyb, parent_panel, "parent_update_own", xor=True),
            swap(pyb),
            pinned(parent_panel),
            parent_list,
            root_acc,
            rhs,
        ],
        [SMEM] + [VMEM] * 6,
        scratch=[
            pltpu.VMEM((1, rcount, parent_local), F32),
            pltpu.VMEM((root_width // LANES + BLOCKS, rcount, LANES), F32),
            pltpu.VMEM((rcount, root_width), F32),
        ],
        name="parent_update",
    )
    rrb = chips_sum(leaf_sum(own + swap(other).astype(F32))).astype(BF16)

    def terms(x_ref, w_ref, out_ref, odd, xor=True):
        _, sets, _, cols = out_ref.shape
        for k in range(chips):
            at = spot(2 * (chip() ^ k if xor else k) + odd, cols)
            for s in range(sets):
                out_ref[k, s] = times(x_ref[s], w_ref[s, :, at]).astype(out_ref.dtype)

    def split_terms(w):
        return (chips, w.shape[0], rcount, w.shape[2] // n)

    def own_terms(x, w, name, xor=True):
        def body(x_ref, w_ref, out_ref):
            terms(x_ref, w_ref, out_ref, core(), xor)

        return call(
            body, [(split_terms(w), F32)], [x, pinned(w)], [VMEM] * 2, moved=12 << 20, name=name
        )[0]

    def total(x, w, other, name):
        own = own_terms(x, w, name, xor=False)
        return chips_sum((own + swap(other).astype(F32))[:, 0])

    def root_solve(part_ref, x_ref, w_ref, out_ref, y_ref):
        y_ref[0] = both_halves(part_ref, x_ref, w_ref, 0).astype(BF16)
        terms(y_ref, w_ref, out_ref, 1 - core(), xor=False)

    term, ryb = call(
        root_solve,
        [(split_terms(root_inv), BF16), ((1, rcount, root_local), BF16)],
        [own_half(rrb, root_inv, "root_solve_own"), swap(rrb), pinned(root_inv)],
        [VMEM] * 3,
        name="root_solve",
    )
    rxb = total(ryb, root_inv, term, "root_solve_back_own").astype(BF16)

    def blocks_of(source_ref, target_ref, start, width):
        for b in range(width // LANES):
            target_ref[start + b] = source_ref[:, b * LANES : (b + 1) * LANES].astype(F32)

    def reduce(own, other):
        other = swap(other)
        sums = [own[k] + other[k].astype(F32) for k in range(chips)]
        return [sums[0]] + from_chips(lambda k: sums[k].astype(BF16))

    def parent_back(
        plan_ref, own_ref, other_ref, rows_ref, w_ref, out_ref, whole_ref, sol_ref, found_ref, x_ref,
    ):
        unite(own_ref, other_ref, x_ref)
        if root_aligned:
            sol_ref[...] = x_ref[:, spot(flat(), root_cols)].astype(F32)
        else:
            sol_ref[...] = x_ref[...].astype(F32)
        blocks_of(x_ref, whole_ref, 0, root_width)
        gather_walk(plan_ref, rows_ref, whole_ref, found_ref)
        terms(found_ref, w_ref, out_ref, 1 - core())

    term, root_whole, root_sol, found = call(
        parent_back,
        [
            (split_terms(parent_panel), BF16),
            ((root_width // LANES + BLOCKS, rcount, LANES), F32),
            ((rcount, root_cols if root_aligned else root_width), F32),
            ((1, rcount, parent_local), BF16),
        ],
        [parent_plan, rxb, swap(rxb), parent_list, pinned(parent_panel)],
        [SMEM] + [VMEM] * 4,
        scratch=[pltpu.VMEM((rcount, root_width), BF16)],
        name="parent_back",
    )
    tails = reduce(own_terms(found, parent_panel, "parent_back_own"), term)

    def parent_solve_back(*refs):
        tail_refs, (y_ref, w_ref, out_ref, v_ref) = refs[:chips], refs[chips:]
        lost = sum(ref[0].astype(F32) for ref in tail_refs)
        v_ref[0] = (y_ref[...] - lost).astype(BF16)
        terms(v_ref, w_ref, out_ref, 1 - core(), xor=False)

    term, pvb = call(
        parent_solve_back,
        [(split_terms(parent_inv), BF16), ((1, rcount, parent_cols), BF16)],
        [*tails, py, pinned(parent_inv)],
        [VMEM] * (chips + 2),
        name="parent_solve_back",
    )
    px = total(pvb, parent_inv, term, "parent_solve_back_own")
    pxb = px.astype(BF16)

    def ancestors(
        plan_ref, px_ref, own_ref, other_ref, root_ref, rows_ref, sol_ref,
        x_ref, whole_ref, found_ref,
    ):
        sol_ref[...] = px_ref[chip()]
        unite(own_ref, other_ref, x_ref)
        blocks_of(x_ref, whole_ref, 0, parent_width)
        for b in range(root_width // LANES):
            whole_ref[parent_width // LANES + b] = root_ref[b]
        gather_walk(plan_ref, rows_ref, whole_ref, found_ref)

    def all_terms(x_ref, w_ref, out_ref):
        for s in range(leaves):
            out_ref[s] = times(x_ref[s], w_ref[s]).astype(BF16)

    def pieces_apart(term):
        return jnp.moveaxis(term.reshape(leaves, rcount, n, leaf_cols), 2, 0)

    whole_term = (leaves, rcount, leaf_width)
    found_shape = (leaves, rcount, leaf_local)
    scratch = [
        pltpu.VMEM((rcount, parent_width), BF16),
        pltpu.VMEM((tall // LANES + BLOCKS, rcount, LANES), F32),
    ]

    def leaf_back(*refs):
        ins, (w_ref, out_ref, sol_ref, found_ref, x_ref, whole_ref) = refs[:6], refs[6:]
        ancestors(*ins, sol_ref, x_ref, whole_ref, found_ref)
        if leaf_aligned:
            terms(found_ref, w_ref, out_ref, 1 - core())
        else:
            all_terms(found_ref, w_ref, out_ref)

    term, parent_sol, found = call(
        leaf_back,
        [
            (split_terms(leaf_panel) if leaf_aligned else whole_term, BF16),
            ((rcount, parent_cols), F32),
            (found_shape, BF16),
        ],
        [leaf_plan, px, pxb, swap(pxb), root_whole, leaf_list, pinned(leaf_panel)],
        [SMEM] + [VMEM] * 6,
        scratch=scratch,
        name="leaf_back",
    )
    if leaf_aligned:
        tails = reduce(own_terms(found, leaf_panel, "leaf_back_own"), term)
    else:
        tails = [all_to_all(pieces_apart(term)).astype(F32).sum(0)]

    def leaf_solve_back(*refs):
        tail_refs, (y_ref, w_ref, out_ref, v_ref) = refs[: len(tails)], refs[len(tails) :]
        for s in range(leaves):
            lost = sum(ref[s].astype(F32) for ref in tail_refs)
            v_ref[s] = (y_ref[s] - lost).astype(BF16)
        if leaf_aligned:
            terms(v_ref, w_ref, out_ref, 1 - core())
        else:
            all_terms(v_ref, w_ref, out_ref)

    term, lvb = call(
        leaf_solve_back,
        [
            (split_terms(leaf_panel) if leaf_aligned else whole_term, BF16),
            ((leaves, rcount, leaf_cols), BF16),
        ],
        [*tails, ly, pinned(leaf_inv)],
        [VMEM] * (len(tails) + 2),
        name="leaf_solve_back",
    )
    if leaf_aligned:
        parts = reduce(own_terms(lvb, leaf_inv, "leaf_solve_back_own"), term)
        leaf_sol = sum(p.astype(F32) for p in parts)
    else:
        leaf_sol = all_to_all(pieces_apart(term)).astype(F32).sum(0)
    if not root_aligned:
        root_sol = lax.dynamic_slice_in_dim(root_sol, flat() * root_cols, root_cols, 1)
    return (jnp.moveaxis(leaf_sol, 0, 1), parent_sol[:, None, :], root_sol)


def solution(mesh):
    return jax.shard_map(
        shards,
        mesh=mesh,
        in_specs=(
            P(None, "leaf", "rows"),
            P(None, "leaf", "rows"),
            P(None, ("leaf", "rows")),
            P("leaf", "rows", None),
            P("leaf", "rows", None),
            P("leaf", "rows"),
            P("leaf"),
            P("leaf", "rows", None),
            P("leaf", "rows", None),
            P("leaf", "rows"),
            P("leaf"),
            P("rows", None),
        ),
        out_specs=(P(None, "leaf", "rows"), P(None, "leaf", "rows"), P(None, ("leaf", "rows"))),
        check_vma=False,
    )
```

```python
import jax
import jax.numpy as jnp
from jax import lax
from jax.experimental import pallas as pl
from jax.experimental.pallas import tpu as pltpu
from jax.sharding import PartitionSpec as P

F32 = jnp.float32
BF16 = jnp.bfloat16
I32 = jnp.int32
LANES = 128
BLOCKS = 8
NONE = 1 << 24

VMEM = pl.BlockSpec(memory_space=pltpu.VMEM)
SMEM = pl.BlockSpec(memory_space=pltpu.SMEM)


def pinned(w):
    return pltpu.with_memory_space_constraint(w, pltpu.VMEM)


def outside(w):
    return pltpu.with_memory_space_constraint(w, pltpu.HBM)


def call(
    body, outs, ins, specs, out_specs=None, scratch=(), moved=0, limit=6 << 20, name=None
):
    return pl.pallas_call(
        body,
        out_shape=[jax.ShapeDtypeStruct(*o) if isinstance(o, tuple) else o for o in outs],
        in_specs=list(specs),
        out_specs=out_specs or [VMEM] * len(outs),
        scratch_shapes=list(scratch),
        cost_estimate=pl.CostEstimate(flops=0, bytes_accessed=moved, transcendentals=0),
        compiler_params=pltpu.CompilerParams(vmem_limit_bytes=limit),
        name=name,
    )(*ins)


def times_transposed(x, w):
    return lax.dot_general(x, w, (((1,), (1,)), ((), ())), preferred_element_type=F32)


def times(x, w):
    return lax.dot_general(x, w, (((1,), (0,)), ((), ())), preferred_element_type=F32)


def prepare(after, lists):
    count = len(lists)

    def one(first, rows_ref, height_ref, list_ref, plan_ref, scalar_ref):
        sets, length = rows_ref.shape
        tiles = length // LANES
        start = lax.axis_index("rows") * first
        lane = lax.broadcasted_iota(I32, (1, LANES), 1)
        rounds = 0
        for s in range(sets):
            used = height_ref[s] - start
            for tile in range(tiles):
                lanes = slice(tile * LANES, (tile + 1) * LANES)
                line = rows_ref[s : s + 1, lanes]
                list_ref[s : s + 1, lanes] = jnp.where(lane + tile * LANES < used, line, NONE)
                end = jnp.maximum(jnp.minimum(used, (tile + 1) * LANES) - 1, 0)
                lo = lax.shift_right_logical(scalar_ref[s, tile * LANES], 7)
                hi = lax.shift_right_logical(scalar_ref[s, end], 7)
                met = used > tile * LANES
                plan_ref[s * tiles + tile] = jnp.where(met, lo, 0)
                span = jnp.where(met, hi - lo + BLOCKS, 0)
                rounds = jnp.maximum(rounds, lax.shift_right_logical(span, 3))
        plan_ref[sets * tiles] = rounds

    def body(*refs):
        ins, outs = refs[1 : 2 * count + 1], refs[2 * count + 1 : 4 * count + 1]
        scalars, sems = refs[4 * count + 1 : -1], refs[-1]
        copies = [
            pltpu.make_async_copy(ins[2 * i], scalars[i], sems.at[i]) for i in range(count)
        ]
        for copy in copies:
            copy.start()
        for i, copy in enumerate(copies):
            copy.wait()
            one(lists[i][1], *ins[2 * i : 2 * i + 2], *outs[2 * i : 2 * i + 2], scalars[i])

    shapes, ins = [], [after]
    for rows, _, height in lists:
        sets, length = rows.shape
        shapes += [(rows.shape, I32), ((sets * (length // LANES) + 1,), I32)]
        ins += [rows, height]
    return call(
        body,
        shapes,
        ins,
        [pl.BlockSpec(memory_space=pl.ANY)] + [VMEM, SMEM] * count,
        out_specs=[VMEM, SMEM] * count,
        scratch=[pltpu.SMEM(x[0].shape, I32) for x in lists] + [pltpu.SemaphoreType.DMA((count,))],
        moved=4 << 20,
        limit=4 << 20,
        name="prepare",
    )


def walk(plan_ref, list_ref, blocks, visit):
    sets, length = list_ref.shape
    tiles = length // LANES

    def take_round(i, first):
        for tile in range(tiles):
            lanes = slice(tile * LANES, (tile + 1) * LANES)
            for s in range(sets):
                line = jnp.broadcast_to(list_ref[s : s + 1, lanes], (BLOCKS, LANES))
                lo = jnp.minimum(plan_ref[s * tiles + tile] + i * BLOCKS, blocks)
                visit(s, lanes, line, lo, first)

    take_round(0, True)

    def again(i, carry):
        take_round(i, False)
        return carry

    lax.fori_loop(1, plan_ref[sets * tiles], again, 0)


def along(x, index):
    return jnp.take_along_axis(x, index, axis=1, mode="promise_in_bounds")


def pick(x, index):
    inside = (index >= 0) & (index < LANES)
    return jnp.where(inside, along(x, index & (LANES - 1)), 0.0)


def position(line, lo):
    block = lax.broadcasted_iota(I32, line.shape, 0) + lo
    target = block * LANES + lax.broadcasted_iota(I32, line.shape, 1)
    below = jnp.zeros(line.shape, I32)
    step = LANES // 2
    while step:
        below = jnp.where(along(line, below + (step - 1)) < target, below + step, below)
        step //= 2
    return jnp.where(along(line, below) == target, below, -1)


def scatter_walk(plan_ref, list_ref, update_ref, acc_ref):
    def visit(s, lanes, line, lo, first):
        x, at = update_ref[s, :, lanes], position(line, lo)
        parts = [pick(x, jnp.broadcast_to(at[u : u + 1], x.shape)) for u in range(BLOCKS)]
        acc_ref[pl.ds(lo, BLOCKS)] += jnp.stack(parts)

    walk(plan_ref, list_ref, acc_ref.shape[0] - BLOCKS, visit)


def gather_walk(plan_ref, list_ref, source_ref, out_ref):
    def visit(s, lanes, line, lo, first):
        x = source_ref[pl.ds(lo, BLOCKS)]
        parts = [pick(x[u], line - (lo + u) * LANES) for u in range(BLOCKS)]
        found = sum(parts[1:], parts[0]).astype(out_ref.dtype)
        out_ref[s, :, lanes] = found if first else out_ref[s, :, lanes] + found

    walk(plan_ref, list_ref, source_ref.shape[0] - BLOCKS, visit)


def far_order(chips):
    order = list(range(chips))
    if chips > 3:
        order[-2:] = [chips - 1, chips - 2]
    return order


def core():
    return lax.axis_index("rows") & 1


def chip():
    return lax.axis_index("rows") // 2


def spot(r, w):
    return pl.ds(pl.multiple_of(r * w, LANES), w)


def unite(own_ref, other_ref, out_ref, *at, xor=False):
    odd, w = core(), own_ref.shape[-1]
    for k, j in enumerate(far_order(own_ref.shape[0])):
        c = chip() ^ j if xor else k
        out_ref[:, spot(2 * c + odd, w)] = own_ref[(k,) + at]
        out_ref[:, spot(2 * c + 1 - odd, w)] = other_ref[(k,) + at]


def deal(value_ref, own_ref, other_ref):
    odd = core()
    chips, _, w = own_ref.shape
    for k in range(chips):
        own_ref[k] = value_ref[:, spot(2 * k + odd, w)].astype(own_ref.dtype)
        other_ref[k] = value_ref[:, spot(2 * k + 1 - odd, w)].astype(other_ref.dtype)


def half_of(x_ref, w_ref, s, odd, xor, start=0):
    at = (s,) if len(x_ref.shape) == 4 else ()
    chips, cols = x_ref.shape[0], x_ref.shape[-1]
    picked, columns = [], []
    for k, j in list(enumerate(far_order(chips)))[start:]:
        c = chip() ^ j if xor else k
        picked.append(x_ref[(k,) + at])
        columns.append(w_ref[s, :, spot(2 * c + odd, cols)])
    return times_transposed(jnp.concatenate(picked, axis=1), jnp.concatenate(columns, axis=1))


def own_half(x, w, name, xor=False, first=None):
    sets, rows = w.shape[:2]

    def body(x_ref, w_ref, *refs):
        for s in range(sets):
            got = half_of(x_ref, w_ref, s, core(), xor, len(refs) - 1)
            refs[-1][s] = got if first is None else got + refs[0][s]

    return call(
        body,
        [((sets, x.shape[-2], rows), F32)],
        [x, pinned(w)] + ([] if first is None else [first]),
        [VMEM] * (2 if first is None else 3),
        moved=12 << 20,
        name=name,
    )[0]


def own_piece(x, w, name):
    sets, rows = w.shape[:2]

    def body(x_ref, w_ref, out_ref):
        for s in range(sets):
            columns = spot(lax.axis_index("rows"), x_ref.shape[-1])
            out_ref[s] = times_transposed(x_ref[s], w_ref[s, :, columns])

    return call(
        body,
        [((sets, x.shape[-2], rows), F32)],
        [x, pinned(w)],
        [VMEM] * 2,
        moved=4 << 20,
        name=name,
    )[0]


def both_halves(part_ref, x_ref, w_ref, s, xor=False):
    return part_ref[s] + half_of(x_ref, w_ref, s, 1 - core(), xor)


def all_to_all(x):
    return lax.all_to_all(x, "rows", 0, 0)


def swap(x):
    n = lax.axis_size("rows")
    return lax.ppermute(x, "rows", [(i, i ^ 1) for i in range(n)])


def far(x, k):
    n = lax.axis_size("rows")
    return lax.ppermute(x, "rows", [(i, i ^ (2 * k)) for i in range(n)])


def from_chips(piece):
    return [far(piece(k), k) for k in far_order(lax.axis_size("rows") // 2)[1:]]


def chips_sum(x):
    b = x.astype(BF16)
    return x + sum(got.astype(F32) for got in from_chips(lambda k: b))


def leaf_sum(x):
    n = lax.axis_size("leaf")
    b = x.astype(BF16)
    for k in range(1, n):
        x = x + lax.ppermute(b, "leaf", [(i, (i + k) % n) for i in range(n)]).astype(F32)
    return x


def shards(
    leaf_rhs,
    parent_rhs,
    root_rhs,
    leaf_inv,
    leaf_panel,
    leaf_rows,
    leaf_height,
    parent_inv,
    parent_panel,
    parent_rows,
    parent_height,
    root_inv,
):
    n = lax.axis_size("rows")
    chips = n // 2
    rcount, leaves, leaf_cols = leaf_rhs.shape
    leaf_local, leaf_width = leaf_panel.shape[1:]
    parent_cols, parent_width = parent_inv.shape[1:]
    parent_local = parent_panel.shape[1]
    root_width = root_inv.shape[1]
    root_inv = root_inv[None]
    root_local = root_inv.shape[1]
    root_cols = root_rhs.shape[1]
    piece = root_width // n
    tall = parent_width + root_width
    leaf_aligned = leaf_cols % LANES == 0
    root_aligned = root_cols % LANES == 0

    def flat():
        return lax.axis_index("leaf") * n + lax.axis_index("rows")

    def far_gather(x):
        return jnp.stack([x] + from_chips(lambda k: x))

    def leaf_columns(x):
        got = all_to_all(jnp.broadcast_to(x[None], (n,) + x.shape))
        return jnp.moveaxis(got, 0, 2).reshape(1, leaves, rcount, leaf_width)

    def leaf_product(x_refs, w_ref, s):
        if leaf_aligned:
            return both_halves(*x_refs, w_ref, s, xor=True)
        return times_transposed(x_refs[0][0, s], w_ref[s])

    def leaf_halves(x, w, name, first=None):
        return own_half(x, w, name, True, first), swap(x)

    rhs = root_rhs
    if not root_aligned:
        rhs = lax.dynamic_update_slice_in_dim(
            jnp.zeros((rcount, root_width), F32), root_rhs, flat() * root_cols, 1
        )
    weights = (leaf_inv, leaf_panel, parent_inv, parent_panel, root_inv, leaf_rows, parent_rows)

    def round_rhs(x_ref, *refs):
        out_ref = refs[-1]
        for s in range(leaves):
            out_ref[s] = x_ref[:, s, :].astype(BF16)

    lb = call(
        round_rhs,
        [((leaves, rcount, leaf_cols), BF16)],
        [leaf_rhs] + [outside(w) for w in weights],
        [VMEM] + [pl.BlockSpec(memory_space=pltpu.HBM)] * len(weights),
        name="round_rhs",
    )[0]
    prepared = prepare(
        lb,
        [(leaf_rows, leaf_local, leaf_height), (parent_rows, parent_local, parent_height)],
    )
    lb = far_gather(lb) if leaf_aligned else leaf_columns(lb)
    lb, prepared, rhs = lax.optimization_barrier((lb, prepared, rhs))
    leaf_list, leaf_plan, parent_list, parent_plan = prepared
    lb = leaf_halves(lb, leaf_inv, "leaf_solve_own") if leaf_aligned else (lb,)

    def leaf_solve(*refs):
        x_refs, (w_ref, y_ref, send_ref) = refs[: len(lb)], refs[len(lb) :]
        for s in range(leaves):
            y = leaf_product(x_refs, w_ref, s)
            y_ref[s] = y
            send_ref[s] = y.astype(BF16)

    ly, lyb = call(
        leaf_solve,
        [((leaves, rcount, leaf_cols), F32), ((leaves, rcount, leaf_cols), BF16)],
        [*lb, pinned(leaf_inv)],
        [VMEM] * (len(lb) + 1),
        name="leaf_solve",
    )
    if leaf_aligned:
        first = own_piece(lyb, leaf_panel, "leaf_update_first")
        lyb, first = lax.optimization_barrier((far_gather(lyb), first))
        lyb = leaf_halves(lyb, leaf_panel, "leaf_update_own", first)
    else:
        lyb = (leaf_columns(lyb),)

    def leaf_update(*refs):
        x_refs, refs = refs[: len(lyb)], refs[len(lyb) :]
        plan_ref, w_ref, list_ref, rhs_ref, own_ref, other_ref, root_ref, *refs = refs
        update_ref, acc_ref, sum_ref = refs
        acc_ref[...] = jnp.zeros(acc_ref.shape, F32)
        for s in range(leaves):
            update_ref[s] = leaf_product(x_refs, w_ref, s)
        scatter_walk(plan_ref, list_ref, update_ref, acc_ref)
        for b in range(parent_width // LANES):
            sum_ref[:, b * LANES : (b + 1) * LANES] = -acc_ref[b]
        sum_ref[:, spot(lax.axis_index("rows"), parent_cols)] += rhs_ref[:, 0, :]
        deal(sum_ref, own_ref, other_ref)
        for b in range(root_width // LANES):
            root_ref[b] = acc_ref[parent_width // LANES + b]

    own, other, root_acc = call(
        leaf_update,
        [
            ((chips, rcount, parent_cols), F32),
            ((chips, rcount, parent_cols), BF16),
            ((root_width // LANES, rcount, LANES), F32),
        ],
        [*lyb, leaf_plan, pinned(leaf_panel), leaf_list, parent_rhs],
        [VMEM] * len(lyb) + [SMEM] + [VMEM] * 3,
        scratch=[
            pltpu.VMEM((leaves, rcount, leaf_local), F32),
            pltpu.VMEM((tall // LANES + BLOCKS, rcount, LANES), F32),
            pltpu.VMEM((rcount, parent_width), F32),
        ],
        name="leaf_update",
    )
    prb = chips_sum(own + swap(other).astype(F32)).astype(BF16)

    def parent_solve(part_ref, x_ref, w_ref, y_ref, send_ref):
        y = both_halves(part_ref, x_ref, w_ref, 0)
        y_ref[...] = y
        send_ref[...] = y.astype(BF16)

    py, pyb = call(
        parent_solve,
        [((rcount, parent_cols), F32), ((rcount, parent_cols), BF16)],
        [own_half(prb, parent_inv, "parent_solve_own"), swap(prb), pinned(parent_inv)],
        [VMEM] * 3,
        name="parent_solve",
    )
    pyb = far_gather(pyb)

    def parent_update(
        plan_ref, part_ref, x_ref, w_ref, list_ref, root_ref, rhs_ref, own_ref, other_ref,
        update_ref, acc_ref, sum_ref,
    ):
        for b in range(root_width // LANES):
            acc_ref[b] = root_ref[b]
        update_ref[0] = both_halves(part_ref, x_ref, w_ref, 0, xor=True)
        scatter_walk(plan_ref, list_ref, update_ref, acc_ref)
        for b in range(root_width // LANES):
            sum_ref[:, b * LANES : (b + 1) * LANES] = -acc_ref[b]
        if root_aligned:
            sum_ref[:, spot(flat(), root_cols)] += rhs_ref[...]
        else:
            sum_ref[...] += rhs_ref[...]
        deal(sum_ref, own_ref, other_ref)

    own, other = call(
        parent_update,
        [((chips, rcount, piece), F32), ((chips, rcount, piece), BF16)],
        [
            parent_plan,
            own_half(pyb, parent_panel, "parent_update_own", xor=True),
            swap(pyb),
            pinned(parent_panel),
            parent_list,
            root_acc,
            rhs,
        ],
        [SMEM] + [VMEM] * 6,
        scratch=[
            pltpu.VMEM((1, rcount, parent_local), F32),
            pltpu.VMEM((root_width // LANES + BLOCKS, rcount, LANES), F32),
            pltpu.VMEM((rcount, root_width), F32),
        ],
        name="parent_update",
    )
    rrb = chips_sum(leaf_sum(own + swap(other).astype(F32))).astype(BF16)

    def terms(x_ref, w_ref, out_ref, odd, xor=True):
        _, sets, _, cols = out_ref.shape
        for k in range(chips):
            at = spot(2 * (chip() ^ k if xor else k) + odd, cols)
            for s in range(sets):
                out_ref[k, s] = times(x_ref[s], w_ref[s, :, at]).astype(out_ref.dtype)

    def split_terms(w):
        return (chips, w.shape[0], rcount, w.shape[2] // n)

    def own_terms(x, w, name, xor=True):
        def body(x_ref, w_ref, out_ref):
            terms(x_ref, w_ref, out_ref, core(), xor)

        return call(
            body, [(split_terms(w), F32)], [x, pinned(w)], [VMEM] * 2, moved=12 << 20, name=name
        )[0]

    def total(x, w, other, name):
        own = own_terms(x, w, name, xor=False)
        return chips_sum((own + swap(other).astype(F32))[:, 0])

    def root_solve(part_ref, x_ref, w_ref, out_ref, y_ref):
        y_ref[0] = both_halves(part_ref, x_ref, w_ref, 0).astype(BF16)
        terms(y_ref, w_ref, out_ref, 1 - core(), xor=False)

    term, ryb = call(
        root_solve,
        [(split_terms(root_inv), BF16), ((1, rcount, root_local), BF16)],
        [own_half(rrb, root_inv, "root_solve_own"), swap(rrb), pinned(root_inv)],
        [VMEM] * 3,
        name="root_solve",
    )
    rxb = total(ryb, root_inv, term, "root_solve_back_own").astype(BF16)

    def blocks_of(source_ref, target_ref, start, width):
        for b in range(width // LANES):
            target_ref[start + b] = source_ref[:, b * LANES : (b + 1) * LANES].astype(F32)

    def reduce(own, other):
        other = swap(other)
        sums = [own[k] + other[k].astype(F32) for k in range(chips)]
        return [sums[0]] + from_chips(lambda k: sums[k].astype(BF16))

    def parent_back(
        plan_ref, own_ref, other_ref, rows_ref, w_ref, out_ref, whole_ref, sol_ref, found_ref, x_ref,
    ):
        unite(own_ref, other_ref, x_ref)
        if root_aligned:
            sol_ref[...] = x_ref[:, spot(flat(), root_cols)].astype(F32)
        else:
            sol_ref[...] = x_ref[...].astype(F32)
        blocks_of(x_ref, whole_ref, 0, root_width)
        gather_walk(plan_ref, rows_ref, whole_ref, found_ref)
        terms(found_ref, w_ref, out_ref, 1 - core())

    term, root_whole, root_sol, found = call(
        parent_back,
        [
            (split_terms(parent_panel), BF16),
            ((root_width // LANES + BLOCKS, rcount, LANES), F32),
            ((rcount, root_cols if root_aligned else root_width), F32),
            ((1, rcount, parent_local), BF16),
        ],
        [parent_plan, rxb, swap(rxb), parent_list, pinned(parent_panel)],
        [SMEM] + [VMEM] * 4,
        scratch=[pltpu.VMEM((rcount, root_width), BF16)],
        name="parent_back",
    )
    tails = reduce(own_terms(found, parent_panel, "parent_back_own"), term)

    def parent_solve_back(*refs):
        tail_refs, (y_ref, w_ref, out_ref, v_ref) = refs[:chips], refs[chips:]
        lost = sum(ref[0].astype(F32) for ref in tail_refs)
        v_ref[0] = (y_ref[...] - lost).astype(BF16)
        terms(v_ref, w_ref, out_ref, 1 - core(), xor=False)

    term, pvb = call(
        parent_solve_back,
        [(split_terms(parent_inv), BF16), ((1, rcount, parent_cols), BF16)],
        [*tails, py, pinned(parent_inv)],
        [VMEM] * (chips + 2),
        name="parent_solve_back",
    )
    px = total(pvb, parent_inv, term, "parent_solve_back_own")
    pxb = px.astype(BF16)

    def ancestors(
        plan_ref, px_ref, own_ref, other_ref, root_ref, rows_ref, sol_ref,
        x_ref, whole_ref, found_ref,
    ):
        sol_ref[...] = px_ref[chip()]
        unite(own_ref, other_ref, x_ref)
        blocks_of(x_ref, whole_ref, 0, parent_width)
        for b in range(root_width // LANES):
            whole_ref[parent_width // LANES + b] = root_ref[b]
        gather_walk(plan_ref, rows_ref, whole_ref, found_ref)

    def all_terms(x_ref, w_ref, out_ref):
        for s in range(leaves):
            out_ref[s] = times(x_ref[s], w_ref[s]).astype(BF16)

    def pieces_apart(term):
        return jnp.moveaxis(term.reshape(leaves, rcount, n, leaf_cols), 2, 0)

    whole_term = (leaves, rcount, leaf_width)
    found_shape = (leaves, rcount, leaf_local)
    scratch = [
        pltpu.VMEM((rcount, parent_width), BF16),
        pltpu.VMEM((tall // LANES + BLOCKS, rcount, LANES), F32),
    ]

    def leaf_back(*refs):
        ins, (w_ref, out_ref, sol_ref, found_ref, x_ref, whole_ref) = refs[:6], refs[6:]
        ancestors(*ins, sol_ref, x_ref, whole_ref, found_ref)
        if leaf_aligned:
            terms(found_ref, w_ref, out_ref, 1 - core())
        else:
            all_terms(found_ref, w_ref, out_ref)

    term, parent_sol, found = call(
        leaf_back,
        [
            (split_terms(leaf_panel) if leaf_aligned else whole_term, BF16),
            ((rcount, parent_cols), F32),
            (found_shape, BF16),
        ],
        [leaf_plan, px, pxb, swap(pxb), root_whole, leaf_list, pinned(leaf_panel)],
        [SMEM] + [VMEM] * 6,
        scratch=scratch,
        name="leaf_back",
    )
    if leaf_aligned:
        tails = reduce(own_terms(found, leaf_panel, "leaf_back_own"), term)
    else:
        tails = [all_to_all(pieces_apart(term)).astype(F32).sum(0)]

    def leaf_solve_back(*refs):
        tail_refs, (y_ref, w_ref, out_ref, v_ref) = refs[: len(tails)], refs[len(tails) :]
        for s in range(leaves):
            lost = sum(ref[s].astype(F32) for ref in tail_refs)
            v_ref[s] = (y_ref[s] - lost).astype(BF16)
        if leaf_aligned:
            terms(v_ref, w_ref, out_ref, 1 - core())
        else:
            all_terms(v_ref, w_ref, out_ref)

    term, lvb = call(
        leaf_solve_back,
        [
            (split_terms(leaf_panel) if leaf_aligned else whole_term, BF16),
            ((leaves, rcount, leaf_cols), BF16),
        ],
        [*tails, ly, pinned(leaf_inv)],
        [VMEM] * (len(tails) + 2),
        name="leaf_solve_back",
    )
    if leaf_aligned:
        parts = reduce(own_terms(lvb, leaf_inv, "leaf_solve_back_own"), term)
        leaf_sol = sum(p.astype(F32) for p in parts)
    else:
        leaf_sol = all_to_all(pieces_apart(term)).astype(F32).sum(0)
    if not root_aligned:
        root_sol = lax.dynamic_slice_in_dim(root_sol, flat() * root_cols, root_cols, 1)
    return (jnp.moveaxis(leaf_sol, 0, 1), parent_sol[:, None, :], root_sol)


def solution(mesh):
    return jax.shard_map(
        shards,
        mesh=mesh,
        in_specs=(
            P(None, "leaf", "rows"),
            P(None, "leaf", "rows"),
            P(None, ("leaf", "rows")),
            P("leaf", "rows", None),
            P("leaf", "rows", None),
            P("leaf", "rows"),
            P("leaf"),
            P("leaf", "rows", None),
            P("leaf", "rows", None),
            P("leaf", "rows"),
            P("leaf"),
            P("rows", None),
        ),
        out_specs=(P(None, "leaf", "rows"), P(None, "leaf", "rows"), P(None, ("leaf", "rows"))),
        check_vma=False,
    )
```

```python
import jax
import jax.numpy as jnp
from jax import lax
from jax.experimental import pallas as pl
from jax.experimental.pallas import tpu as pltpu
from jax.sharding import PartitionSpec as P

F32 = jnp.float32
BF16 = jnp.bfloat16
I32 = jnp.int32
LANES = 128
BLOCKS = 8
NONE = 1 << 24

VMEM = pl.BlockSpec(memory_space=pltpu.VMEM)
SMEM = pl.BlockSpec(memory_space=pltpu.SMEM)


def pinned(w):
    return pltpu.with_memory_space_constraint(w, pltpu.VMEM)


def outside(w):
    return pltpu.with_memory_space_constraint(w, pltpu.HBM)


def call(
    body, outs, ins, specs, out_specs=None, scratch=(), moved=0, limit=6 << 20, name=None
):
    return pl.pallas_call(
        body,
        out_shape=[jax.ShapeDtypeStruct(*o) if isinstance(o, tuple) else o for o in outs],
        in_specs=list(specs),
        out_specs=out_specs or [VMEM] * len(outs),
        scratch_shapes=list(scratch),
        cost_estimate=pl.CostEstimate(flops=0, bytes_accessed=moved, transcendentals=0),
        compiler_params=pltpu.CompilerParams(vmem_limit_bytes=limit),
        name=name,
    )(*ins)


def times_transposed(x, w):
    return lax.dot_general(x, w, (((1,), (1,)), ((), ())), preferred_element_type=F32)


def times(x, w):
    return lax.dot_general(x, w, (((1,), (0,)), ((), ())), preferred_element_type=F32)


def prepare(after, lists):
    count = len(lists)

    def one(first, rows_ref, height_ref, list_ref, plan_ref, scalar_ref):
        sets, length = rows_ref.shape
        tiles = length // LANES
        start = lax.axis_index("rows") * first
        lane = lax.broadcasted_iota(I32, (1, LANES), 1)
        rounds = 0
        for s in range(sets):
            used = height_ref[s] - start
            for tile in range(tiles):
                lanes = slice(tile * LANES, (tile + 1) * LANES)
                line = rows_ref[s : s + 1, lanes]
                list_ref[s : s + 1, lanes] = jnp.where(lane + tile * LANES < used, line, NONE)
                end = jnp.maximum(jnp.minimum(used, (tile + 1) * LANES) - 1, 0)
                lo = lax.shift_right_logical(scalar_ref[s, tile * LANES], 7)
                hi = lax.shift_right_logical(scalar_ref[s, end], 7)
                met = used > tile * LANES
                plan_ref[s * tiles + tile] = jnp.where(met, lo, 0)
                span = jnp.where(met, hi - lo + BLOCKS, 0)
                rounds = jnp.maximum(rounds, lax.shift_right_logical(span, 3))
        plan_ref[sets * tiles] = rounds

    def body(*refs):
        ins, outs = refs[1 : 2 * count + 1], refs[2 * count + 1 : 4 * count + 1]
        scalars, sems = refs[4 * count + 1 : -1], refs[-1]
        copies = [
            pltpu.make_async_copy(ins[2 * i], scalars[i], sems.at[i]) for i in range(count)
        ]
        for copy in copies:
            copy.start()
        for i, copy in enumerate(copies):
            copy.wait()
            one(lists[i][1], *ins[2 * i : 2 * i + 2], *outs[2 * i : 2 * i + 2], scalars[i])

    shapes, ins = [], [after]
    for rows, _, height in lists:
        sets, length = rows.shape
        shapes += [(rows.shape, I32), ((sets * (length // LANES) + 1,), I32)]
        ins += [rows, height]
    return call(
        body,
        shapes,
        ins,
        [pl.BlockSpec(memory_space=pl.ANY)] + [VMEM, SMEM] * count,
        out_specs=[VMEM, SMEM] * count,
        scratch=[pltpu.SMEM(x[0].shape, I32) for x in lists] + [pltpu.SemaphoreType.DMA((count,))],
        moved=4 << 20,
        limit=4 << 20,
        name="prepare",
    )


def walk(plan_ref, list_ref, blocks, visit):
    sets, length = list_ref.shape
    tiles = length // LANES

    def take_round(i, first):
        for tile in range(tiles):
            lanes = slice(tile * LANES, (tile + 1) * LANES)
            for s in range(sets):
                line = jnp.broadcast_to(list_ref[s : s + 1, lanes], (BLOCKS, LANES))
                lo = jnp.minimum(plan_ref[s * tiles + tile] + i * BLOCKS, blocks)
                visit(s, lanes, line, lo, first)

    take_round(0, True)

    def again(i, carry):
        take_round(i, False)
        return carry

    lax.fori_loop(1, plan_ref[sets * tiles], again, 0)


def along(x, index):
    return jnp.take_along_axis(x, index, axis=1, mode="promise_in_bounds")


def pick(x, index):
    inside = (index >= 0) & (index < LANES)
    return jnp.where(inside, along(x, index & (LANES - 1)), 0.0)


def position(line, lo):
    block = lax.broadcasted_iota(I32, line.shape, 0) + lo
    target = block * LANES + lax.broadcasted_iota(I32, line.shape, 1)
    below = jnp.zeros(line.shape, I32)
    step = LANES // 2
    while step:
        below = jnp.where(along(line, below + (step - 1)) < target, below + step, below)
        step //= 2
    return jnp.where(along(line, below) == target, below, -1)


def find(plan, targets, width):
    sets, length = targets.shape

    def body(plan_ref, list_ref, out_ref):
        tiles = length // LANES
        for tile in range(tiles):
            for s in range(sets):
                line = list_ref[s : s + 1, tile * LANES : (tile + 1) * LANES]
                lo = plan_ref[s * tiles + tile]
                out_ref[s, tile] = position(jnp.broadcast_to(line, (BLOCKS, LANES)), lo)

    return call(
        body,
        [((sets, length // LANES, BLOCKS, LANES), I32)],
        [plan, targets],
        [SMEM, VMEM],
        moved=2 << 20,
        name="find",
    )[0]


def scatter_walk(plan_ref, list_ref, at_ref, update_ref, acc_ref):
    def visit(s, lanes, line, lo, first):
        x = update_ref[s, :, lanes]
        at = at_ref[s, lanes.start // LANES] if first else position(line, lo)
        parts = [pick(x, jnp.broadcast_to(at[u : u + 1], x.shape)) for u in range(BLOCKS)]
        acc_ref[pl.ds(lo, BLOCKS)] += jnp.stack(parts)

    walk(plan_ref, list_ref, acc_ref.shape[0] - BLOCKS, visit)


def gather_walk(plan_ref, list_ref, source_ref, out_ref):
    def visit(s, lanes, line, lo, first):
        x = source_ref[pl.ds(lo, BLOCKS)]
        parts = [pick(x[u], line - (lo + u) * LANES) for u in range(BLOCKS)]
        found = sum(parts[1:], parts[0]).astype(out_ref.dtype)
        out_ref[s, :, lanes] = found if first else out_ref[s, :, lanes] + found

    walk(plan_ref, list_ref, source_ref.shape[0] - BLOCKS, visit)


def far_order(chips):
    return [0] + list(range(2, chips)) + [1] if chips > 1 else [0]


def core():
    return lax.axis_index("rows") & 1


def chip():
    return lax.axis_index("rows") // 2


def spot(r, w):
    return pl.ds(pl.multiple_of(r * w, LANES), w)


def unite(own_ref, other_ref, out_ref, *at, xor=False):
    odd, w = core(), own_ref.shape[-1]
    for k, j in enumerate(far_order(own_ref.shape[0])):
        c = chip() ^ j if xor else k
        out_ref[:, spot(2 * c + odd, w)] = own_ref[(k,) + at]
        out_ref[:, spot(2 * c + 1 - odd, w)] = other_ref[(k,) + at]


def deal(value_ref, own_ref, other_ref):
    odd = core()
    chips, _, w = own_ref.shape
    for k in range(chips):
        own_ref[k] = value_ref[:, spot(2 * k + odd, w)].astype(own_ref.dtype)
        other_ref[k] = value_ref[:, spot(2 * k + 1 - odd, w)].astype(other_ref.dtype)


def half_of(x_ref, w_ref, s, odd, xor, but=()):
    at = (s,) if len(x_ref.shape) == 4 else ()
    chips, cols = x_ref.shape[0], x_ref.shape[-1]
    picked, columns = [], []
    for k, j in enumerate(far_order(chips)):
        if j in but:
            continue
        c = chip() ^ j if xor else k
        picked.append(x_ref[(k,) + at])
        columns.append(w_ref[s, :, spot(2 * c + odd, cols)])
    return times_transposed(jnp.concatenate(picked, axis=1), jnp.concatenate(columns, axis=1))


def own_half(x, w, name, xor=False, done=None, but=()):
    sets, rows = w.shape[:2]

    def body(x_ref, w_ref, *refs):
        for s in range(sets):
            got = half_of(x_ref, w_ref, s, core(), xor, but)
            refs[-1][s] = got if done is None else got + refs[0][s]

    return call(
        body,
        [((sets, x.shape[-2], rows), F32)],
        [x, pinned(w)] + ([] if done is None else [done]),
        [VMEM] * (2 if done is None else 3),
        moved=12 << 20,
        name=name,
    )[0]


def one_piece(x, w, k, name, done=None):
    sets, rows = w.shape[:2]

    def body(x_ref, w_ref, *refs):
        columns = spot(2 * (chip() ^ k) + core(), x_ref.shape[-1])
        for s in range(sets):
            got = times_transposed(x_ref[s], w_ref[s, :, columns])
            refs[-1][s] = got if done is None else got + refs[0][s]

    return call(
        body,
        [((sets, x.shape[-2], rows), F32)],
        [x, pinned(w)] + ([] if done is None else [done]),
        [VMEM] * (2 if done is None else 3),
        moved=4 << 20,
        name=name,
    )[0]


def both_halves(part_ref, x_ref, w_ref, s, xor=False):
    return part_ref[s] + half_of(x_ref, w_ref, s, 1 - core(), xor)


def all_to_all(x):
    return lax.all_to_all(x, "rows", 0, 0)


def swap(x):
    n = lax.axis_size("rows")
    return lax.ppermute(x, "rows", [(i, i ^ 1) for i in range(n)])


def far(x, k):
    n = lax.axis_size("rows")
    return lax.ppermute(x, "rows", [(i, i ^ (2 * k)) for i in range(n)])


def from_chips(piece):
    return [far(piece(k), k) for k in far_order(lax.axis_size("rows") // 2)[1:]]


def chips_sum(x):
    b = x.astype(BF16)
    return x + sum(got.astype(F32) for got in from_chips(lambda k: b))


def leaf_sum(x):
    n = lax.axis_size("leaf")
    b = x.astype(BF16)
    for k in range(1, n):
        x = x + lax.ppermute(b, "leaf", [(i, (i + k) % n) for i in range(n)]).astype(F32)
    return x


def shards(
    leaf_rhs,
    parent_rhs,
    root_rhs,
    leaf_inv,
    leaf_panel,
    leaf_rows,
    leaf_height,
    parent_inv,
    parent_panel,
    parent_rows,
    parent_height,
    root_inv,
):
    n = lax.axis_size("rows")
    chips = n // 2
    rcount, leaves, leaf_cols = leaf_rhs.shape
    leaf_local, leaf_width = leaf_panel.shape[1:]
    parent_cols, parent_width = parent_inv.shape[1:]
    parent_local = parent_panel.shape[1]
    root_width = root_inv.shape[1]
    root_inv = root_inv[None]
    root_local = root_inv.shape[1]
    root_cols = root_rhs.shape[1]
    piece = root_width // n
    tall = parent_width + root_width
    leaf_aligned = leaf_cols % LANES == 0
    root_aligned = root_cols % LANES == 0

    def flat():
        return lax.axis_index("leaf") * n + lax.axis_index("rows")

    def far_gather(x):
        return jnp.stack([x] + from_chips(lambda k: x))

    def leaf_columns(x):
        got = all_to_all(jnp.broadcast_to(x[None], (n,) + x.shape))
        return jnp.moveaxis(got, 0, 2).reshape(1, leaves, rcount, leaf_width)

    def leaf_product(x_refs, w_ref, s):
        if leaf_aligned:
            return both_halves(*x_refs, w_ref, s, xor=True)
        return times_transposed(x_refs[0][0, s], w_ref[s])

    def leaf_halves(x, w, name, done=None, but=()):
        return own_half(x, w, name, True, done, but), swap(x)

    rhs = root_rhs
    if not root_aligned:
        rhs = lax.dynamic_update_slice_in_dim(
            jnp.zeros((rcount, root_width), F32), root_rhs, flat() * root_cols, 1
        )
    weights = (leaf_inv, leaf_panel, parent_inv, parent_panel, root_inv, leaf_rows, parent_rows)

    def round_rhs(x_ref, *refs):
        out_ref = refs[-1]
        for s in range(leaves):
            out_ref[s] = x_ref[:, s, :].astype(BF16)

    lb = call(
        round_rhs,
        [((leaves, rcount, leaf_cols), BF16)],
        [leaf_rhs] + [outside(w) for w in weights],
        [VMEM] + [pl.BlockSpec(memory_space=pltpu.HBM)] * len(weights),
        name="round_rhs",
    )[0]
    prepared = prepare(lb, [(leaf_rows, leaf_local, leaf_height)])
    lb = far_gather(lb) if leaf_aligned else leaf_columns(lb)
    lb, prepared, rhs = lax.optimization_barrier((lb, prepared, rhs))
    leaf_list, leaf_plan = prepared
    lb = leaf_halves(lb, leaf_inv, "leaf_solve_own") if leaf_aligned else (lb,)
    lb, leaf_at = lax.optimization_barrier((lb, find(leaf_plan, leaf_list, tall)))

    def leaf_solve(*refs):
        x_refs, (w_ref, y_ref, send_ref) = refs[: len(lb)], refs[len(lb) :]
        for s in range(leaves):
            y = leaf_product(x_refs, w_ref, s)
            y_ref[s] = y
            send_ref[s] = y.astype(BF16)

    ly, lyb = call(
        leaf_solve,
        [((leaves, rcount, leaf_cols), F32), ((leaves, rcount, leaf_cols), BF16)],
        [*lb, pinned(leaf_inv)],
        [VMEM] * (len(lb) + 1),
        name="leaf_solve",
    )
    if leaf_aligned:
        done = one_piece(lyb, leaf_panel, 0, "leaf_update_first")
        lyb, done = lax.optimization_barrier((far_gather(lyb), done))
        lyb = leaf_halves(lyb, leaf_panel, "leaf_update_own", done, (0,))
    else:
        lyb = (leaf_columns(lyb),)

    def leaf_update(*refs):
        x_refs, refs = refs[: len(lyb)], refs[len(lyb) :]
        plan_ref, w_ref, list_ref, at_ref, rhs_ref, own_ref, other_ref, root_ref, *refs = refs
        update_ref, acc_ref, sum_ref = refs
        acc_ref[...] = jnp.zeros(acc_ref.shape, F32)
        for s in range(leaves):
            update_ref[s] = leaf_product(x_refs, w_ref, s)
        scatter_walk(plan_ref, list_ref, at_ref, update_ref, acc_ref)
        for b in range(parent_width // LANES):
            sum_ref[:, b * LANES : (b + 1) * LANES] = -acc_ref[b]
        sum_ref[:, spot(lax.axis_index("rows"), parent_cols)] += rhs_ref[:, 0, :]
        deal(sum_ref, own_ref, other_ref)
        for b in range(root_width // LANES):
            root_ref[b] = acc_ref[parent_width // LANES + b]

    own, other, root_acc = call(
        leaf_update,
        [
            ((chips, rcount, parent_cols), F32),
            ((chips, rcount, parent_cols), BF16),
            ((root_width // LANES, rcount, LANES), F32),
        ],
        [*lyb, leaf_plan, pinned(leaf_panel), leaf_list, leaf_at, parent_rhs],
        [VMEM] * len(lyb) + [SMEM] + [VMEM] * 4,
        scratch=[
            pltpu.VMEM((leaves, rcount, leaf_local), F32),
            pltpu.VMEM((tall // LANES + BLOCKS, rcount, LANES), F32),
            pltpu.VMEM((rcount, parent_width), F32),
        ],
        name="leaf_update",
    )
    own = own + swap(other).astype(F32)
    prepared = prepare(own, [(parent_rows, parent_local, parent_height)])
    prb, prepared = lax.optimization_barrier((chips_sum(own).astype(BF16), prepared))
    parent_list, parent_plan = prepared
    parent_at = find(parent_plan, parent_list, root_width)

    prb_other, parent_at = lax.optimization_barrier((swap(prb), parent_at))

    def parent_solve(part_ref, x_ref, w_ref, y_ref, send_ref):
        y = both_halves(part_ref, x_ref, w_ref, 0)
        y_ref[...] = y
        send_ref[...] = y.astype(BF16)

    py, pyb = call(
        parent_solve,
        [((rcount, parent_cols), F32), ((rcount, parent_cols), BF16)],
        [own_half(prb, parent_inv, "parent_solve_own"), prb_other, pinned(parent_inv)],
        [VMEM] * 3,
        name="parent_solve",
    )
    pyb = far_gather(pyb)

    def parent_update(
        plan_ref, part_ref, x_ref, w_ref, list_ref, at_ref, root_ref, rhs_ref, own_ref, other_ref,
        update_ref, acc_ref, sum_ref,
    ):
        for b in range(root_width // LANES):
            acc_ref[b] = root_ref[b]
        update_ref[0] = both_halves(part_ref, x_ref, w_ref, 0, xor=True)
        scatter_walk(plan_ref, list_ref, at_ref, update_ref, acc_ref)
        for b in range(root_width // LANES):
            sum_ref[:, b * LANES : (b + 1) * LANES] = -acc_ref[b]
        if root_aligned:
            sum_ref[:, spot(flat(), root_cols)] += rhs_ref[...]
        else:
            sum_ref[...] += rhs_ref[...]
        deal(sum_ref, own_ref, other_ref)

    own, other = call(
        parent_update,
        [((chips, rcount, piece), F32), ((chips, rcount, piece), BF16)],
        [
            parent_plan,
            own_half(pyb, parent_panel, "parent_update_own", xor=True),
            swap(pyb),
            pinned(parent_panel),
            parent_list,
            parent_at,
            root_acc,
            rhs,
        ],
        [SMEM] + [VMEM] * 7,
        scratch=[
            pltpu.VMEM((1, rcount, parent_local), F32),
            pltpu.VMEM((root_width // LANES + BLOCKS, rcount, LANES), F32),
            pltpu.VMEM((rcount, root_width), F32),
        ],
        name="parent_update",
    )
    rrb = chips_sum(leaf_sum(own + swap(other).astype(F32))).astype(BF16)

    def terms(x_ref, w_ref, out_ref, odd, xor=True):
        _, sets, _, cols = out_ref.shape
        for k in range(chips):
            at = spot(2 * (chip() ^ k if xor else k) + odd, cols)
            for s in range(sets):
                out_ref[k, s] = times(x_ref[s], w_ref[s, :, at]).astype(out_ref.dtype)

    def split_terms(w):
        return (chips, w.shape[0], rcount, w.shape[2] // n)

    def own_terms(x, w, name, xor=True):
        def body(x_ref, w_ref, out_ref):
            terms(x_ref, w_ref, out_ref, core(), xor)

        return call(
            body, [(split_terms(w), F32)], [x, pinned(w)], [VMEM] * 2, moved=12 << 20, name=name
        )[0]

    def total(x, w, other, name):
        own = own_terms(x, w, name, xor=False)
        return chips_sum((own + swap(other).astype(F32))[:, 0])

    def root_solve(part_ref, x_ref, w_ref, out_ref, y_ref):
        y_ref[0] = both_halves(part_ref, x_ref, w_ref, 0).astype(BF16)
        terms(y_ref, w_ref, out_ref, 1 - core(), xor=False)

    term, ryb = call(
        root_solve,
        [(split_terms(root_inv), BF16), ((1, rcount, root_local), BF16)],
        [own_half(rrb, root_inv, "root_solve_own"), swap(rrb), pinned(root_inv)],
        [VMEM] * 3,
        name="root_solve",
    )
    rxb = total(ryb, root_inv, term, "root_solve_back_own").astype(BF16)

    def blocks_of(source_ref, target_ref, start, width):
        for b in range(width // LANES):
            target_ref[start + b] = source_ref[:, b * LANES : (b + 1) * LANES].astype(F32)

    def reduce(own, other):
        other = swap(other)
        sums = [own[k] + other[k].astype(F32) for k in range(chips)]
        return [sums[0]] + from_chips(lambda k: sums[k].astype(BF16))

    def parent_back(
        plan_ref, own_ref, other_ref, rows_ref, w_ref, out_ref, whole_ref, sol_ref, found_ref, x_ref,
    ):
        unite(own_ref, other_ref, x_ref)
        if root_aligned:
            sol_ref[...] = x_ref[:, spot(flat(), root_cols)].astype(F32)
        else:
            sol_ref[...] = x_ref[...].astype(F32)
        blocks_of(x_ref, whole_ref, 0, root_width)
        gather_walk(plan_ref, rows_ref, whole_ref, found_ref)
        terms(found_ref, w_ref, out_ref, 1 - core())

    term, root_whole, root_sol, found = call(
        parent_back,
        [
            (split_terms(parent_panel), BF16),
            ((root_width // LANES + BLOCKS, rcount, LANES), F32),
            ((rcount, root_cols if root_aligned else root_width), F32),
            ((1, rcount, parent_local), BF16),
        ],
        [parent_plan, rxb, swap(rxb), parent_list, pinned(parent_panel)],
        [SMEM] + [VMEM] * 4,
        scratch=[pltpu.VMEM((rcount, root_width), BF16)],
        name="parent_back",
    )
    tails = reduce(own_terms(found, parent_panel, "parent_back_own"), term)

    def parent_solve_back(*refs):
        tail_refs, (y_ref, w_ref, out_ref, v_ref) = refs[:chips], refs[chips:]
        lost = sum(ref[0].astype(F32) for ref in tail_refs)
        v_ref[0] = (y_ref[...] - lost).astype(BF16)
        terms(v_ref, w_ref, out_ref, 1 - core(), xor=False)

    term, pvb = call(
        parent_solve_back,
        [(split_terms(parent_inv), BF16), ((1, rcount, parent_cols), BF16)],
        [*tails, py, pinned(parent_inv)],
        [VMEM] * (chips + 2),
        name="parent_solve_back",
    )
    px = total(pvb, parent_inv, term, "parent_solve_back_own")
    pxb = px.astype(BF16)

    def ancestors(
        plan_ref, px_ref, own_ref, other_ref, root_ref, rows_ref, sol_ref,
        x_ref, whole_ref, found_ref,
    ):
        sol_ref[...] = px_ref[chip()]
        unite(own_ref, other_ref, x_ref)
        blocks_of(x_ref, whole_ref, 0, parent_width)
        for b in range(root_width // LANES):
            whole_ref[parent_width // LANES + b] = root_ref[b]
        gather_walk(plan_ref, rows_ref, whole_ref, found_ref)

    def all_terms(x_ref, w_ref, out_ref):
        for s in range(leaves):
            out_ref[s] = times(x_ref[s], w_ref[s]).astype(BF16)

    def pieces_apart(term):
        return jnp.moveaxis(term.reshape(leaves, rcount, n, leaf_cols), 2, 0)

    whole_term = (leaves, rcount, leaf_width)
    found_shape = (leaves, rcount, leaf_local)
    scratch = [
        pltpu.VMEM((rcount, parent_width), BF16),
        pltpu.VMEM((tall // LANES + BLOCKS, rcount, LANES), F32),
    ]

    def leaf_back(*refs):
        ins, (w_ref, out_ref, sol_ref, found_ref, x_ref, whole_ref) = refs[:6], refs[6:]
        ancestors(*ins, sol_ref, x_ref, whole_ref, found_ref)
        if leaf_aligned:
            terms(found_ref, w_ref, out_ref, 1 - core())
        else:
            all_terms(found_ref, w_ref, out_ref)

    term, parent_sol, found = call(
        leaf_back,
        [
            (split_terms(leaf_panel) if leaf_aligned else whole_term, BF16),
            ((rcount, parent_cols), F32),
            (found_shape, BF16),
        ],
        [leaf_plan, px, pxb, swap(pxb), root_whole, leaf_list, pinned(leaf_panel)],
        [SMEM] + [VMEM] * 6,
        scratch=scratch,
        name="leaf_back",
    )
    if leaf_aligned:
        tails = reduce(own_terms(found, leaf_panel, "leaf_back_own"), term)
    else:
        tails = [all_to_all(pieces_apart(term)).astype(F32).sum(0)]

    def leaf_solve_back(*refs):
        tail_refs, (y_ref, w_ref, out_ref, v_ref) = refs[: len(tails)], refs[len(tails) :]
        for s in range(leaves):
            lost = sum(ref[s].astype(F32) for ref in tail_refs)
            v_ref[s] = (y_ref[s] - lost).astype(BF16)
        if leaf_aligned:
            terms(v_ref, w_ref, out_ref, 1 - core())
        else:
            all_terms(v_ref, w_ref, out_ref)

    term, lvb = call(
        leaf_solve_back,
        [
            (split_terms(leaf_panel) if leaf_aligned else whole_term, BF16),
            ((leaves, rcount, leaf_cols), BF16),
        ],
        [*tails, ly, pinned(leaf_inv)],
        [VMEM] * (len(tails) + 2),
        name="leaf_solve_back",
    )
    if leaf_aligned:
        parts = reduce(own_terms(lvb, leaf_inv, "leaf_solve_back_own"), term)
        leaf_sol = sum(p.astype(F32) for p in parts)
    else:
        leaf_sol = all_to_all(pieces_apart(term)).astype(F32).sum(0)
    if not root_aligned:
        root_sol = lax.dynamic_slice_in_dim(root_sol, flat() * root_cols, root_cols, 1)
    return (jnp.moveaxis(leaf_sol, 0, 1), parent_sol[:, None, :], root_sol)


def solution(mesh):
    return jax.shard_map(
        shards,
        mesh=mesh,
        in_specs=(
            P(None, "leaf", "rows"),
            P(None, "leaf", "rows"),
            P(None, ("leaf", "rows")),
            P("leaf", "rows", None),
            P("leaf", "rows", None),
            P("leaf", "rows"),
            P("leaf"),
            P("leaf", "rows", None),
            P("leaf", "rows", None),
            P("leaf", "rows"),
            P("leaf"),
            P("rows", None),
        ),
        out_specs=(P(None, "leaf", "rows"), P(None, "leaf", "rows"), P(None, ("leaf", "rows"))),
        check_vma=False,
    )
```

```python
import jax
import jax.numpy as jnp
from jax import lax
from jax.experimental import pallas as pl
from jax.experimental.pallas import tpu as pltpu
from jax.sharding import PartitionSpec as P

F32 = jnp.float32
BF16 = jnp.bfloat16
I32 = jnp.int32
LANES = 128
BLOCKS = 8
NONE = 1 << 24

VMEM = pl.BlockSpec(memory_space=pltpu.VMEM)
SMEM = pl.BlockSpec(memory_space=pltpu.SMEM)


def pinned(w):
    return pltpu.with_memory_space_constraint(w, pltpu.VMEM)


def outside(w):
    return pltpu.with_memory_space_constraint(w, pltpu.HBM)


def call(
    body, outs, ins, specs, out_specs=None, scratch=(), moved=0, limit=6 << 20, name=None
):
    return pl.pallas_call(
        body,
        out_shape=[jax.ShapeDtypeStruct(*o) if isinstance(o, tuple) else o for o in outs],
        in_specs=list(specs),
        out_specs=out_specs or [VMEM] * len(outs),
        scratch_shapes=list(scratch),
        cost_estimate=pl.CostEstimate(flops=0, bytes_accessed=moved, transcendentals=0),
        compiler_params=pltpu.CompilerParams(vmem_limit_bytes=limit),
        name=name,
    )(*ins)


def times_transposed(x, w):
    return lax.dot_general(x, w, (((1,), (1,)), ((), ())), preferred_element_type=F32)


def times(x, w):
    return lax.dot_general(x, w, (((1,), (0,)), ((), ())), preferred_element_type=F32)


def prepare(after, lists):
    count = len(lists)

    def one(first, rows_ref, height_ref, list_ref, plan_ref, scalar_ref):
        sets, length = rows_ref.shape
        tiles = length // LANES
        start = lax.axis_index("rows") * first
        lane = lax.broadcasted_iota(I32, (1, LANES), 1)
        rounds = 0
        for s in range(sets):
            used = height_ref[s] - start
            for tile in range(tiles):
                lanes = slice(tile * LANES, (tile + 1) * LANES)
                line = rows_ref[s : s + 1, lanes]
                list_ref[s : s + 1, lanes] = jnp.where(lane + tile * LANES < used, line, NONE)
                end = jnp.maximum(jnp.minimum(used, (tile + 1) * LANES) - 1, 0)
                lo = lax.shift_right_logical(scalar_ref[s, tile * LANES], 7)
                hi = lax.shift_right_logical(scalar_ref[s, end], 7)
                met = used > tile * LANES
                plan_ref[s * tiles + tile] = jnp.where(met, lo, 0)
                span = jnp.where(met, hi - lo + BLOCKS, 0)
                rounds = jnp.maximum(rounds, lax.shift_right_logical(span, 3))
        plan_ref[sets * tiles] = rounds

    def body(*refs):
        ins, outs = refs[1 : 2 * count + 1], refs[2 * count + 1 : 4 * count + 1]
        scalars, sems = refs[4 * count + 1 : -1], refs[-1]
        copies = [
            pltpu.make_async_copy(ins[2 * i], scalars[i], sems.at[i]) for i in range(count)
        ]
        for copy in copies:
            copy.start()
        for i, copy in enumerate(copies):
            copy.wait()
            one(lists[i][1], *ins[2 * i : 2 * i + 2], *outs[2 * i : 2 * i + 2], scalars[i])

    shapes, ins = [], [after]
    for rows, _, height in lists:
        sets, length = rows.shape
        shapes += [(rows.shape, I32), ((sets * (length // LANES) + 1,), I32)]
        ins += [rows, height]
    return call(
        body,
        shapes,
        ins,
        [pl.BlockSpec(memory_space=pl.ANY)] + [VMEM, SMEM] * count,
        out_specs=[VMEM, SMEM] * count,
        scratch=[pltpu.SMEM(x[0].shape, I32) for x in lists] + [pltpu.SemaphoreType.DMA((count,))],
        moved=4 << 20,
        limit=4 << 20,
        name="prepare",
    )


def walk(plan_ref, list_ref, blocks, visit):
    sets, length = list_ref.shape
    tiles = length // LANES

    def take_round(i, first):
        for tile in range(tiles):
            lanes = slice(tile * LANES, (tile + 1) * LANES)
            for s in range(sets):
                line = jnp.broadcast_to(list_ref[s : s + 1, lanes], (BLOCKS, LANES))
                lo = jnp.minimum(plan_ref[s * tiles + tile] + i * BLOCKS, blocks)
                visit(s, lanes, line, lo, first)

    take_round(0, True)

    def again(i, carry):
        take_round(i, False)
        return carry

    lax.fori_loop(1, plan_ref[sets * tiles], again, 0)


def along(x, index):
    return jnp.take_along_axis(x, index, axis=1, mode="promise_in_bounds")


def pick(x, index):
    inside = (index >= 0) & (index < LANES)
    return jnp.where(inside, along(x, index & (LANES - 1)), 0.0)


def position(line, lo):
    block = lax.broadcasted_iota(I32, line.shape, 0) + lo
    target = block * LANES + lax.broadcasted_iota(I32, line.shape, 1)
    below = jnp.zeros(line.shape, I32)
    step = LANES // 2
    while step:
        below = jnp.where(along(line, below + (step - 1)) < target, below + step, below)
        step //= 2
    return jnp.where(along(line, below) == target, below, -1)


def scatter_walk(plan_ref, list_ref, update_ref, acc_ref):
    def visit(s, lanes, line, lo, first):
        x, at = update_ref[s, :, lanes], position(line, lo)
        parts = [pick(x, jnp.broadcast_to(at[u : u + 1], x.shape)) for u in range(BLOCKS)]
        acc_ref[pl.ds(lo, BLOCKS)] += jnp.stack(parts)

    walk(plan_ref, list_ref, acc_ref.shape[0] - BLOCKS, visit)


def gather_walk(plan_ref, list_ref, source_ref, out_ref):
    def visit(s, lanes, line, lo, first):
        x = source_ref[pl.ds(lo, BLOCKS)]
        parts = [pick(x[u], line - (lo + u) * LANES) for u in range(BLOCKS)]
        found = sum(parts[1:], parts[0]).astype(out_ref.dtype)
        out_ref[s, :, lanes] = found if first else out_ref[s, :, lanes] + found

    walk(plan_ref, list_ref, source_ref.shape[0] - BLOCKS, visit)


def far_order(chips):
    return [0] + list(range(2, chips)) + [1] if chips > 1 else [0]


def core():
    return lax.axis_index("rows") & 1


def chip():
    return lax.axis_index("rows") // 2


def spot(r, w):
    return pl.ds(pl.multiple_of(r * w, LANES), w)


def unite(own_ref, other_ref, out_ref, *at, xor=False):
    odd, w = core(), own_ref.shape[-1]
    for k, j in enumerate(far_order(own_ref.shape[0])):
        c = chip() ^ j if xor else k
        out_ref[:, spot(2 * c + odd, w)] = own_ref[(k,) + at]
        out_ref[:, spot(2 * c + 1 - odd, w)] = other_ref[(k,) + at]


def deal(value_ref, own_ref, other_ref):
    odd = core()
    chips, _, w = own_ref.shape
    for k in range(chips):
        own_ref[k] = value_ref[:, spot(2 * k + odd, w)].astype(own_ref.dtype)
        other_ref[k] = value_ref[:, spot(2 * k + 1 - odd, w)].astype(other_ref.dtype)


def half_of(x_ref, w_ref, s, odd, xor, but=()):
    at = (s,) if len(x_ref.shape) == 4 else ()
    chips, cols = x_ref.shape[0], x_ref.shape[-1]
    picked, columns = [], []
    for k, j in enumerate(far_order(chips)):
        if j in but:
            continue
        c = chip() ^ j if xor else k
        picked.append(x_ref[(k,) + at])
        columns.append(w_ref[s, :, spot(2 * c + odd, cols)])
    return times_transposed(jnp.concatenate(picked, axis=1), jnp.concatenate(columns, axis=1))


def own_half(x, w, name, xor=False, done=None, but=()):
    sets, rows = w.shape[:2]

    def body(x_ref, w_ref, *refs):
        for s in range(sets):
            got = half_of(x_ref, w_ref, s, core(), xor, but)
            refs[-1][s] = got if done is None else got + refs[0][s]

    return call(
        body,
        [((sets, x.shape[-2], rows), F32)],
        [x, pinned(w)] + ([] if done is None else [done]),
        [VMEM] * (2 if done is None else 3),
        moved=12 << 20,
        name=name,
    )[0]


def one_piece(x, w, k, name, done=None):
    sets, rows = w.shape[:2]

    def body(x_ref, w_ref, *refs):
        columns = spot(2 * (chip() ^ k) + core(), x_ref.shape[-1])
        for s in range(sets):
            got = times_transposed(x_ref[s], w_ref[s, :, columns])
            refs[-1][s] = got if done is None else got + refs[0][s]

    return call(
        body,
        [((sets, x.shape[-2], rows), F32)],
        [x, pinned(w)] + ([] if done is None else [done]),
        [VMEM] * (2 if done is None else 3),
        moved=4 << 20,
        name=name,
    )[0]


def both_halves(part_ref, x_ref, w_ref, s, xor=False):
    return part_ref[s] + half_of(x_ref, w_ref, s, 1 - core(), xor)


def all_to_all(x):
    return lax.all_to_all(x, "rows", 0, 0)


def swap(x):
    n = lax.axis_size("rows")
    return lax.ppermute(x, "rows", [(i, i ^ 1) for i in range(n)])


def far(x, k):
    n = lax.axis_size("rows")
    return lax.ppermute(x, "rows", [(i, i ^ (2 * k)) for i in range(n)])


def from_chips(piece):
    return [far(piece(k), k) for k in far_order(lax.axis_size("rows") // 2)[1:]]


def chips_sum(x):
    b = x.astype(BF16)
    return x + sum(got.astype(F32) for got in from_chips(lambda k: b))


def leaf_sum(x):
    n = lax.axis_size("leaf")
    b = x.astype(BF16)
    for k in range(1, n):
        x = x + lax.ppermute(b, "leaf", [(i, (i + k) % n) for i in range(n)]).astype(F32)
    return x


def shards(
    leaf_rhs,
    parent_rhs,
    root_rhs,
    leaf_inv,
    leaf_panel,
    leaf_rows,
    leaf_height,
    parent_inv,
    parent_panel,
    parent_rows,
    parent_height,
    root_inv,
):
    n = lax.axis_size("rows")
    chips = n // 2
    rcount, leaves, leaf_cols = leaf_rhs.shape
    leaf_local, leaf_width = leaf_panel.shape[1:]
    parent_cols, parent_width = parent_inv.shape[1:]
    parent_local = parent_panel.shape[1]
    root_width = root_inv.shape[1]
    root_inv = root_inv[None]
    root_local = root_inv.shape[1]
    root_cols = root_rhs.shape[1]
    piece = root_width // n
    tall = parent_width + root_width
    leaf_aligned = leaf_cols % LANES == 0
    root_aligned = root_cols % LANES == 0

    def flat():
        return lax.axis_index("leaf") * n + lax.axis_index("rows")

    def far_gather(x):
        return jnp.stack([x] + from_chips(lambda k: x))

    def leaf_columns(x):
        got = all_to_all(jnp.broadcast_to(x[None], (n,) + x.shape))
        return jnp.moveaxis(got, 0, 2).reshape(1, leaves, rcount, leaf_width)

    def leaf_product(x_refs, w_ref, s):
        if leaf_aligned:
            return both_halves(*x_refs, w_ref, s, xor=True)
        return times_transposed(x_refs[0][0, s], w_ref[s])

    def leaf_halves(x, w, name, done=None, but=()):
        return own_half(x, w, name, True, done, but), swap(x)

    rhs = root_rhs
    if not root_aligned:
        rhs = lax.dynamic_update_slice_in_dim(
            jnp.zeros((rcount, root_width), F32), root_rhs, flat() * root_cols, 1
        )
    weights = (leaf_inv, leaf_panel, parent_inv, parent_panel, root_inv, leaf_rows, parent_rows)

    def round_rhs(x_ref, *refs):
        out_ref = refs[-1]
        for s in range(leaves):
            out_ref[s] = x_ref[:, s, :].astype(BF16)

    lb = call(
        round_rhs,
        [((leaves, rcount, leaf_cols), BF16)],
        [leaf_rhs] + [outside(w) for w in weights],
        [VMEM] + [pl.BlockSpec(memory_space=pltpu.HBM)] * len(weights),
        name="round_rhs",
    )[0]
    prepared = prepare(lb, [(leaf_rows, leaf_local, leaf_height)])
    lb = far_gather(lb) if leaf_aligned else leaf_columns(lb)
    lb, prepared, rhs = lax.optimization_barrier((lb, prepared, rhs))
    leaf_list, leaf_plan = prepared
    lb = leaf_halves(lb, leaf_inv, "leaf_solve_own") if leaf_aligned else (lb,)

    def leaf_solve(*refs):
        x_refs, (w_ref, y_ref, send_ref) = refs[: len(lb)], refs[len(lb) :]
        for s in range(leaves):
            y = leaf_product(x_refs, w_ref, s)
            y_ref[s] = y
            send_ref[s] = y.astype(BF16)

    ly, lyb = call(
        leaf_solve,
        [((leaves, rcount, leaf_cols), F32), ((leaves, rcount, leaf_cols), BF16)],
        [*lb, pinned(leaf_inv)],
        [VMEM] * (len(lb) + 1),
        name="leaf_solve",
    )
    if leaf_aligned:
        done = one_piece(lyb, leaf_panel, 0, "leaf_update_first")
        lyb, done = lax.optimization_barrier((far_gather(lyb), done))
        lyb = leaf_halves(lyb, leaf_panel, "leaf_update_own", done, (0,))
    else:
        lyb = (leaf_columns(lyb),)

    def leaf_update(*refs):
        x_refs, refs = refs[: len(lyb)], refs[len(lyb) :]
        plan_ref, w_ref, list_ref, rhs_ref, own_ref, other_ref, root_ref, *refs = refs
        update_ref, acc_ref, sum_ref = refs
        acc_ref[...] = jnp.zeros(acc_ref.shape, F32)
        for s in range(leaves):
            update_ref[s] = leaf_product(x_refs, w_ref, s)
        scatter_walk(plan_ref, list_ref, update_ref, acc_ref)
        for b in range(parent_width // LANES):
            sum_ref[:, b * LANES : (b + 1) * LANES] = -acc_ref[b]
        sum_ref[:, spot(lax.axis_index("rows"), parent_cols)] += rhs_ref[:, 0, :]
        deal(sum_ref, own_ref, other_ref)
        for b in range(root_width // LANES):
            root_ref[b] = acc_ref[parent_width // LANES + b]

    own, other, root_acc = call(
        leaf_update,
        [
            ((chips, rcount, parent_cols), F32),
            ((chips, rcount, parent_cols), BF16),
            ((root_width // LANES, rcount, LANES), F32),
        ],
        [*lyb, leaf_plan, pinned(leaf_panel), leaf_list, parent_rhs],
        [VMEM] * len(lyb) + [SMEM] + [VMEM] * 3,
        scratch=[
            pltpu.VMEM((leaves, rcount, leaf_local), F32),
            pltpu.VMEM((tall // LANES + BLOCKS, rcount, LANES), F32),
            pltpu.VMEM((rcount, parent_width), F32),
        ],
        name="leaf_update",
    )
    own = own + swap(other).astype(F32)
    prepared = prepare(own, [(parent_rows, parent_local, parent_height)])
    prb, prepared = lax.optimization_barrier((chips_sum(own).astype(BF16), prepared))
    parent_list, parent_plan = prepared

    def parent_solve(part_ref, x_ref, w_ref, y_ref, send_ref):
        y = both_halves(part_ref, x_ref, w_ref, 0)
        y_ref[...] = y
        send_ref[...] = y.astype(BF16)

    py, pyb = call(
        parent_solve,
        [((rcount, parent_cols), F32), ((rcount, parent_cols), BF16)],
        [own_half(prb, parent_inv, "parent_solve_own"), swap(prb), pinned(parent_inv)],
        [VMEM] * 3,
        name="parent_solve",
    )
    pyb = far_gather(pyb)

    def parent_update(
        plan_ref, part_ref, x_ref, w_ref, list_ref, root_ref, rhs_ref, own_ref, other_ref,
        update_ref, acc_ref, sum_ref,
    ):
        for b in range(root_width // LANES):
            acc_ref[b] = root_ref[b]
        update_ref[0] = both_halves(part_ref, x_ref, w_ref, 0, xor=True)
        scatter_walk(plan_ref, list_ref, update_ref, acc_ref)
        for b in range(root_width // LANES):
            sum_ref[:, b * LANES : (b + 1) * LANES] = -acc_ref[b]
        if root_aligned:
            sum_ref[:, spot(flat(), root_cols)] += rhs_ref[...]
        else:
            sum_ref[...] += rhs_ref[...]
        deal(sum_ref, own_ref, other_ref)

    own, other = call(
        parent_update,
        [((chips, rcount, piece), F32), ((chips, rcount, piece), BF16)],
        [
            parent_plan,
            own_half(pyb, parent_panel, "parent_update_own", xor=True),
            swap(pyb),
            pinned(parent_panel),
            parent_list,
            root_acc,
            rhs,
        ],
        [SMEM] + [VMEM] * 6,
        scratch=[
            pltpu.VMEM((1, rcount, parent_local), F32),
            pltpu.VMEM((root_width // LANES + BLOCKS, rcount, LANES), F32),
            pltpu.VMEM((rcount, root_width), F32),
        ],
        name="parent_update",
    )
    rrb = chips_sum(leaf_sum(own + swap(other).astype(F32))).astype(BF16)

    def terms(x_ref, w_ref, out_ref, odd, xor=True):
        _, sets, _, cols = out_ref.shape
        for k in range(chips):
            at = spot(2 * (chip() ^ k if xor else k) + odd, cols)
            for s in range(sets):
                out_ref[k, s] = times(x_ref[s], w_ref[s, :, at]).astype(out_ref.dtype)

    def split_terms(w):
        return (chips, w.shape[0], rcount, w.shape[2] // n)

    def own_terms(x, w, name, xor=True):
        def body(x_ref, w_ref, out_ref):
            terms(x_ref, w_ref, out_ref, core(), xor)

        return call(
            body, [(split_terms(w), F32)], [x, pinned(w)], [VMEM] * 2, moved=12 << 20, name=name
        )[0]

    def total(x, w, other, name):
        own = own_terms(x, w, name, xor=False)
        return chips_sum((own + swap(other).astype(F32))[:, 0])

    def root_solve(part_ref, x_ref, w_ref, out_ref, y_ref):
        y_ref[0] = both_halves(part_ref, x_ref, w_ref, 0).astype(BF16)
        terms(y_ref, w_ref, out_ref, 1 - core(), xor=False)

    term, ryb = call(
        root_solve,
        [(split_terms(root_inv), BF16), ((1, rcount, root_local), BF16)],
        [own_half(rrb, root_inv, "root_solve_own"), swap(rrb), pinned(root_inv)],
        [VMEM] * 3,
        name="root_solve",
    )
    rxb = total(ryb, root_inv, term, "root_solve_back_own").astype(BF16)

    def blocks_of(source_ref, target_ref, start, width):
        for b in range(width // LANES):
            target_ref[start + b] = source_ref[:, b * LANES : (b + 1) * LANES].astype(F32)

    def reduce(own, other):
        other = swap(other)
        sums = [own[k] + other[k].astype(F32) for k in range(chips)]
        return [sums[0]] + from_chips(lambda k: sums[k].astype(BF16))

    def parent_back(
        plan_ref, own_ref, other_ref, rows_ref, w_ref, out_ref, whole_ref, sol_ref, found_ref, x_ref,
    ):
        unite(own_ref, other_ref, x_ref)
        if root_aligned:
            sol_ref[...] = x_ref[:, spot(flat(), root_cols)].astype(F32)
        else:
            sol_ref[...] = x_ref[...].astype(F32)
        blocks_of(x_ref, whole_ref, 0, root_width)
        gather_walk(plan_ref, rows_ref, whole_ref, found_ref)
        terms(found_ref, w_ref, out_ref, 1 - core())

    term, root_whole, root_sol, found = call(
        parent_back,
        [
            (split_terms(parent_panel), BF16),
            ((root_width // LANES + BLOCKS, rcount, LANES), F32),
            ((rcount, root_cols if root_aligned else root_width), F32),
            ((1, rcount, parent_local), BF16),
        ],
        [parent_plan, rxb, swap(rxb), parent_list, pinned(parent_panel)],
        [SMEM] + [VMEM] * 4,
        scratch=[pltpu.VMEM((rcount, root_width), BF16)],
        name="parent_back",
    )
    tails = reduce(own_terms(found, parent_panel, "parent_back_own"), term)

    def parent_solve_back(*refs):
        tail_refs, (y_ref, w_ref, out_ref, v_ref) = refs[:chips], refs[chips:]
        lost = sum(ref[0].astype(F32) for ref in tail_refs)
        v_ref[0] = (y_ref[...] - lost).astype(BF16)
        terms(v_ref, w_ref, out_ref, 1 - core(), xor=False)

    term, pvb = call(
        parent_solve_back,
        [(split_terms(parent_inv), BF16), ((1, rcount, parent_cols), BF16)],
        [*tails, py, pinned(parent_inv)],
        [VMEM] * (chips + 2),
        name="parent_solve_back",
    )
    px = total(pvb, parent_inv, term, "parent_solve_back_own")
    pxb = px.astype(BF16)

    def ancestors(
        plan_ref, px_ref, own_ref, other_ref, root_ref, rows_ref, sol_ref,
        x_ref, whole_ref, found_ref,
    ):
        sol_ref[...] = px_ref[chip()]
        unite(own_ref, other_ref, x_ref)
        blocks_of(x_ref, whole_ref, 0, parent_width)
        for b in range(root_width // LANES):
            whole_ref[parent_width // LANES + b] = root_ref[b]
        gather_walk(plan_ref, rows_ref, whole_ref, found_ref)

    def all_terms(x_ref, w_ref, out_ref):
        for s in range(leaves):
            out_ref[s] = times(x_ref[s], w_ref[s]).astype(BF16)

    def pieces_apart(term):
        return jnp.moveaxis(term.reshape(leaves, rcount, n, leaf_cols), 2, 0)

    whole_term = (leaves, rcount, leaf_width)
    found_shape = (leaves, rcount, leaf_local)
    scratch = [
        pltpu.VMEM((rcount, parent_width), BF16),
        pltpu.VMEM((tall // LANES + BLOCKS, rcount, LANES), F32),
    ]

    def leaf_back(*refs):
        ins, (w_ref, out_ref, sol_ref, found_ref, x_ref, whole_ref) = refs[:6], refs[6:]
        ancestors(*ins, sol_ref, x_ref, whole_ref, found_ref)
        if leaf_aligned:
            terms(found_ref, w_ref, out_ref, 1 - core())
        else:
            all_terms(found_ref, w_ref, out_ref)

    term, parent_sol, found = call(
        leaf_back,
        [
            (split_terms(leaf_panel) if leaf_aligned else whole_term, BF16),
            ((rcount, parent_cols), F32),
            (found_shape, BF16),
        ],
        [leaf_plan, px, pxb, swap(pxb), root_whole, leaf_list, pinned(leaf_panel)],
        [SMEM] + [VMEM] * 6,
        scratch=scratch,
        name="leaf_back",
    )
    if leaf_aligned:
        tails = reduce(own_terms(found, leaf_panel, "leaf_back_own"), term)
    else:
        tails = [all_to_all(pieces_apart(term)).astype(F32).sum(0)]

    def leaf_solve_back(*refs):
        tail_refs, (y_ref, w_ref, out_ref, v_ref) = refs[: len(tails)], refs[len(tails) :]
        for s in range(leaves):
            lost = sum(ref[s].astype(F32) for ref in tail_refs)
            v_ref[s] = (y_ref[s] - lost).astype(BF16)
        if leaf_aligned:
            terms(v_ref, w_ref, out_ref, 1 - core())
        else:
            all_terms(v_ref, w_ref, out_ref)

    term, lvb = call(
        leaf_solve_back,
        [
            (split_terms(leaf_panel) if leaf_aligned else whole_term, BF16),
            ((leaves, rcount, leaf_cols), BF16),
        ],
        [*tails, ly, pinned(leaf_inv)],
        [VMEM] * (len(tails) + 2),
        name="leaf_solve_back",
    )
    if leaf_aligned:
        parts = reduce(own_terms(lvb, leaf_inv, "leaf_solve_back_own"), term)
        leaf_sol = sum(p.astype(F32) for p in parts)
    else:
        leaf_sol = all_to_all(pieces_apart(term)).astype(F32).sum(0)
    if not root_aligned:
        root_sol = lax.dynamic_slice_in_dim(root_sol, flat() * root_cols, root_cols, 1)
    return (jnp.moveaxis(leaf_sol, 0, 1), parent_sol[:, None, :], root_sol)


def solution(mesh):
    return jax.shard_map(
        shards,
        mesh=mesh,
        in_specs=(
            P(None, "leaf", "rows"),
            P(None, "leaf", "rows"),
            P(None, ("leaf", "rows")),
            P("leaf", "rows", None),
            P("leaf", "rows", None),
            P("leaf", "rows"),
            P("leaf"),
            P("leaf", "rows", None),
            P("leaf", "rows", None),
            P("leaf", "rows"),
            P("leaf"),
            P("rows", None),
        ),
        out_specs=(P(None, "leaf", "rows"), P(None, "leaf", "rows"), P(None, ("leaf", "rows"))),
        check_vma=False,
    )
```
